128 devices in a mesh: grid: 8 (over x, core), mark: 16 (over z, y).
Axes of the slice: x: 4, y: 4, z: 4, core: 2. Of those that a mesh axis runs over, the one named last changes fastest.
Arguments:
- velocity: float32 [3, 256, 256, 256], P(None, 'grid', 'mark'), may hold values from -6 to 6
- pressure: float32 [256, 256, 256], P('grid', 'mark'), may hold values from -6 to 6
- cell_visc: float32 [256, 256, 256], P('grid', 'mark'), may hold values from 0.2 to 5
- cell_dens: float32 [256, 256, 256], P('grid', 'mark'), may hold values from 0.5 to 1.5
- block_brick: int32 [2048, 48], P(('grid', 'mark')), may hold values from 0 to 1023
- block_counts: int32 [128, 16], P(('grid', 'mark')), may hold values from 0 to 48, as said below
- positions: float32 [2048, 3, 48, 256], P(('grid', 'mark')), may hold values from 0 to 1
- start_visc: float32 [2048, 48, 256], P(('grid', 'mark')), may hold values from 0.2 to 5
- marker_dens: float32 [2048, 48, 256], P(('grid', 'mark')), may hold values from 0.5 to 1.5
Outputs:
- velocity_next: float32 [3, 256, 256, 256], P(None, 'grid', 'mark')
- pressure_next: float32 [256, 256, 256], P('grid', 'mark')
- visc_next: float32 [256, 256, 256], P('grid', 'mark')
- dens_next: float32 [256, 256, 256], P('grid', 'mark')
- marker_visc: float32 [2048, 48, 256], P(('grid', 'mark'))
The draws below stay inside these ranges and needn't reach their ends.
Inputs may be any that keep to these rules, and one draw needn't show every extreme that they name: `block_counts`: entry q of a marker device's row counts its live slots toward the grid device of mark index q in its group; in every group some grid device gets exactly 48 live slots from every marker device. `block_brick`: dead slots name bricks too.
All inputs are finite; a program needn't handle non-finite values.
Results may differ from the reference program's by a relative error of at most 0.0003.
Values sent between devices are 32-bit elements; how exact they have to be, the bound alone decides.
A program may use at most 128 MiB of HBM per device.

```python
import math
import jax
import jax.numpy as jnp
from jax import lax

CX = 32
CY = 16
CZ = 256
CAP = 48
BLOCK = 256
ITERS = 4
NX = 256
NY = 256
BRICKS_DEV = 1024
SLOT_ROWS = 2048
N_GRID = 8
N_MARK = 16


def draw_block_counts(key, part):
    key = jax.random.fold_in(key, 11)
    level_key, count_key, owner_key = jax.random.split(key, 3)
    levels = jax.random.randint(level_key, (N_GRID * N_MARK, 1), 0, 4)
    ceiling = jnp.array([CAP // 8, CAP // 4, CAP // 2, CAP], dtype=jnp.int32)[levels]
    lowest = ceiling // 2
    counts = jax.random.randint(count_key, (N_GRID * N_MARK, N_MARK), lowest, ceiling + 1)
    full_owner = jax.random.randint(owner_key, (N_GRID, 1), 0, N_MARK)
    chosen = jnp.repeat(full_owner, N_MARK, axis=0) == jnp.arange(N_MARK, dtype=jnp.int32)[None, :]
    return jnp.where(chosen, CAP, counts).astype(jnp.int32)


def set_ends(entries, stream_key, smallest, top_value):
    shape = entries.shape
    spot = [jax.random.randint(jax.random.fold_in(stream_key, axis), (), 0, shape[axis]) for axis in range(len(shape))]
    entries = entries.at[tuple(spot)].set(smallest)
    longest = shape.index(max(shape))
    spot[longest] = (spot[longest] + 1) % shape[longest]
    return entries.at[tuple(spot)].set(top_value)


def block_levels(own_key, dims, cuts, smallest, largest):
    loudness, own = 1.0, jax.random.fold_in(own_key, 6)
    for dim, shards_of in cuts:
        steps = jnp.exp(jax.random.uniform(jax.random.fold_in(own, dim), (shards_of,), jnp.float32, smallest / len(cuts), largest / len(cuts)))
        loudness = loudness * jnp.repeat(steps, dims[dim] // shards_of).reshape([-1 if axis == dim else 1 for axis in range(len(dims))])
    return loudness


def scatter_about(key, dims, deviation, most, cuts=(), kind=jnp.bfloat16):
    result = jax.random.normal(key, dims, jnp.float32) * deviation
    if len(cuts) > 0:
        result = block_levels(key, dims, cuts, -0.22, 0.18) * result
    return jnp.clip(result, min=-most, max=most).astype(kind)


def setup_inputs(seed: int = 0) -> dict:
    keys = jax.random.split(jax.random.key(seed), 10)
    velocity = scatter_about(keys[0], (3, NX, NY, CZ), 1.0, 6.0, ((1, 8), (2, 16)), jnp.float32)
    pressure = scatter_about(keys[1], (NX, NY, CZ), 1.0, 6.0, ((0, 8), (1, 16)), jnp.float32)
    cell_visc = jnp.clip(jnp.exp(math.log(5.0) - 3.218876 * jax.random.uniform(keys[2], (NX, NY, CZ), jnp.float32) ** block_levels(keys[2], (NX, NY, CZ), ((0, 8), (1, 16)), -0.2, 0.2)), 0.2, 5.0)
    cell_dens = jnp.clip(0.5 + 1.0 * jax.random.uniform(keys[3], (NX, NY, CZ), jnp.float32) ** block_levels(keys[3], (NX, NY, CZ), ((0, 8), (1, 16)), -0.2, 0.2), 0.5, 1.5)
    block_brick = set_ends(jax.random.randint(keys[4], (SLOT_ROWS, CAP), 0, BRICKS_DEV), jax.random.fold_in(keys[4], 1), 0, BRICKS_DEV - 1).astype(jnp.int32)
    block_counts = draw_block_counts(jax.random.fold_in(keys[9], 71), 0)
    positions = jnp.clip(1.0 * jax.random.uniform(keys[6], (SLOT_ROWS, 3, CAP, BLOCK), jnp.float32) ** block_levels(keys[6], (SLOT_ROWS, 3, CAP, BLOCK), ((0, 128),), -0.2, 0.2), 0.0, 1.0)
    start_visc = jnp.clip(jnp.exp(math.log(5.0) - 3.218876 * jax.random.uniform(keys[7], (SLOT_ROWS, CAP, BLOCK), jnp.float32) ** block_levels(keys[7], (SLOT_ROWS, CAP, BLOCK), ((0, 128),), -0.2, 0.2)), 0.2, 5.0)
    marker_dens = jnp.clip(0.5 + 1.0 * jax.random.uniform(keys[8], (SLOT_ROWS, CAP, BLOCK), jnp.float32) ** block_levels(keys[8], (SLOT_ROWS, CAP, BLOCK), ((0, 128),), -0.2, 0.2), 0.5, 1.5)
    return {"velocity": velocity, "pressure": pressure, "cell_visc": cell_visc, "cell_dens": cell_dens, "block_brick": block_brick, "block_counts": block_counts, "positions": positions, "start_visc": start_visc, "marker_dens": marker_dens}


relax_weight = 0.6
pressure_rate = 0.25
gravity = 1.0
strain_scale = 0.5


def neighbours(padded):
    centre = padded[1:-1, 1:-1, 1:-1]
    return centre, [padded[2:, 1:-1, 1:-1], padded[:-2, 1:-1, 1:-1], padded[1:-1, 2:, 1:-1], padded[1:-1, :-2, 1:-1], padded[1:-1, 1:-1, 2:], padded[1:-1, 1:-1, :-2]]


def relax_sweep(padded_velocity, padded_pressure, padded_visc, density):
    viscosity, visc_near = neighbours(padded_visc)
    couplings = [0.5 * (viscosity + nearby) for nearby in visc_near]
    diagonal = sum(couplings)
    pressure, pressure_near = neighbours(padded_pressure)
    divergence = jnp.zeros_like(pressure)
    updated = []
    for component in range(3):
        current, current_near = neighbours(padded_velocity[component])
        laplace = sum(weight * (nearby - current) for weight, nearby in zip(couplings, current_near))
        forcing = laplace - (pressure - pressure_near[2 * component + 1])
        if component == 2:
            forcing = forcing - gravity * density
        updated.append(current + relax_weight * forcing / diagonal)
        divergence = divergence + current_near[2 * component] - current
    return jnp.stack(updated), pressure - pressure_rate * viscosity * divergence


def kernel(fraction, number_cells):
    position = fraction * number_cells
    centres = jnp.arange(number_cells, dtype=jnp.float32) + 0.5
    offset = position[:, None, :] - centres[None, :, None]
    gaussian = jnp.exp(-offset * offset)
    weights = gaussian / jnp.sum(gaussian, axis=1, keepdims=True)
    slopes = weights * (2.0 * jnp.sum(weights * offset, axis=1, keepdims=True) - 2.0 * offset)
    return weights, slopes


def marker_blocks(bricks, positions, start_visc, density, live_slots):
    highest = lax.Precision.HIGHEST
    blocks = bricks.shape[0]
    markers = positions.shape[-1]
    across_x, slope_x = kernel(positions[0], 4)
    across_y, slope_y = kernel(positions[1], 4)
    across_z, slope_z = kernel(positions[2], 8)
    values = bricks.reshape(blocks, 48, 8)
    interpolated = jnp.einsum("kcz,kzm->kcm", values, across_z, precision=highest).reshape(blocks, 3, 4, 4, markers)
    rising = jnp.einsum("kcz,kzm->kcm", values, slope_z, precision=highest).reshape(blocks, 3, 4, 4, markers)
    plane_xy = across_x[:, :, None, :] * across_y[:, None, :, :]
    plane_dx = slope_x[:, :, None, :] * across_y[:, None, :, :]
    plane_dy = across_x[:, :, None, :] * slope_y[:, None, :, :]
    grad_x = jnp.sum(interpolated * plane_dx[:, None], axis=(2, 3))
    grad_y = jnp.sum(interpolated * plane_dy[:, None], axis=(2, 3))
    grad_z = jnp.sum(rising * plane_xy[:, None], axis=(2, 3))
    normal = grad_x[:, 0] ** 2 + grad_y[:, 1] ** 2 + grad_z[:, 2] ** 2
    shear_xy = 0.5 * (grad_y[:, 0] + grad_x[:, 1])
    shear_xz = 0.5 * (grad_z[:, 0] + grad_x[:, 2])
    shear_yz = 0.5 * (grad_z[:, 1] + grad_y[:, 2])
    invariant = 0.5 * normal + shear_xy ** 2 + shear_xz ** 2 + shear_yz ** 2
    weakened = start_visc * jnp.exp(-jnp.log(1.0 + invariant / (strain_scale * strain_scale)) / 3.0)
    marker_visc = jnp.where(live_slots[:, None], weakened, 0.0)
    filled = jnp.broadcast_to(live_slots[:, None], weakened.shape).astype(jnp.float32)
    carried = jnp.stack([filled, filled * jnp.log(weakened), filled * density], axis=1)
    spread = (carried[:, :, None, None, :] * plane_xy[:, None]).reshape(blocks, 48, markers)
    moments = jnp.einsum("kcm,kzm->kcz", spread, across_z, precision=highest).reshape(blocks, 384)
    return marker_visc, moments


def reference(velocity, pressure, cell_visc, cell_dens, block_brick, block_counts, positions, start_visc, marker_dens):
    padded_visc = jnp.pad(cell_visc, 1)
    velocity_now, pressure_now = velocity, pressure
    for iteration in range(ITERS):
        velocity_now, pressure_now = relax_sweep(jnp.pad(velocity_now, ((0, 0), (1, 1), (1, 1), (1, 1))), jnp.pad(pressure_now, 1), padded_visc, cell_dens)
    shaped = velocity.reshape(3, N_GRID, CX // 4, 4, N_MARK, CY // 4, 4, CZ // 8, 8)
    bricks = shaped.transpose(1, 4, 2, 5, 7, 0, 3, 6, 8).reshape(N_GRID, N_MARK, BRICKS_DEV, 384)
    owners = jnp.arange(N_MARK, dtype=jnp.int32)
    devices = N_GRID * N_MARK

    def visit_device(totals, inputs):
        device, brick_ids, counts, places, visc_start, dens_start = inputs
        group_index = device // N_MARK
        group_bricks = bricks[group_index]
        fetched = group_bricks[owners[:, None], brick_ids]
        live_slots = (jnp.arange(CAP, dtype=jnp.int32)[None, :] < counts[:, None]).reshape(-1)
        flat_places = jnp.moveaxis(places, 1, 0).reshape(3, N_MARK * CAP, BLOCK)
        marker_visc, moments = marker_blocks(fetched.reshape(-1, 384), flat_places, visc_start.reshape(-1, BLOCK), dens_start.reshape(-1, BLOCK), live_slots)
        totals = totals.at[group_index, owners[:, None], brick_ids].add(moments.reshape(N_MARK, CAP, 384))
        return totals, marker_visc.reshape(N_MARK, CAP, BLOCK)

    inputs = (jnp.arange(devices, dtype=jnp.int32), block_brick.reshape(devices, N_MARK, CAP), block_counts, positions.reshape(devices, N_MARK, 3, CAP, BLOCK), start_visc.reshape(devices, N_MARK, CAP, BLOCK), marker_dens.reshape(devices, N_MARK, CAP, BLOCK))
    totals, marker_out = lax.scan(visit_device, jnp.zeros((N_GRID, N_MARK, BRICKS_DEV, 384), jnp.float32), inputs)
    moment_sums = totals.reshape(N_GRID, N_MARK, CX // 4, CY // 4, CZ // 8, 3, 4, 4, 8).transpose(5, 0, 2, 6, 1, 3, 7, 4, 8).reshape(3, NX, NY, CZ)
    visc_next = jnp.exp((moment_sums[1] + jnp.log(cell_visc)) / (moment_sums[0] + 1.0))
    dens_next = (moment_sums[2] + cell_dens) / (moment_sums[0] + 1.0)
    return velocity_now, pressure_now, visc_next, dens_next, marker_out.reshape(SLOT_ROWS, CAP, BLOCK)
```

```python
import functools
import math
import jax
import jax.numpy as jnp
from jax import lax
from jax.sharding import PartitionSpec as P
from jax.experimental import pallas as pl
from jax.experimental.pallas import tpu as pltpu

F32, BF16 = jnp.float32, jnp.bfloat16
VMEM = pltpu.VMEM
CAP, BLOCK, OWNERS = 48, 256, 16
NT = (((1,), (1,)), ((), ()))
UNROLL = 4


def split(x):
    hi = x.astype(BF16)
    return hi, (x - hi.astype(F32)).astype(BF16)


def axis_weights(fraction, cells):
    half = 0.5 * cells
    factor = jnp.exp(2.0 * cells * fraction - 2.0 * half)
    centres = [i + 0.5 - half for i in range(cells)]
    powers = [None, factor]
    for i in range(2, cells):
        powers.append(powers[i // 2] * powers[i - i // 2])
    raw = [jnp.full_like(factor, math.exp(-centres[0] ** 2))]
    raw += [math.exp(-(centres[i] ** 2)) * powers[i] for i in range(1, cells)]
    total = functools.reduce(jnp.add, raw)
    scale = 1.0 / total
    weights = [r * scale for r in raw]
    mean = functools.reduce(jnp.add, [c * w for c, w in zip(centres, weights)])
    return weights, mean


def marker_group(q, row, u, pos, visc, dens, bricks, marker_out, moments, count, wz_s, wy_s, planes):
    rows = pl.ds(row, 8)
    sub = lax.broadcasted_iota(jnp.int32, (8, 128), 0)
    lane = lax.broadcasted_iota(jnp.int32, (8, 128), 1)
    sub2 = lax.broadcasted_iota(jnp.int32, (8, 256), 0)
    low, low2 = sub < 4, sub2 < 4
    diag = (lane // 32) == (sub % 4)
    shifts = [(sub - (2 * ip + sub // 4) + 4) % 4 for ip in range(2)]
    spread = [[diag & (shifts[ip] == s) for s in range(4)] for ip in range(2)]

    def both(x):
        wide = x.shape[1] == 256
        turned = pltpu.roll(x, 4, 0)
        mask = low2 if wide else low
        return jnp.where(mask, x, turned), jnp.where(mask, turned, x)

    wx, mean_x = axis_weights(pos[q, 0, rows, :], 4)
    wy, mean_y = axis_weights(pos[q, 1, rows, :], 4)
    wz, mean_z = axis_weights(pos[q, 2, rows, :], 8)
    for k in range(8):
        for h in range(2):
            wz_s[u, h, pl.ds(8 * k, 8), :] = wz[k][:, 128 * h : 128 * h + 128]
    for j in range(4):
        for h in range(2):
            wy_s[u, h, pl.ds(8 * j, 8), :] = wy[j][:, 128 * h : 128 * h + 128]
    for b in range(8):
        for h in range(2):
            col = wz_s[u, h, pl.ds(b, 8, stride=8), :]
            for jp in range(2):
                pair = [
                    col * jnp.broadcast_to(wy_s[u, h, pl.ds(8 * j + b, 1), :], (8, 128))
                    for j in (2 * jp, 2 * jp + 1)
                ]
                hi, lo = split(jnp.concatenate(pair, axis=0))
                at = 32 * (b % 4) + 16 * jp
                planes[u, b // 4, pl.ds(at, 16), pl.ds(128 * h, 128)] = hi
                planes[u, b // 4, pl.ds(128 + at, 16), pl.ds(128 * h, 128)] = lo

    cell = lane.astype(F32)
    c_i = (lane // 32).astype(F32) - 1.5
    c_j = ((lane // 8) % 4).astype(F32) - 1.5
    c_k = (lane % 8).astype(F32) - 3.5
    v = [bricks[q, rows, pl.ds(128 * c, 128)] for c in range(3)]
    kinds = [
        v[0],
        v[1],
        v[2],
        c_j * v[1],
        c_k * v[2],
        c_j * v[0] + c_i * v[1],
        c_k * v[0] + c_i * v[2],
        c_k * v[1] + c_j * v[2],
    ]
    tiles = ([], [])
    for kind in kinds:
        for side, src in enumerate(both(kind)):
            turned = [src] + [pltpu.roll(src, 32 * s, 1) for s in range(1, 4)]
            for ip in range(2):
                tile = jnp.zeros_like(src)
                for s in range(4):
                    tile = jnp.where(spread[ip][s], turned[s], tile)
                tiles[side].append(tile)
    results = []
    for side in range(2):
        his, los = [], []
        for n in range(0, 16, 2):
            hi, lo = split(jnp.concatenate(tiles[side][n : n + 2], axis=0))
            his.append(hi)
            los.append(lo)
        left = jnp.concatenate(his + los, axis=0)
        left = jnp.concatenate([left, left], axis=1)
        out = jnp.dot(left, planes[u, side], preferred_element_type=F32)
        results.append(out[:128] + out[128:])
    pairs = ([], [])
    centred = ([], [])
    for ip in range(2):
        first, second = both(wx[2 * ip]), both(wx[2 * ip + 1])
        for side in range(2):
            w = jnp.where(low2, first[side], second[side])
            c = jnp.where(low2, 2 * ip - 1.5, 2 * ip - 0.5)
            pairs[side].append(w)
            centred[side].append(w * c)

    def fold(a, b):
        return jnp.where(low2, a, b) + pltpu.roll(jnp.where(low2, b, a), 4, 0)

    def along_x(kind, weights):
        sums = []
        for side in range(2):
            at = 16 * kind
            sums.append(
                results[side][at : at + 8] * weights[side][0]
                + results[side][at + 8 : at + 16] * weights[side][1]
            )
        return fold(*sums)

    vx, vy, vz, yy, zz, xy, xz, yz = [along_x(n, pairs) for n in range(8)]
    xx = along_x(0, centred) - mean_x * vx
    yy = yy - mean_y * vy
    zz = zz - mean_z * vz
    xy = xy - mean_y * vx - mean_x * vy
    xz = xz - mean_z * vx - mean_x * vz
    yz = yz - mean_z * vy - mean_y * vz
    invariant = 2.0 * (xx * xx + yy * yy + zz * zz) + xy * xy + xz * xz + yz * yz
    shift = jnp.log(1.0 + invariant * 4.0) * (1.0 / 3.0)
    start = visc[q, rows, :]
    live = (sub2 + row) < count
    weakened = start * jnp.exp(-shift)
    marker_out[q, rows, :] = jnp.where(live, weakened, 0.0)
    carried = [
        jnp.where(live, 1.0, 0.0),
        jnp.where(live, jnp.log(weakened), 0.0),
        jnp.where(live, dens[q, rows, :], 0.0),
    ]
    carried = [both(c) for c in carried]
    sums = []
    for side in range(2):
        rows_a = [carried[m][side] * pairs[side][ip] for m in range(3) for ip in range(2)]
        his, los = [], []
        for n in range(0, 6, 2):
            hi, lo = split(jnp.concatenate(rows_a[n : n + 2], axis=0))
            his.append(hi)
            los.append(lo)
        left = jnp.concatenate(his + los, axis=0)
        out = lax.dot_general(left, planes[u, side], NT, preferred_element_type=F32)
        sums.append(out[:48, :128] + out[:48, 128:] + out[48:, :128])
    for m in range(3):
        halves = []
        for side in range(2):
            total = None
            for ip in range(2):
                at = 16 * m + 8 * ip
                piece = jnp.where(diag, sums[side][at : at + 8], 0.0)
                placed = piece
                for s in range(1, 4):
                    placed = jnp.where(shifts[ip] == (4 - s), pltpu.roll(piece, 32 * s, 1), placed)
                total = placed if total is None else total + placed
            halves.append(total)
        moments[q, rows, pl.ds(128 * m, 128)] = jnp.where(low, halves[0], halves[1]) + pltpu.roll(
            jnp.where(low, halves[1], halves[0]), 4, 0
        )


def marker_kernel(counts, pos, visc, dens, bricks, marker_out, moments, todo, wz_s, wy_s, planes):
    def clear(q, _):
        marker_out[q] = jnp.zeros((CAP, BLOCK), F32)
        moments[q] = jnp.zeros((CAP, 384), F32)
        return 0

    lax.fori_loop(0, OWNERS, clear, 0)

    def listed(q, n):
        groups = (counts[0, q] + 7) // 8

        def put(g, at):
            todo[at] = q * 8 + g
            return at + 1

        return lax.fori_loop(0, groups, put, n)

    total = lax.fori_loop(0, OWNERS, listed, 0)

    def step(n, _):
        for u in range(UNROLL):
            item = todo[jnp.minimum(n * UNROLL + u, total - 1)]
            q = item // 8
            row = pl.multiple_of((item % 8) * 8, 8)
            marker_group(
                q, row, u, pos, visc, dens, bricks, marker_out, moments, counts[0, q], wz_s, wy_s, planes
            )
        return 0

    lax.fori_loop(0, (total + UNROLL - 1) // UNROLL, step, 0)


def marker_call(counts, pos, visc, dens, bricks):
    vm = pl.BlockSpec(memory_space=pltpu.VMEM)
    return pl.pallas_call(
        marker_kernel,
        out_shape=(
            jax.ShapeDtypeStruct((OWNERS, CAP, BLOCK), F32),
            jax.ShapeDtypeStruct((OWNERS, CAP, 384), F32),
        ),
        in_specs=[pl.BlockSpec(memory_space=pltpu.SMEM)] + [vm] * 4,
        out_specs=(vm, vm),
        scratch_shapes=[
            pltpu.SMEM((OWNERS * 8 + 8,), jnp.int32),
            VMEM((UNROLL, 2, 64, 128), F32),
            VMEM((UNROLL, 2, 32, 128), F32),
            VMEM((UNROLL, 2, 256, 256), BF16),
        ],
        compiler_params=pltpu.CompilerParams(vmem_limit_bytes=50 << 20),
        name="markers",
    )(counts, pos, visc, dens, bricks)


NX_L, NY_L, NZ = 32, 16, 256
BRICKS = 1024
MESH = pl.DeviceIdType.MESH
SWEEPS = 4
relax_weight = 0.6
pressure_rate = 0.25
gravity = 1.0


def group_transpose(tiles, group):
    tiles = list(tiles)
    for d in (8, 4, 2, 1):
        upper = (group & d) != 0
        for t in range(16):
            if t & d == 0:
                a, b = tiles[t], tiles[t + d]
                tiles[t] = jnp.where(upper, pltpu.roll(b, 8 * d, 1), a)
                tiles[t + d] = jnp.where(upper, b, pltpu.roll(a, 128 - 8 * d, 1))
    return tiles


def peers():
    g, me = lax.axis_index("grid"), lax.axis_index("mark")

    def after(k):
        return lax.rem(me + k, OWNERS)

    def before(k):
        return lax.rem(me + OWNERS - k, OWNERS)

    return g, me, after, before


def remote(src, dst, send, recv, device):
    return pltpu.make_async_remote_copy(
        src_ref=src, dst_ref=dst, send_sem=send, recv_sem=recv, device_id=device, device_id_type=MESH
    )


def grid_kernel(
    brick_ids, velocity, pressure, visc, dens, ids_out, bricks_out, velocity_out, pressure_out,
    state_a, state_b, visc_s, dens_s, halves, planes_hi, planes_lo, one_hot, ids_send, ids_recv, brick_send,
    kx, kym, kyp, kzm, kzp, damp, x_lo, x_hi, face_lo, face_hi, y_lo, y_hi,
    vx_lo, vx_hi, vface_lo, vface_hi, vy_lo, vy_hi,
    load_sem, id_send, id_recv, b_send, b_recv, h_send, h_recv, v_send, v_recv,
):
    g, me, after, before = peers()
    ahead, behind = lax.rem(g + 1, 8), lax.rem(g + 7, 8)
    loads = [
        pltpu.make_async_copy(velocity, state_a.at[pl.ds(0, 3), pl.ds(1, NX_L)], load_sem.at[0]),
        pltpu.make_async_copy(pressure, state_a.at[3, pl.ds(1, NX_L)], load_sem.at[1]),
        pltpu.make_async_copy(visc, visc_s.at[pl.ds(1, NX_L)], load_sem.at[2]),
        pltpu.make_async_copy(dens, dens_s, load_sem.at[3]),
    ]
    for c in loads:
        c.start()
    barrier = pltpu.get_barrier_semaphore()
    for k in range(1, OWNERS):
        pl.semaphore_signal(barrier, inc=1, device_id=(g, after(k)), device_id_type=MESH)
    pl.semaphore_signal(barrier, inc=1, device_id=(ahead, me), device_id_type=MESH)
    pl.semaphore_signal(barrier, inc=1, device_id=(behind, me), device_id_type=MESH)

    number = brick_ids[...]
    number = (((number >> 5) & 3) * 32 + (number & 31)) * 8 + (number >> 7)
    number = number.astype(F32)
    ids_send[...] = jnp.full((OWNERS, 8, 128), -1.0, F32)
    for q in range(OWNERS):
        ids_send[q, :, pl.ds(0, CAP)] = jnp.broadcast_to(number[q : q + 1], (8, CAP))
    pl.semaphore_wait(barrier, OWNERS + 1)

    def send_ids(k, _):
        remote(ids_send.at[after(k)], ids_recv.at[k], id_send.at[k], id_recv.at[k], (g, after(k))).start()
        return 0

    lax.fori_loop(1, OWNERS, send_ids, 0)
    ids_recv[0] = ids_send[me]
    for c in loads:
        c.wait()

    def halo(n, state):
        return [
            remote(state.at[:, 1], x_hi.at[n], h_send.at[n, 0], h_recv.at[n, 0], (behind, me)),
            remote(state.at[:, NX_L], x_lo.at[n], h_send.at[n, 1], h_recv.at[n, 1], (ahead, me)),
            remote(face_lo.at[n], y_hi.at[n], h_send.at[n, 2], h_recv.at[n, 2], (g, before(1))),
            remote(face_hi.at[n], y_lo.at[n], h_send.at[n, 3], h_recv.at[n, 3], (g, after(1))),
        ]

    def first_faces(x, _):
        face_lo[0, x] = jnp.concatenate([state_a[c, x + 1, 0:1, :] for c in range(4)], axis=0)
        face_hi[0, x] = jnp.concatenate([state_a[c, x + 1, 15:16, :] for c in range(4)], axis=0)
        return 0

    lax.fori_loop(0, NX_L, first_faces, 0)
    for x in range(NX_L):
        vface_lo[x : x + 1, :] = visc_s[x + 1, 0:1, :]
        vface_hi[x : x + 1, :] = visc_s[x + 1, 15:16, :]
    visc_halo = [
        remote(visc_s.at[1], vx_hi, v_send.at[0], v_recv.at[0], (behind, me)),
        remote(visc_s.at[NX_L], vx_lo, v_send.at[1], v_recv.at[1], (ahead, me)),
        remote(vface_lo, vy_hi, v_send.at[2], v_recv.at[2], (g, before(1))),
        remote(vface_hi, vy_lo, v_send.at[3], v_recv.at[3], (g, after(1))),
    ]
    for c in halo(0, state_a) + visc_halo:
        c.start()

    def to_halves(x, _):
        for c in range(3):
            plane = state_a[c, x + 1]
            at = pl.multiple_of(c * 512 + x * 16, 16)
            for h in range(2):
                halves[h, pl.ds(at, 16), :] = plane[:, 128 * h : 128 * h + 128]
        return 0

    lax.fori_loop(0, NX_L, to_halves, 0)
    group = lax.broadcasted_iota(jnp.int32, (8, 128), 1) // 8

    def to_bricks(n, _):
        bj, h = n // 2, lax.rem(n, 2)
        for c in range(3):
            tiles = [
                halves[h, pl.ds(c * 512 + 16 * i + 4 * bj + j, 8, stride=64), :]
                for i in range(4)
                for j in range(4)
            ]
            tiles = group_transpose(tiles, group)
            for t in range(0, 16, 2):
                hi, lo = split(jnp.concatenate(tiles[t : t + 2], axis=0))
                at = pl.multiple_of((bj * 32 + h * 16 + t) * 8, 16)
                planes_hi[pl.ds(at, 16), pl.ds(128 * c, 128)] = hi
                planes_lo[pl.ds(at, 16), pl.ds(128 * c, 128)] = lo
        return 0

    lax.fori_loop(0, 8, to_bricks, 0)

    def wait_ids(k, _):
        remote(ids_send.at[after(k)], ids_recv.at[k], id_send.at[k], id_recv.at[k], (g, after(k))).wait()
        return 0

    lax.fori_loop(1, OWNERS, wait_ids, 0)

    def brick_copy(k):
        return remote(
            brick_send.at[k], bricks_out.at[me], b_send.at[k], b_recv.at[k], (g, before(k))
        )

    lanes = lax.broadcasted_iota(jnp.int32, (CAP, 128), 1).astype(F32)

    def gather(n, _):
        for m in range(4):
            column = jnp.transpose(jnp.broadcast_to(ids_recv[4 * n + m][0:1, :], (128, 128)))[:CAP]
            for t in range(8):
                hit = jnp.where(column == lanes + 128.0 * t, 1.0, 0.0).astype(BF16)
                one_hot[pl.ds(CAP * m, CAP), pl.ds(128 * t, 128)] = hit
        found = jnp.dot(one_hot[...], planes_hi[...], preferred_element_type=F32)
        found = found + jnp.dot(one_hot[...], planes_lo[...], preferred_element_type=F32)
        for m in range(4):
            brick_send[4 * n + m] = found[CAP * m : CAP * m + CAP]
        for m in range(4):
            k = 4 * n + m

            @pl.when(k > 0)
            def _():
                brick_copy(k).start()

        return 0

    lax.fori_loop(0, 4, gather, 0)
    own = pltpu.make_async_copy(brick_send.at[0], bricks_out.at[me], load_sem.at[4])
    own.start()
    ids_out[...] = ids_recv[...]

    x_lo_on = (g > 0).astype(F32)
    x_hi_on = (g < 7).astype(F32)
    y_lo_on = (me > 0).astype(F32)
    y_hi_on = (me < OWNERS - 1).astype(F32)
    row = lax.broadcasted_iota(jnp.int32, (NY_L, NZ), 0)
    col = lax.broadcasted_iota(jnp.int32, (NY_L, NZ), 1)
    first_y, last_y = row == 0, row == NY_L - 1
    first_z, last_z = col == 0, col == NZ - 1

    def y_minus(plane, edge):
        return jnp.where(first_y, jnp.broadcast_to(edge, plane.shape), pltpu.roll(plane, 1, 0))

    def y_plus(plane, edge):
        return jnp.where(last_y, jnp.broadcast_to(edge, plane.shape), pltpu.roll(plane, NY_L - 1, 0))

    def z_minus(plane):
        return jnp.where(first_z, 0.0, pltpu.roll(plane, 1, 1))

    def z_plus(plane):
        return jnp.where(last_z, 0.0, pltpu.roll(plane, NZ - 1, 1))

    for c in visc_halo:
        c.wait()
    visc_s[0] = vx_lo[...] * x_lo_on
    visc_s[NX_L + 1] = vx_hi[...] * x_hi_on

    def couplings(x, _):
        here, below, above = visc_s[x + 1], visc_s[x], visc_s[x + 2]
        k_xm, k_xp = 0.5 * (here + below), 0.5 * (here + above)
        k_ym = 0.5 * (here + y_minus(here, vy_lo[pl.ds(x, 1), :] * y_lo_on))
        k_yp = 0.5 * (here + y_plus(here, vy_hi[pl.ds(x, 1), :] * y_hi_on))
        k_zm, k_zp = 0.5 * (here + z_minus(here)), 0.5 * (here + z_plus(here))
        kx[x] = k_xm
        kx[x + 1] = k_xp
        kym[x] = k_ym
        kyp[x] = k_yp
        kzm[x] = k_zm
        kzp[x] = k_zp
        damp[x] = relax_weight / (k_xm + k_xp + k_ym + k_yp + k_zm + k_zp)
        return 0

    lax.fori_loop(0, NX_L, couplings, 0)

    for n in range(SWEEPS):
        old, new = (state_a, state_b) if n % 2 == 0 else (state_b, state_a)
        for c in halo(n, old):
            c.wait()
        old[:, 0] = x_lo[n] * x_lo_on
        old[:, NX_L + 1] = x_hi[n] * x_hi_on

        def sweep(x, _, n=n, old=old, new=new):
            low = y_lo[n, x] * y_lo_on
            high = y_hi[n, x] * y_hi_on
            press = old[3, x + 1]
            press_near = [
                old[3, x],
                y_minus(press, low[3:4]),
                z_minus(press),
            ]
            weights = [kx[x + 1], kx[x], kyp[x], kym[x], kzp[x], kzm[x]]
            scale = damp[x]
            divergence = jnp.zeros_like(press)
            fresh = []
            for c in range(3):
                v = old[c, x + 1]
                near = [
                    old[c, x + 2],
                    old[c, x],
                    y_plus(v, high[c : c + 1]),
                    y_minus(v, low[c : c + 1]),
                    z_plus(v),
                    z_minus(v),
                ]
                forcing = press_near[c] - press
                for w, s in zip(weights, near):
                    forcing = forcing + w * (s - v)
                if c == 2:
                    forcing = forcing - gravity * dens_s[x]
                fresh.append(v + scale * forcing)
                divergence = divergence + (near[2 * c] - v)
            fresh.append(press - pressure_rate * visc_s[x + 1] * divergence)
            for c in range(4):
                new[c, x + 1] = fresh[c]
            if n + 1 < SWEEPS:
                face_lo[n + 1, x] = jnp.concatenate([f[0:1] for f in fresh], axis=0)
                face_hi[n + 1, x] = jnp.concatenate([f[15:16] for f in fresh], axis=0)
            return 0

        lax.fori_loop(0, NX_L, sweep, 0)
        if n + 1 < SWEEPS:
            for c in halo(n + 1, new):
                c.start()
    last = state_a if SWEEPS % 2 == 0 else state_b
    stores = [
        pltpu.make_async_copy(last.at[pl.ds(0, 3), pl.ds(1, NX_L)], velocity_out, load_sem.at[5]),
        pltpu.make_async_copy(last.at[3, pl.ds(1, NX_L)], pressure_out, load_sem.at[6]),
    ]
    for c in stores:
        c.start()

    def wait_bricks(k, _):
        remote(
            brick_send.at[k], bricks_out.at[after(k)], b_send.at[k], b_recv.at[k], (g, before(k))
        ).wait()
        return 0

    lax.fori_loop(1, OWNERS, wait_bricks, 0)
    own.wait()
    for c in stores:
        c.wait()


def grid_call(block_brick, velocity, pressure, visc, dens):
    vm = pl.BlockSpec(memory_space=pltpu.VMEM)
    hbm = pl.BlockSpec(memory_space=pl.ANY)
    dma = pltpu.SemaphoreType.DMA
    field = (NX_L, NY_L, NZ)
    padded = (NX_L + 2, NY_L, NZ)
    return pl.pallas_call(
        grid_kernel,
        out_shape=(
            jax.ShapeDtypeStruct((OWNERS, 8, 128), F32),
            jax.ShapeDtypeStruct((OWNERS, CAP, 384), F32),
            jax.ShapeDtypeStruct((3,) + field, F32),
            jax.ShapeDtypeStruct(field, F32),
        ),
        in_specs=[vm] + [hbm] * 4,
        out_specs=(vm, hbm, hbm, hbm),
        scratch_shapes=[
            VMEM((4,) + padded, F32),
            VMEM((4,) + padded, F32),
            VMEM(padded, F32),
            VMEM(field, F32),
            VMEM((2, 1536, 128), F32),
            VMEM((BRICKS, 384), BF16),
            VMEM((BRICKS, 384), BF16),
            VMEM((4 * CAP, BRICKS), BF16),
            VMEM((OWNERS, 8, 128), F32),
            VMEM((OWNERS, 8, 128), F32),
            VMEM((OWNERS, CAP, 384), F32),
            VMEM((NX_L + 1, NY_L, NZ), F32),
            VMEM(field, F32),
            VMEM(field, F32),
            VMEM(field, F32),
            VMEM(field, F32),
            VMEM(field, F32),
            VMEM((SWEEPS, 4, NY_L, NZ), F32),
            VMEM((SWEEPS, 4, NY_L, NZ), F32),
            VMEM((SWEEPS, NX_L, 4, NZ), F32),
            VMEM((SWEEPS, NX_L, 4, NZ), F32),
            VMEM((SWEEPS, NX_L, 4, NZ), F32),
            VMEM((SWEEPS, NX_L, 4, NZ), F32),
            VMEM((NY_L, NZ), F32),
            VMEM((NY_L, NZ), F32),
            VMEM((NX_L, NZ), F32),
            VMEM((NX_L, NZ), F32),
            VMEM((NX_L, NZ), F32),
            VMEM((NX_L, NZ), F32),
            dma((7,)),
            dma((OWNERS,)),
            dma((OWNERS,)),
            dma((OWNERS,)),
            dma((OWNERS,)),
            dma((SWEEPS, 4)),
            dma((SWEEPS, 4)),
            dma((4,)),
            dma((4,)),
        ],
        compiler_params=pltpu.CompilerParams(
            collective_id=0, has_side_effects=True, vmem_limit_bytes=50 << 20
        ),
        name="grid_step",
    )(block_brick, velocity, pressure, visc, dens)


def moments_kernel(
    moments, ids, visc, dens, visc_out, dens_out,
    arrived, hits, hi_s, lo_s, sums, cells, send, recv, own_sem,
):
    g, me, after, before = peers()
    barrier = pltpu.get_barrier_semaphore()
    for k in range(1, OWNERS):
        pl.semaphore_signal(barrier, inc=1, device_id=(g, after(k)), device_id_type=MESH)
    pl.semaphore_wait(barrier, OWNERS - 1)

    def copy(k):
        return remote(moments.at[after(k)], arrived.at[k], send.at[k], recv.at[k], (g, after(k)))

    def start(k, _):
        copy(k).start()
        return 0

    lax.fori_loop(1, OWNERS, start, 0)
    own = pltpu.make_async_copy(moments.at[me], arrived.at[0], own_sem)
    own.start()

    lane = lax.broadcasted_iota(jnp.int32, (8, 128), 1)
    rows = [jnp.full((8, 128), -1.0, F32) for _ in range(6)]
    for k in range(OWNERS):
        at = CAP * k
        t, off = at // 128, at % 128
        tile = ids[k]
        turned = pltpu.roll(tile, off, 1) if off else tile
        rows[t] = jnp.where((lane >= off) & (lane < off + CAP), turned, rows[t])
        over = off + CAP - 128
        if over > 0:
            rows[t + 1] = jnp.where(lane < over, turned, rows[t + 1])

    wide = [jnp.concatenate([r, r], axis=0) for r in rows]
    sub = lax.broadcasted_iota(jnp.int32, (16, 128), 0).astype(F32)

    def mark_hits(r, _):
        at = pl.multiple_of(r * 16, 16)
        here = sub + (r * 16).astype(F32)
        for t in range(6):
            hits[pl.ds(at, 16), pl.ds(128 * t, 128)] = jnp.where(wide[t] == here, 1.0, 0.0).astype(BF16)
        return 0

    lax.fori_loop(0, BRICKS // 16, mark_hits, 0)

    def arrive(k, _):
        copy(k).wait()
        return 0

    own.wait()
    lax.fori_loop(1, OWNERS, arrive, 0)

    def pieces(k, _):
        hi, lo = split(arrived[k])
        at = pl.multiple_of(k * CAP, 16)
        hi_s[pl.ds(at, CAP), :] = hi
        lo_s[pl.ds(at, CAP), :] = lo
        return 0

    lax.fori_loop(0, OWNERS, pieces, 0)

    def scatter(n, _):
        at = pl.ds(pl.multiple_of(n * 256, 256), 256)
        block = hits[at, :]
        total = jnp.dot(block, hi_s[...], preferred_element_type=F32)
        total = total + jnp.dot(block, lo_s[...], preferred_element_type=F32)
        for m in range(3):
            sums[m, at, :] = total[:, 128 * m : 128 * m + 128]
        return 0

    lax.fori_loop(0, 4, scatter, 0)
    group = lane // 8

    def to_cells(n, _):
        bj, h = n // 2, lax.rem(n, 2)
        for m in range(3):
            tiles = [
                sums[m, pl.ds(pl.multiple_of((bj * 32 + h * 16 + t) * 8, 8), 8), :] for t in range(16)
            ]
            tiles = group_transpose(tiles, group)
            for i in range(4):
                for j in range(4):
                    cells[m, h, pl.ds(16 * i + 4 * bj + j, 8, stride=64), :] = tiles[4 * i + j]
        return 0

    lax.fori_loop(0, 8, to_cells, 0)

    def finish(x, _):
        at = pl.ds(pl.multiple_of(x * 16, 16), 16)
        for h in range(2):
            part = pl.ds(128 * h, 128)
            below = 1.0 / (cells[0, h, at, :] + 1.0)
            visc_out[x, :, part] = jnp.exp((cells[1, h, at, :] + jnp.log(visc[x, :, part])) * below)
            dens_out[x, :, part] = (cells[2, h, at, :] + dens[x, :, part]) * below
        return 0

    lax.fori_loop(0, NX_L, finish, 0)


def moments_call(moments, ids, visc, dens):
    vm = pl.BlockSpec(memory_space=pltpu.VMEM)
    hbm = pl.BlockSpec(memory_space=pl.ANY)
    dma = pltpu.SemaphoreType.DMA
    field = jax.ShapeDtypeStruct((NX_L, NY_L, NZ), F32)
    return pl.pallas_call(
        moments_kernel,
        out_shape=(field, field),
        in_specs=[hbm, vm, vm, vm],
        out_specs=(vm, vm),
        scratch_shapes=[
            VMEM((OWNERS, CAP, 384), F32),
            VMEM((BRICKS, OWNERS * CAP), BF16),
            VMEM((OWNERS * CAP, 384), BF16),
            VMEM((OWNERS * CAP, 384), BF16),
            VMEM((3, BRICKS, 128), F32),
            VMEM((3, 2, 512, 128), F32),
            dma((OWNERS,)),
            dma((OWNERS,)),
            dma,
        ],
        compiler_params=pltpu.CompilerParams(
            collective_id=1, has_side_effects=True, vmem_limit_bytes=50 << 20
        ),
        name="moments_home",
    )(moments, ids, visc, dens)


def per_device(
    velocity, pressure, cell_visc, cell_dens, block_brick, block_counts, positions, start_visc, marker_dens
):
    ids, bricks, velocity_next, pressure_next = grid_call(
        block_brick, velocity, pressure, cell_visc, cell_dens
    )
    marker_visc, moments = marker_call(block_counts, positions, start_visc, marker_dens, bricks)
    visc_next, dens_next = moments_call(moments, ids, cell_visc, cell_dens)
    return velocity_next, pressure_next, visc_next, dens_next, marker_visc


def solution(mesh):
    in_specs = (
        P(None, "grid", "mark", None),
        P("grid", "mark", None),
        P("grid", "mark", None),
        P("grid", "mark", None),
        P(("grid", "mark"), None),
        P(("grid", "mark"), None),
        P(("grid", "mark"), None, None, None),
        P(("grid", "mark"), None, None),
        P(("grid", "mark"), None, None),
    )
    out_specs = (
        P(None, "grid", "mark", None),
        P("grid", "mark", None),
        P("grid", "mark", None),
        P("grid", "mark", None),
        P(("grid", "mark"), None, None),
    )
    return jax.shard_map(
        per_device, mesh=mesh, in_specs=in_specs, out_specs=out_specs, check_vma=False
    )
```

```python
import functools
import math
import jax
import jax.numpy as jnp
from jax import lax
from jax.sharding import PartitionSpec as P
from jax.experimental import pallas as pl
from jax.experimental.pallas import tpu as pltpu

F32, BF16 = jnp.float32, jnp.bfloat16
VMEM = pltpu.VMEM
CAP, BLOCK, OWNERS = 48, 256, 16
NT = (((1,), (1,)), ((), ()))
GROUPS = 6


def split(x):
    hi = x.astype(BF16)
    return hi, (x - hi.astype(F32)).astype(BF16)


def axis_weights(fraction, cells):
    half = 0.5 * cells
    factor = jnp.exp(2.0 * cells * fraction - 2.0 * half)
    centres = [i + 0.5 - half for i in range(cells)]
    powers = [None, factor]
    for i in range(2, cells):
        powers.append(powers[i // 2] * powers[i - i // 2])
    raw = [jnp.full_like(factor, math.exp(-centres[0] ** 2))]
    raw += [math.exp(-(centres[i] ** 2)) * powers[i] for i in range(1, cells)]
    total = functools.reduce(jnp.add, raw)
    scale = 1.0 / total
    weights = [r * scale for r in raw]
    mean = functools.reduce(jnp.add, [c * w for c, w in zip(centres, weights)])
    return weights, mean


def masks():
    sub = lax.broadcasted_iota(jnp.int32, (8, 128), 0)
    lane = lax.broadcasted_iota(jnp.int32, (8, 128), 1)
    sub2 = lax.broadcasted_iota(jnp.int32, (8, 256), 0)
    return sub, lane, sub2, sub < 4, sub2 < 4


def both(x, low):
    turned = pltpu.roll(x, 4, 0)
    return jnp.where(low, x, turned), jnp.where(low, turned, x)


def fold(a, b, low):
    return jnp.where(low, a, b) + pltpu.roll(jnp.where(low, b, a), 4, 0)


def skew(x, sub, sign):
    out = x
    for s in range(1, 4):
        out = jnp.where(sub % 4 == s, pltpu.roll(x, (sign * 32 * s) % 128, 1), out)
    return out


def pieces(tiles):
    his, los = [], []
    for n in range(0, len(tiles), 2):
        hi, lo = split(jnp.concatenate(tiles[n : n + 2], axis=0))
        his.append(hi)
        los.append(lo)
    return jnp.concatenate(his + los, axis=0)


def prepare(q, k, row, u, pos, bricks, wz_s, wy_s, planes):
    rows = pl.ds(row, 8)
    sub, lane, sub2, low, low2 = masks()
    wx, mean_x = axis_weights(pos[q, 0, rows, :], 4)
    wy, mean_y = axis_weights(pos[q, 1, rows, :], 4)
    wz, mean_z = axis_weights(pos[q, 2, rows, :], 8)
    for h in range(2):
        part = slice(128 * h, 128 * h + 128)
        for n in range(8):
            wz_s[u, h, pl.ds(8 * n, 8), :] = wz[n][:, part]
        for j in range(4):
            wy_s[u, h, pl.ds(8 * j, 8), :] = wy[j][:, part]
    for b in range(8):
        for h in range(2):
            col = wz_s[u, h, pl.ds(b, 8, stride=8), :]
            for jp in range(2):
                pair = [
                    col * jnp.broadcast_to(wy_s[u, h, pl.ds(8 * j + b, 1), :], (8, 128))
                    for j in (2 * jp, 2 * jp + 1)
                ]
                hi, lo = split(jnp.concatenate(pair, axis=0))
                at = 32 * (b % 4) + 16 * jp
                planes[u, b // 4, pl.ds(at, 16), pl.ds(128 * h, 128)] = hi
                planes[u, b // 4, pl.ds(128 + at, 16), pl.ds(128 * h, 128)] = lo

    diag = (lane // 32) == (sub % 4)
    turned_i = (lane // 32 + 4 - sub % 4) % 4
    c_i = turned_i.astype(F32) - 1.5
    c_j = ((lane // 8) % 4).astype(F32) - 1.5
    c_k = (lane % 8).astype(F32) - 3.5
    v = [both(skew(bricks[k, rows, pl.ds(128 * c, 128)], sub, 1), low) for c in range(3)]
    lefts = []
    for side in range(2):
        vx, vy, vz = [x[side] for x in v]
        kinds = [
            vx, vy, vz, c_j * vy, c_k * vz,
            c_j * vx + c_i * vy, c_k * vx + c_i * vz, c_k * vy + c_j * vz,
        ]
        tiles = []
        for kind in kinds:
            turned = [kind] + [pltpu.roll(kind, 128 - 32 * i, 1) for i in range(1, 4)]
            for ip in range(2):
                tile = jnp.where(low, turned[2 * ip], turned[2 * ip + 1])
                tiles.append(jnp.where(diag, tile, 0.0))
        lefts.append(pieces(tiles))
    pairs = ([], [])
    for ip in range(2):
        first, second = both(wx[2 * ip], low2), both(wx[2 * ip + 1], low2)
        for side in range(2):
            pairs[side].append(jnp.where(low2, first[side], second[side]))
    return lefts, pairs, (mean_x, mean_y, mean_z)


def strain(q, k, row, u, prepared, visc, dens, marker_out, count, planes):
    rows = pl.ds(row, 8)
    sub, lane, sub2, low, low2 = masks()
    lefts, pairs, (mean_x, mean_y, mean_z) = prepared
    results = []
    for side in range(2):
        left = jnp.concatenate([lefts[side], lefts[side]], axis=1)
        out = jnp.dot(left, planes[u, side], preferred_element_type=F32)
        results.append(out[:128] + out[128:])
    centred = [
        [pairs[side][ip] * jnp.where(low2, 2 * ip - 1.5, 2 * ip - 0.5) for ip in range(2)]
        for side in range(2)
    ]

    def along_x(kind, weights):
        at = 16 * kind
        sums = [
            results[side][at : at + 8] * weights[side][0]
            + results[side][at + 8 : at + 16] * weights[side][1]
            for side in range(2)
        ]
        return fold(*sums, low2)

    vx, vy, vz, yy, zz, xy, xz, yz = [along_x(n, pairs) for n in range(8)]
    xx = along_x(0, centred) - mean_x * vx
    yy = yy - mean_y * vy
    zz = zz - mean_z * vz
    xy = xy - mean_y * vx - mean_x * vy
    xz = xz - mean_z * vx - mean_x * vz
    yz = yz - mean_z * vy - mean_y * vz
    invariant = 2.0 * (xx * xx + yy * yy + zz * zz) + xy * xy + xz * xz + yz * yz
    shift = jnp.log(1.0 + invariant * 4.0) * (1.0 / 3.0)
    start = visc[q, rows, :]
    live = (sub2 + row) < count
    weakened = start * jnp.exp(-shift)
    marker_out[k, rows, :] = jnp.where(live, weakened, 0.0)
    carried = [
        jnp.where(live, 1.0, 0.0),
        jnp.where(live, jnp.log(weakened), 0.0),
        jnp.where(live, dens[q, rows, :], 0.0),
    ]
    carried = [both(c, low2) for c in carried]
    return [
        pieces([carried[m][side] * pairs[side][ip] for m in range(3) for ip in range(2)])
        for side in range(2)
    ]


def deposit(k, row, u, lefts, moments, planes):
    rows = pl.ds(row, 8)
    sub, lane, sub2, low, low2 = masks()
    diag = (lane // 32) == (sub % 4)
    sums = []
    for side in range(2):
        out = lax.dot_general(lefts[side], planes[u, side], NT, preferred_element_type=F32)
        sums.append(out[:48, :128] + out[:48, 128:] + out[48:, :128])
    for m in range(3):
        halves = []
        for side in range(2):
            p = [jnp.where(diag, sums[side][16 * m + 8 * ip : 16 * m + 8 * ip + 8], 0.0) for ip in range(2)]
            halves.append(
                jnp.where(low, p[0], pltpu.roll(p[0], 32, 1))
                + jnp.where(low, pltpu.roll(p[1], 64, 1), pltpu.roll(p[1], 96, 1))
            )
        moments[k, rows, pl.ds(128 * m, 128)] = skew(fold(*halves, low), sub, -1)


NX_L, NY_L, NZ = 32, 16, 256
BRICKS = 1024
MESH = pl.DeviceIdType.MESH
SWEEPS = 4
relax_weight = 0.6
pressure_rate = 0.25
gravity = 1.0


def group_transpose(tiles, group):
    tiles = list(tiles)
    for d in (8, 4, 2, 1):
        upper = (group & d) != 0
        for t in range(16):
            if t & d == 0:
                a, b = tiles[t], tiles[t + d]
                tiles[t] = jnp.where(upper, pltpu.roll(b, 8 * d, 1), a)
                tiles[t + d] = jnp.where(upper, b, pltpu.roll(a, 128 - 8 * d, 1))
    return tiles


def peers():
    g, me = lax.axis_index("grid"), lax.axis_index("mark")

    def after(k):
        return lax.rem(me + k, OWNERS)

    def before(k):
        return lax.rem(me + OWNERS - k, OWNERS)

    return g, me, after, before


def remote(src, dst, send, recv, device):
    return pltpu.make_async_remote_copy(
        src_ref=src, dst_ref=dst, send_sem=send, recv_sem=recv, device_id=device, device_id_type=MESH
    )


def step_kernel(
    counts, brick_ids, velocity, pressure, visc, dens, positions, start_visc, marker_dens,
    velocity_out, pressure_out, visc_out, dens_out, marker_out,
    state_a, state_b, visc_s, dens_s, halves, planes_hi, planes_lo, one_hot, ids_send, ids_recv,
    brick_send, bricks, kx, kym, kyp, kzm, kzp, damp, x_lo, x_hi, face_lo, face_hi, y_lo, y_hi,
    vx_lo, vx_hi, vface_lo, vface_hi, vy_lo, vy_hi, pos, mvisc, mdens, marker_s, moments, arrived,
    wz_s, wy_s, planes, hits, hi_s, lo_s, sums, cells,
    load_sem, id_send, id_recv, b_send, b_recv, h_send, h_recv, v_send, v_recv, m_send, m_recv, out_sem,
):
    g, me, after, before = peers()
    ahead, behind = lax.rem(g + 1, 8), lax.rem(g + 7, 8)
    loads = [
        pltpu.make_async_copy(velocity, state_a.at[pl.ds(0, 3), pl.ds(1, NX_L)], load_sem.at[0]),
        pltpu.make_async_copy(pressure, state_a.at[3, pl.ds(1, NX_L)], load_sem.at[1]),
        pltpu.make_async_copy(visc, visc_s.at[pl.ds(1, NX_L)], load_sem.at[2]),
        pltpu.make_async_copy(dens, dens_s, load_sem.at[3]),
    ]
    marker_loads = [
        pltpu.make_async_copy(positions, pos, load_sem.at[4]),
        pltpu.make_async_copy(start_visc, mvisc, load_sem.at[7]),
        pltpu.make_async_copy(marker_dens, mdens, load_sem.at[8]),
    ]
    for c in loads + marker_loads:
        c.start()
    barrier = pltpu.get_barrier_semaphore()
    for k in range(1, OWNERS):
        pl.semaphore_signal(barrier, inc=1, device_id=(g, after(k)), device_id_type=MESH)
    pl.semaphore_signal(barrier, inc=1, device_id=(ahead, me), device_id_type=MESH)
    pl.semaphore_signal(barrier, inc=1, device_id=(behind, me), device_id_type=MESH)

    number = brick_ids[...]
    number = (((number >> 5) & 3) * 32 + (number & 31)) * 8 + (number >> 7)
    number = number.astype(F32)
    ids_send[...] = jnp.full((OWNERS, 8, 128), -1.0, F32)
    for q in range(OWNERS):
        ids_send[q, :, pl.ds(0, CAP)] = jnp.broadcast_to(number[q : q + 1], (8, CAP))
    pl.semaphore_wait(barrier, OWNERS + 1)

    def send_ids(k, _):
        remote(ids_send.at[after(k)], ids_recv.at[k], id_send.at[k], id_recv.at[k], (g, after(k))).start()
        return 0

    lax.fori_loop(1, OWNERS, send_ids, 0)
    ids_recv[0] = ids_send[me]
    for c in loads:
        c.wait()

    def halo(n, state):
        return [
            remote(state.at[:, 1], x_hi.at[n], h_send.at[n, 0], h_recv.at[n, 0], (behind, me)),
            remote(state.at[:, NX_L], x_lo.at[n], h_send.at[n, 1], h_recv.at[n, 1], (ahead, me)),
            remote(face_lo.at[n], y_hi.at[n], h_send.at[n, 2], h_recv.at[n, 2], (g, before(1))),
            remote(face_hi.at[n], y_lo.at[n], h_send.at[n, 3], h_recv.at[n, 3], (g, after(1))),
        ]

    def first_faces(x, _):
        face_lo[0, x] = jnp.concatenate([state_a[c, x + 1, 0:1, :] for c in range(4)], axis=0)
        face_hi[0, x] = jnp.concatenate([state_a[c, x + 1, 15:16, :] for c in range(4)], axis=0)
        return 0

    lax.fori_loop(0, NX_L, first_faces, 0)
    for x in range(NX_L):
        vface_lo[x : x + 1, :] = visc_s[x + 1, 0:1, :]
        vface_hi[x : x + 1, :] = visc_s[x + 1, 15:16, :]
    visc_halo = [
        remote(visc_s.at[1], vx_hi, v_send.at[0], v_recv.at[0], (behind, me)),
        remote(visc_s.at[NX_L], vx_lo, v_send.at[1], v_recv.at[1], (ahead, me)),
        remote(vface_lo, vy_hi, v_send.at[2], v_recv.at[2], (g, before(1))),
        remote(vface_hi, vy_lo, v_send.at[3], v_recv.at[3], (g, after(1))),
    ]
    for c in halo(0, state_a) + visc_halo:
        c.start()

    def to_halves(x, _):
        for c in range(3):
            plane = state_a[c, x + 1]
            at = pl.multiple_of(c * 512 + x * 16, 16)
            for h in range(2):
                halves[h, pl.ds(at, 16), :] = plane[:, 128 * h : 128 * h + 128]
        return 0

    lax.fori_loop(0, NX_L, to_halves, 0)
    group = lax.broadcasted_iota(jnp.int32, (8, 128), 1) // 8

    def to_bricks(n, _):
        bj, h = n // 2, lax.rem(n, 2)
        for c in range(3):
            tiles = [
                halves[h, pl.ds(c * 512 + 16 * i + 4 * bj + j, 8, stride=64), :]
                for i in range(4)
                for j in range(4)
            ]
            tiles = group_transpose(tiles, group)
            for t in range(0, 16, 2):
                hi, lo = split(jnp.concatenate(tiles[t : t + 2], axis=0))
                at = pl.multiple_of((bj * 32 + h * 16 + t) * 8, 16)
                planes_hi[pl.ds(at, 16), pl.ds(128 * c, 128)] = hi
                planes_lo[pl.ds(at, 16), pl.ds(128 * c, 128)] = lo
        return 0

    lax.fori_loop(0, 8, to_bricks, 0)

    def wait_ids(k, _):
        remote(ids_send.at[after(k)], ids_recv.at[k], id_send.at[k], id_recv.at[k], (g, after(k))).wait()
        return 0

    lax.fori_loop(1, OWNERS, wait_ids, 0)

    def brick_copy(k):
        return remote(
            brick_send.at[k], bricks.at[k], b_send.at[k], b_recv.at[k], (g, before(k))
        )

    lanes = lax.broadcasted_iota(jnp.int32, (CAP, 128), 1).astype(F32)

    def gather(n, _):
        for m in range(4):
            column = jnp.transpose(jnp.broadcast_to(ids_recv[4 * n + m][0:1, :], (128, 128)))[:CAP]
            for t in range(8):
                hit = jnp.where(column == lanes + 128.0 * t, 1.0, 0.0).astype(BF16)
                one_hot[pl.ds(CAP * m, CAP), pl.ds(128 * t, 128)] = hit
        found = jnp.dot(one_hot[...], planes_hi[...], preferred_element_type=F32)
        found = found + jnp.dot(one_hot[...], planes_lo[...], preferred_element_type=F32)
        for m in range(4):
            brick_send[4 * n + m] = found[CAP * m : CAP * m + CAP]
        for m in range(4):
            k = 4 * n + m

            @pl.when(k > 0)
            def _():
                brick_copy(k).start()

        return 0

    lax.fori_loop(0, 4, gather, 0)
    bricks[0] = brick_send[0]
    for c in marker_loads:
        c.wait()

    def moment_copy(k):
        return remote(moments.at[k], arrived.at[k], m_send.at[k], m_recv.at[k], (g, after(k)))

    def marker_store(k):
        return pltpu.make_async_copy(marker_s.at[k], marker_out.at[after(k)], out_sem.at[k])

    def owner_markers(k, _):
        q = after(k)
        count = counts[0, q]

        @pl.when(k > 0)
        def _():
            brick_copy(k).wait()

        ready, spread = {}, {}
        for t in range(GROUPS + 2):
            if t < GROUPS:
                ready[t] = prepare(q, k, 8 * t, t, pos, bricks, wz_s, wy_s, planes)
            u = t - 1
            if 0 <= u < GROUPS:
                spread[u] = strain(q, k, 8 * u, u, ready.pop(u), mvisc, mdens, marker_s, count, planes)
            u = t - 2
            if 0 <= u < GROUPS:
                deposit(k, 8 * u, u, spread.pop(u), moments, planes)
        marker_store(k).start()

        @pl.when(k > 0)
        def _():
            moment_copy(k).start()

        return 0

    lax.fori_loop(0, 1, owner_markers, 0)

    x_lo_on = (g > 0).astype(F32)
    x_hi_on = (g < 7).astype(F32)
    y_lo_on = (me > 0).astype(F32)
    y_hi_on = (me < OWNERS - 1).astype(F32)
    row = lax.broadcasted_iota(jnp.int32, (NY_L, NZ), 0)
    col = lax.broadcasted_iota(jnp.int32, (NY_L, NZ), 1)
    first_y, last_y = row == 0, row == NY_L - 1
    first_z, last_z = col == 0, col == NZ - 1

    def y_minus(plane, edge):
        return jnp.where(first_y, jnp.broadcast_to(edge, plane.shape), pltpu.roll(plane, 1, 0))

    def y_plus(plane, edge):
        return jnp.where(last_y, jnp.broadcast_to(edge, plane.shape), pltpu.roll(plane, NY_L - 1, 0))

    def z_minus(plane):
        return jnp.where(first_z, 0.0, pltpu.roll(plane, 1, 1))

    def z_plus(plane):
        return jnp.where(last_z, 0.0, pltpu.roll(plane, NZ - 1, 1))

    for c in visc_halo:
        c.wait()
    visc_s[0] = vx_lo[...] * x_lo_on
    visc_s[NX_L + 1] = vx_hi[...] * x_hi_on

    def couplings(x, _):
        here, below, above = visc_s[x + 1], visc_s[x], visc_s[x + 2]
        k_xm, k_xp = 0.5 * (here + below), 0.5 * (here + above)
        k_ym = 0.5 * (here + y_minus(here, vy_lo[pl.ds(x, 1), :] * y_lo_on))
        k_yp = 0.5 * (here + y_plus(here, vy_hi[pl.ds(x, 1), :] * y_hi_on))
        k_zm, k_zp = 0.5 * (here + z_minus(here)), 0.5 * (here + z_plus(here))
        kx[x] = k_xm
        kx[x + 1] = k_xp
        kym[x] = k_ym
        kyp[x] = k_yp
        kzm[x] = k_zm
        kzp[x] = k_zp
        damp[x] = relax_weight / (k_xm + k_xp + k_ym + k_yp + k_zm + k_zp)
        return 0

    lax.fori_loop(0, NX_L, couplings, 0)

    for n in range(SWEEPS):
        old, new = (state_a, state_b) if n % 2 == 0 else (state_b, state_a)
        for c in halo(n, old):
            c.wait()
        old[:, 0] = x_lo[n] * x_lo_on
        old[:, NX_L + 1] = x_hi[n] * x_hi_on

        def sweep(x, _, n=n, old=old, new=new):
            low = y_lo[n, x] * y_lo_on
            high = y_hi[n, x] * y_hi_on
            press = old[3, x + 1]
            press_near = [
                old[3, x],
                y_minus(press, low[3:4]),
                z_minus(press),
            ]
            weights = [kx[x + 1], kx[x], kyp[x], kym[x], kzp[x], kzm[x]]
            scale = damp[x]
            divergence = jnp.zeros_like(press)
            fresh = []
            for c in range(3):
                v = old[c, x + 1]
                near = [
                    old[c, x + 2],
                    old[c, x],
                    y_plus(v, high[c : c + 1]),
                    y_minus(v, low[c : c + 1]),
                    z_plus(v),
                    z_minus(v),
                ]
                forcing = press_near[c] - press
                for w, s in zip(weights, near):
                    forcing = forcing + w * (s - v)
                if c == 2:
                    forcing = forcing - gravity * dens_s[x]
                fresh.append(v + scale * forcing)
                divergence = divergence + (near[2 * c] - v)
            fresh.append(press - pressure_rate * visc_s[x + 1] * divergence)
            for c in range(4):
                new[c, x + 1] = fresh[c]
            if n + 1 < SWEEPS:
                face_lo[n + 1, x] = jnp.concatenate([f[0:1] for f in fresh], axis=0)
                face_hi[n + 1, x] = jnp.concatenate([f[15:16] for f in fresh], axis=0)
            return 0

        lax.fori_loop(0, NX_L, sweep, 0)
        if n + 1 < SWEEPS:
            for c in halo(n + 1, new):
                c.start()
        if n + 1 < SWEEPS:
            lax.fori_loop(1 + 5 * n, 6 + 5 * n, owner_markers, 0)
    last = state_a if SWEEPS % 2 == 0 else state_b
    stores = [
        pltpu.make_async_copy(last.at[pl.ds(0, 3), pl.ds(1, NX_L)], velocity_out, load_sem.at[5]),
        pltpu.make_async_copy(last.at[3, pl.ds(1, NX_L)], pressure_out, load_sem.at[6]),
    ]
    for c in stores:
        c.start()
    arrived[0] = moments[0]

    lane = lax.broadcasted_iota(jnp.int32, (8, 128), 1)
    rows = [jnp.full((8, 128), -1.0, F32) for _ in range(6)]
    for k in range(OWNERS):
        at = CAP * k
        t, off = at // 128, at % 128
        tile = ids_recv[k]
        turned = pltpu.roll(tile, off, 1) if off else tile
        rows[t] = jnp.where((lane >= off) & (lane < off + CAP), turned, rows[t])
        over = off + CAP - 128
        if over > 0:
            rows[t + 1] = jnp.where(lane < over, turned, rows[t + 1])

    wide = [jnp.concatenate([r, r], axis=0) for r in rows]
    sub = lax.broadcasted_iota(jnp.int32, (16, 128), 0).astype(F32)

    def mark_hits(r, _):
        at = pl.multiple_of(r * 16, 16)
        here = sub + (r * 16).astype(F32)
        for t in range(6):
            hits[pl.ds(at, 16), pl.ds(128 * t, 128)] = jnp.where(wide[t] == here, 1.0, 0.0).astype(BF16)
        return 0

    lax.fori_loop(0, BRICKS // 16, mark_hits, 0)

    def arrive(k, _):
        moment_copy(k).wait()
        return 0

    lax.fori_loop(1, OWNERS, arrive, 0)

    def moment_pieces(k, _):
        hi, lo = split(arrived[k])
        at = pl.multiple_of(k * CAP, 16)
        hi_s[pl.ds(at, CAP), :] = hi
        lo_s[pl.ds(at, CAP), :] = lo
        return 0

    lax.fori_loop(0, OWNERS, moment_pieces, 0)

    def scatter(n, _):
        at = pl.ds(pl.multiple_of(n * 256, 256), 256)
        block = hits[at, :]
        total = jnp.dot(block, hi_s[...], preferred_element_type=F32)
        total = total + jnp.dot(block, lo_s[...], preferred_element_type=F32)
        for m in range(3):
            sums[m, at, :] = total[:, 128 * m : 128 * m + 128]
        return 0

    lax.fori_loop(0, 4, scatter, 0)
    def to_cells(n, _):
        bj, h = n // 2, lax.rem(n, 2)
        for m in range(3):
            tiles = [
                sums[m, pl.ds(pl.multiple_of((bj * 32 + h * 16 + t) * 8, 8), 8), :] for t in range(16)
            ]
            tiles = group_transpose(tiles, group)
            for i in range(4):
                for j in range(4):
                    cells[m, h, pl.ds(16 * i + 4 * bj + j, 8, stride=64), :] = tiles[4 * i + j]
        return 0

    lax.fori_loop(0, 8, to_cells, 0)

    def finish(x, _):
        at = pl.ds(pl.multiple_of(x * 16, 16), 16)
        for h in range(2):
            part = pl.ds(128 * h, 128)
            below = 1.0 / (cells[0, h, at, :] + 1.0)
            visc_out[x, :, part] = jnp.exp((cells[1, h, at, :] + jnp.log(visc_s[x + 1, :, part])) * below)
            dens_out[x, :, part] = (cells[2, h, at, :] + dens_s[x, :, part]) * below
        return 0

    lax.fori_loop(0, NX_L, finish, 0)

    def wait_markers(k, _):
        marker_store(k).wait()
        return 0

    lax.fori_loop(0, OWNERS, wait_markers, 0)
    for c in stores:
        c.wait()


def per_device(
    velocity, pressure, cell_visc, cell_dens, block_brick, block_counts, positions, start_visc, marker_dens
):
    vm = pl.BlockSpec(memory_space=pltpu.VMEM)
    hbm = pl.BlockSpec(memory_space=pl.ANY)
    dma = pltpu.SemaphoreType.DMA
    field = (NX_L, NY_L, NZ)
    padded = (NX_L + 2, NY_L, NZ)
    shape = jax.ShapeDtypeStruct
    return pl.pallas_call(
        step_kernel,
        out_shape=(
            shape((3,) + field, F32),
            shape(field, F32),
            shape(field, F32),
            shape(field, F32),
            shape((OWNERS, CAP, BLOCK), F32),
        ),
        in_specs=[pl.BlockSpec(memory_space=pltpu.SMEM), vm] + [hbm] * 7,
        out_specs=(hbm, hbm, vm, vm, hbm),
        scratch_shapes=[
            VMEM((4,) + padded, F32),
            VMEM((4,) + padded, F32),
            VMEM(padded, F32),
            VMEM(field, F32),
            VMEM((2, 1536, 128), F32),
            VMEM((BRICKS, 384), BF16),
            VMEM((BRICKS, 384), BF16),
            VMEM((4 * CAP, BRICKS), BF16),
            VMEM((OWNERS, 8, 128), F32),
            VMEM((OWNERS, 8, 128), F32),
            VMEM((OWNERS, CAP, 384), F32),
            VMEM((OWNERS, CAP, 384), F32),
            VMEM((NX_L + 1, NY_L, NZ), F32),
            VMEM(field, F32),
            VMEM(field, F32),
            VMEM(field, F32),
            VMEM(field, F32),
            VMEM(field, F32),
            VMEM((SWEEPS, 4, NY_L, NZ), F32),
            VMEM((SWEEPS, 4, NY_L, NZ), F32),
            VMEM((SWEEPS, NX_L, 4, NZ), F32),
            VMEM((SWEEPS, NX_L, 4, NZ), F32),
            VMEM((SWEEPS, NX_L, 4, NZ), F32),
            VMEM((SWEEPS, NX_L, 4, NZ), F32),
            VMEM((NY_L, NZ), F32),
            VMEM((NY_L, NZ), F32),
            VMEM((NX_L, NZ), F32),
            VMEM((NX_L, NZ), F32),
            VMEM((NX_L, NZ), F32),
            VMEM((NX_L, NZ), F32),
            VMEM((OWNERS, 3, CAP, BLOCK), F32),
            VMEM((OWNERS, CAP, BLOCK), F32),
            VMEM((OWNERS, CAP, BLOCK), F32),
            VMEM((OWNERS, CAP, BLOCK), F32),
            VMEM((OWNERS, CAP, 384), F32),
            VMEM((OWNERS, CAP, 384), F32),
            VMEM((GROUPS, 2, 64, 128), F32),
            VMEM((GROUPS, 2, 32, 128), F32),
            VMEM((GROUPS, 2, 256, 256), BF16),
            VMEM((BRICKS, OWNERS * CAP), BF16),
            VMEM((OWNERS * CAP, 384), BF16),
            VMEM((OWNERS * CAP, 384), BF16),
            VMEM((3, BRICKS, 128), F32),
            VMEM((3, 2, 512, 128), F32),
            dma((9,)),
            dma((OWNERS,)),
            dma((OWNERS,)),
            dma((OWNERS,)),
            dma((OWNERS,)),
            dma((SWEEPS, 4)),
            dma((SWEEPS, 4)),
            dma((4,)),
            dma((4,)),
            dma((OWNERS,)),
            dma((OWNERS,)),
            dma((OWNERS,)),
        ],
        compiler_params=pltpu.CompilerParams(
            collective_id=0, has_side_effects=True, vmem_limit_bytes=56 << 20
        ),
        name="step",
    )(
        block_counts, block_brick, velocity, pressure, cell_visc, cell_dens,
        positions, start_visc, marker_dens,
    )


def solution(mesh):
    in_specs = (
        P(None, "grid", "mark", None),
        P("grid", "mark", None),
        P("grid", "mark", None),
        P("grid", "mark", None),
        P(("grid", "mark"), None),
        P(("grid", "mark"), None),
        P(("grid", "mark"), None, None, None),
        P(("grid", "mark"), None, None),
        P(("grid", "mark"), None, None),
    )
    out_specs = (
        P(None, "grid", "mark", None),
        P("grid", "mark", None),
        P("grid", "mark", None),
        P("grid", "mark", None),
        P(("grid", "mark"), None, None),
    )
    return jax.shard_map(
        per_device, mesh=mesh, in_specs=in_specs, out_specs=out_specs, check_vma=False
    )
```

```python
import functools
import math
import jax
import jax.numpy as jnp
from jax import lax
from jax.sharding import PartitionSpec as P
from jax.experimental import pallas as pl
from jax.experimental.pallas import tpu as pltpu

F32, BF16 = jnp.float32, jnp.bfloat16
VMEM = pltpu.VMEM
CAP, BLOCK, OWNERS = 48, 256, 16
NT = (((1,), (1,)), ((), ()))
GROUPS = 6


def split(x):
    hi = x.astype(BF16)
    return hi, (x - hi.astype(F32)).astype(BF16)


def axis_weights(fraction, cells):
    half = 0.5 * cells
    factor = jnp.exp(2.0 * cells * fraction - 2.0 * half)
    centres = [i + 0.5 - half for i in range(cells)]
    powers = [None, factor]
    for i in range(2, cells):
        powers.append(powers[i // 2] * powers[i - i // 2])
    raw = [jnp.full_like(factor, math.exp(-centres[0] ** 2))]
    raw += [math.exp(-(centres[i] ** 2)) * powers[i] for i in range(1, cells)]
    total = functools.reduce(jnp.add, raw)
    scale = 1.0 / total
    weights = [r * scale for r in raw]
    mean = functools.reduce(jnp.add, [c * w for c, w in zip(centres, weights)])
    return weights, mean


def masks():
    sub = lax.broadcasted_iota(jnp.int32, (8, 128), 0)
    lane = lax.broadcasted_iota(jnp.int32, (8, 128), 1)
    sub2 = lax.broadcasted_iota(jnp.int32, (8, 256), 0)
    return sub, lane, sub2, sub < 4, sub2 < 4


def both(x, low):
    turned = pltpu.roll(x, 4, 0)
    return jnp.where(low, x, turned), jnp.where(low, turned, x)


def fold(a, b, low):
    return jnp.where(low, a, b) + pltpu.roll(jnp.where(low, b, a), 4, 0)


def skew(x, sub, sign):
    out = x
    for s in range(1, 4):
        out = jnp.where(sub % 4 == s, pltpu.roll(x, (sign * 32 * s) % 128, 1), out)
    return out


def pieces(tiles):
    his, los = [], []
    for n in range(0, len(tiles), 2):
        hi, lo = split(jnp.concatenate(tiles[n : n + 2], axis=0))
        his.append(hi)
        los.append(lo)
    return jnp.concatenate(his + los, axis=0)


def prepare(q, k, row, u, pos, bricks, wz_s, wy_s, planes):
    rows = pl.ds(row, 8)
    sub, lane, sub2, low, low2 = masks()
    wx, mean_x = axis_weights(pos[q, 0, rows, :], 4)
    wy, mean_y = axis_weights(pos[q, 1, rows, :], 4)
    wz, mean_z = axis_weights(pos[q, 2, rows, :], 8)
    for h in range(2):
        part = slice(128 * h, 128 * h + 128)
        for n in range(8):
            wz_s[u, h, pl.ds(8 * n, 8), :] = wz[n][:, part]
        for j in range(4):
            wy_s[u, h, pl.ds(8 * j, 8), :] = wy[j][:, part]
    for b in range(8):
        for h in range(2):
            col = wz_s[u, h, pl.ds(b, 8, stride=8), :]
            for jp in range(2):
                pair = [
                    col * jnp.broadcast_to(wy_s[u, h, pl.ds(8 * j + b, 1), :], (8, 128))
                    for j in (2 * jp, 2 * jp + 1)
                ]
                hi, lo = split(jnp.concatenate(pair, axis=0))
                at = 32 * (b % 4) + 16 * jp
                planes[u, b // 4, pl.ds(at, 16), pl.ds(128 * h, 128)] = hi
                planes[u, b // 4, pl.ds(128 + at, 16), pl.ds(128 * h, 128)] = lo

    diag = (lane // 32) == (sub % 4)
    turned_i = (lane // 32 + 4 - sub % 4) % 4
    c_i = turned_i.astype(F32) - 1.5
    c_j = ((lane // 8) % 4).astype(F32) - 1.5
    c_k = (lane % 8).astype(F32) - 3.5
    v = [both(skew(bricks[k, rows, pl.ds(128 * c, 128)], sub, 1), low) for c in range(3)]
    lefts = []
    for side in range(2):
        vx, vy, vz = [x[side] for x in v]
        kinds = [
            vx, vy, vz, c_j * vy, c_k * vz,
            c_j * vx + c_i * vy, c_k * vx + c_i * vz, c_k * vy + c_j * vz,
        ]
        tiles = []
        for kind in kinds:
            turned = [kind] + [pltpu.roll(kind, 128 - 32 * i, 1) for i in range(1, 4)]
            for ip in range(2):
                tile = jnp.where(low, turned[2 * ip], turned[2 * ip + 1])
                tiles.append(jnp.where(diag, tile, 0.0))
        lefts.append(pieces(tiles))
    pairs = ([], [])
    for ip in range(2):
        first, second = both(wx[2 * ip], low2), both(wx[2 * ip + 1], low2)
        for side in range(2):
            pairs[side].append(jnp.where(low2, first[side], second[side]))
    return lefts, pairs, (mean_x, mean_y, mean_z)


def strain(q, k, row, u, prepared, visc, dens, marker_out, count, planes):
    rows = pl.ds(row, 8)
    sub, lane, sub2, low, low2 = masks()
    lefts, pairs, (mean_x, mean_y, mean_z) = prepared
    results = []
    for side in range(2):
        left = jnp.concatenate([lefts[side], lefts[side]], axis=1)
        out = jnp.dot(left, planes[u, side], preferred_element_type=F32)
        results.append(out[:128] + out[128:])
    centred = [
        [pairs[side][ip] * jnp.where(low2, 2 * ip - 1.5, 2 * ip - 0.5) for ip in range(2)]
        for side in range(2)
    ]

    def along_x(kind, weights):
        at = 16 * kind
        sums = [
            results[side][at : at + 8] * weights[side][0]
            + results[side][at + 8 : at + 16] * weights[side][1]
            for side in range(2)
        ]
        return fold(*sums, low2)

    vx, vy, vz, yy, zz, xy, xz, yz = [along_x(n, pairs) for n in range(8)]
    xx = along_x(0, centred) - mean_x * vx
    yy = yy - mean_y * vy
    zz = zz - mean_z * vz
    xy = xy - mean_y * vx - mean_x * vy
    xz = xz - mean_z * vx - mean_x * vz
    yz = yz - mean_z * vy - mean_y * vz
    invariant = 2.0 * (xx * xx + yy * yy + zz * zz) + xy * xy + xz * xz + yz * yz
    shift = jnp.log(1.0 + invariant * 4.0) * (1.0 / 3.0)
    start = visc[q, rows, :]
    live = (sub2 + row) < count
    weakened = start * jnp.exp(-shift)
    marker_out[k, rows, :] = jnp.where(live, weakened, 0.0)
    carried = [
        jnp.where(live, 1.0, 0.0),
        jnp.where(live, jnp.log(weakened), 0.0),
        jnp.where(live, dens[q, rows, :], 0.0),
    ]
    carried = [both(c, low2) for c in carried]
    return [
        pieces([carried[m][side] * pairs[side][ip] for m in range(3) for ip in range(2)])
        for side in range(2)
    ]


def deposit(k, row, u, lefts, moments, planes):
    rows = pl.ds(row, 8)
    sub, lane, sub2, low, low2 = masks()
    diag = (lane // 32) == (sub % 4)
    sums = []
    for side in range(2):
        out = lax.dot_general(lefts[side], planes[u, side], NT, preferred_element_type=F32)
        sums.append(out[:48, :128] + out[:48, 128:] + out[48:, :128])
    for m in range(3):
        halves = []
        for side in range(2):
            p = [jnp.where(diag, sums[side][16 * m + 8 * ip : 16 * m + 8 * ip + 8], 0.0) for ip in range(2)]
            halves.append(
                jnp.where(low, p[0], pltpu.roll(p[0], 32, 1))
                + jnp.where(low, pltpu.roll(p[1], 64, 1), pltpu.roll(p[1], 96, 1))
            )
        moments[k, rows, pl.ds(128 * m, 128)] = skew(fold(*halves, low), sub, -1)


NX_L, NY_L, NZ = 32, 16, 256
BRICKS = 1024
MESH = pl.DeviceIdType.MESH
SWEEPS = 4
relax_weight = 0.6
pressure_rate = 0.25
gravity = 1.0


def group_transpose(tiles, group):
    tiles = list(tiles)
    for d in (8, 4, 2, 1):
        upper = (group & d) != 0
        for t in range(16):
            if t & d == 0:
                a, b = tiles[t], tiles[t + d]
                tiles[t] = jnp.where(upper, pltpu.roll(b, 8 * d, 1), a)
                tiles[t + d] = jnp.where(upper, b, pltpu.roll(a, 128 - 8 * d, 1))
    return tiles


PAIRS = (
    (0, 0), (0, 1), (1, 0), (0, 3), (3, 0), (1, 1), (3, 3), (1, 3),
    (3, 1), (0, 2), (2, 0), (2, 1), (1, 2), (2, 3), (3, 2), (2, 2),
)
LEAD = 7


def peers():
    g, me = lax.axis_index("grid"), lax.axis_index("mark")
    z, y = me // 4, lax.rem(me, 4)

    def chosen(k, values):
        if isinstance(k, int):
            return values[k]
        out = values[0]
        for n in range(1, OWNERS):
            out = jnp.where(k == n, values[n], out)
        return out

    def after(k):
        dz = chosen(k, [p[0] for p in PAIRS])
        dy = chosen(k, [p[1] for p in PAIRS])
        return lax.rem(z + dz, 4) * 4 + lax.rem(y + dy, 4)

    def before(k):
        dz = chosen(k, [4 - p[0] for p in PAIRS])
        dy = chosen(k, [4 - p[1] for p in PAIRS])
        return lax.rem(z + dz, 4) * 4 + lax.rem(y + dy, 4)

    return g, me, after, before


def remote(src, dst, send, recv, device):
    return pltpu.make_async_remote_copy(
        src_ref=src, dst_ref=dst, send_sem=send, recv_sem=recv, device_id=device, device_id_type=MESH
    )


def step_kernel(
    counts, brick_ids, velocity, pressure, visc, dens, positions, start_visc, marker_dens,
    velocity_out, pressure_out, marker_out, arrived, ids_out,
    state_a, state_b, visc_s, dens_s, halves, planes_hi, planes_lo, one_hot, ids_send, ids_recv,
    brick_send, bricks, kx, kym, kyp, kzm, kzp, damp, x_lo, x_hi, face_lo, face_hi, y_lo, y_hi,
    vx_lo, vx_hi, vface_lo, vface_hi, vy_lo, vy_hi, pos, mvisc, mdens, marker_s, moments, wz_s, wy_s, planes,
    load_sem, id_send, id_recv, b_send, b_recv, h_send, h_recv, v_send, v_recv, m_send, m_recv, out_sem,
):
    g, me, after, before = peers()
    ahead, behind = lax.rem(g + 1, 8), lax.rem(g + 7, 8)
    north, south = lax.rem(me + 1, OWNERS), lax.rem(me + OWNERS - 1, OWNERS)
    loads = [
        pltpu.make_async_copy(velocity, state_a.at[pl.ds(0, 3), pl.ds(1, NX_L)], load_sem.at[0]),
        pltpu.make_async_copy(pressure, state_a.at[3, pl.ds(1, NX_L)], load_sem.at[1]),
        pltpu.make_async_copy(visc, visc_s.at[pl.ds(1, NX_L)], load_sem.at[2]),
        pltpu.make_async_copy(dens, dens_s, load_sem.at[3]),
    ]
    marker_loads = [
        pltpu.make_async_copy(positions, pos, load_sem.at[4]),
        pltpu.make_async_copy(start_visc, mvisc, load_sem.at[7]),
        pltpu.make_async_copy(marker_dens, mdens, load_sem.at[8]),
    ]
    for c in loads + marker_loads:
        c.start()
    barrier = pltpu.get_barrier_semaphore()
    for k in range(1, OWNERS):
        pl.semaphore_signal(barrier, inc=1, device_id=(g, after(k)), device_id_type=MESH)
    pl.semaphore_signal(barrier, inc=1, device_id=(ahead, me), device_id_type=MESH)
    pl.semaphore_signal(barrier, inc=1, device_id=(behind, me), device_id_type=MESH)

    number = brick_ids[...]
    number = (((number >> 5) & 3) * 32 + (number & 31)) * 8 + (number >> 7)
    number = number.astype(F32)
    ids_send[...] = jnp.full((OWNERS, 8, 128), -1.0, F32)
    for q in range(OWNERS):
        ids_send[q, :, pl.ds(0, CAP)] = jnp.broadcast_to(number[q : q + 1], (8, CAP))

    ids_recv[0] = ids_send[me]
    for c in loads:
        c.wait()

    def first_faces(x, _):
        face_lo[0, x] = jnp.concatenate([state_a[c, x + 1, 0:1, :] for c in range(4)], axis=0)
        face_hi[0, x] = jnp.concatenate([state_a[c, x + 1, 15:16, :] for c in range(4)], axis=0)
        return 0

    lax.fori_loop(0, NX_L, first_faces, 0, unroll=4)
    for x in range(NX_L):
        vface_lo[x : x + 1, :] = visc_s[x + 1, 0:1, :]
        vface_hi[x : x + 1, :] = visc_s[x + 1, 15:16, :]
    pl.semaphore_wait(barrier, OWNERS + 1)

    def send_ids(k, _):
        remote(ids_send.at[after(k)], ids_recv.at[k], id_send.at[k], id_recv.at[k], (g, after(k))).start()
        return 0

    lax.fori_loop(1, OWNERS, send_ids, 0)
    def halo(n, state):
        return [
            remote(state.at[:, 1], x_hi.at[n], h_send.at[n, 0], h_recv.at[n, 0], (behind, me)),
            remote(state.at[:, NX_L], x_lo.at[n], h_send.at[n, 1], h_recv.at[n, 1], (ahead, me)),
            remote(face_lo.at[n], y_hi.at[n], h_send.at[n, 2], h_recv.at[n, 2], (g, south)),
            remote(face_hi.at[n], y_lo.at[n], h_send.at[n, 3], h_recv.at[n, 3], (g, north)),
        ]

    visc_halo = [
        remote(visc_s.at[1], vx_hi, v_send.at[0], v_recv.at[0], (behind, me)),
        remote(visc_s.at[NX_L], vx_lo, v_send.at[1], v_recv.at[1], (ahead, me)),
        remote(vface_lo, vy_hi, v_send.at[2], v_recv.at[2], (g, south)),
        remote(vface_hi, vy_lo, v_send.at[3], v_recv.at[3], (g, north)),
    ]
    for c in halo(0, state_a) + visc_halo:
        c.start()

    def to_halves(x, _):
        for c in range(3):
            plane = state_a[c, x + 1]
            at = pl.multiple_of(c * 512 + x * 16, 16)
            for h in range(2):
                halves[h, pl.ds(at, 16), :] = plane[:, 128 * h : 128 * h + 128]
        return 0

    lax.fori_loop(0, NX_L, to_halves, 0, unroll=2)
    group = lax.broadcasted_iota(jnp.int32, (8, 128), 1) // 8

    def to_bricks(n, _):
        bj, h = n // 2, lax.rem(n, 2)
        for c in range(3):
            tiles = [
                halves[h, pl.ds(c * 512 + 16 * i + 4 * bj + j, 8, stride=64), :]
                for i in range(4)
                for j in range(4)
            ]
            tiles = group_transpose(tiles, group)
            for t in range(0, 16, 2):
                hi, lo = split(jnp.concatenate(tiles[t : t + 2], axis=0))
                at = pl.multiple_of((bj * 32 + h * 16 + t) * 8, 16)
                planes_hi[pl.ds(at, 16), pl.ds(128 * c, 128)] = hi
                planes_lo[pl.ds(at, 16), pl.ds(128 * c, 128)] = lo
        return 0

    lax.fori_loop(0, 8, to_bricks, 0)

    def brick_copy(k):
        return remote(
            brick_send.at[k], bricks.at[k], b_send.at[k], b_recv.at[k], (g, before(k))
        )

    lanes = lax.broadcasted_iota(jnp.int32, (CAP, 128), 1).astype(F32)

    def hits_of(k, m):
        column = jnp.transpose(jnp.broadcast_to(ids_recv[k][0:1, :], (128, 128)))[:CAP]
        for t in range(8):
            hit = jnp.where(column == lanes + 128.0 * t, 1.0, 0.0).astype(BF16)
            one_hot[pl.ds(CAP * m, CAP), pl.ds(128 * t, 128)] = hit

    def gather(n, _):
        for m in range(4):
            hits_of(4 * n + m, m)
        found = jnp.dot(one_hot[...], planes_hi[...], preferred_element_type=F32)
        found = found + jnp.dot(one_hot[...], planes_lo[...], preferred_element_type=F32)
        for m in range(4):
            brick_send[4 * n + m] = found[CAP * m : CAP * m + CAP]
        for m in range(4):
            k = 4 * n + m

            @pl.when((k > 0) & (k <= LEAD))
            def _():
                brick_copy(k).start()

        return 0

    hits_of(0, 0)
    own = one_hot[pl.ds(0, CAP), :]
    bricks[0] = jnp.dot(own, planes_hi[...], preferred_element_type=F32) + jnp.dot(
        own, planes_lo[...], preferred_element_type=F32
    )
    for c in marker_loads:
        c.wait()

    def moment_copy(k):
        return remote(moments.at[k], arrived.at[k], m_send.at[k], m_recv.at[k], (g, after(k)))

    def marker_store(k):
        return pltpu.make_async_copy(marker_s.at[k], marker_out.at[after(k)], out_sem.at[k])

    def owner_markers(k, _):
        q = after(k)
        count = counts[0, q]

        @pl.when((k > 0) & (k + LEAD < OWNERS))
        def _():
            brick_copy(k + LEAD).start()

        @pl.when(k > 0)
        def _():
            brick_copy(k).wait()

        ready, spread = {}, {}
        for t in range(GROUPS + 2):
            if t < GROUPS:
                ready[t] = prepare(q, k, 8 * t, t, pos, bricks, wz_s, wy_s, planes)
            u = t - 1
            if 0 <= u < GROUPS:
                spread[u] = strain(q, k, 8 * u, u, ready.pop(u), mvisc, mdens, marker_s, count, planes)
            u = t - 2
            if 0 <= u < GROUPS:
                deposit(k, 8 * u, u, spread.pop(u), moments, planes)
        marker_store(k).start()

        @pl.when(k > 0)
        def _():
            moment_copy(k).start()

        return 0

    lax.fori_loop(0, 1, owner_markers, 0)
    def wait_ids(k, _):
        remote(ids_send.at[after(k)], ids_recv.at[k], id_send.at[k], id_recv.at[k], (g, after(k))).wait()
        return 0

    lax.fori_loop(1, OWNERS, wait_ids, 0)

    lax.fori_loop(0, 4, gather, 0)

    x_lo_on = (g > 0).astype(F32)
    x_hi_on = (g < 7).astype(F32)
    y_lo_on = (me > 0).astype(F32)
    y_hi_on = (me < OWNERS - 1).astype(F32)
    row = lax.broadcasted_iota(jnp.int32, (NY_L, NZ), 0)
    col = lax.broadcasted_iota(jnp.int32, (NY_L, NZ), 1)
    first_y, last_y = row == 0, row == NY_L - 1
    first_z, last_z = col == 0, col == NZ - 1

    def y_minus(plane, edge):
        return jnp.where(first_y, jnp.broadcast_to(edge, plane.shape), pltpu.roll(plane, 1, 0))

    def y_plus(plane, edge):
        return jnp.where(last_y, jnp.broadcast_to(edge, plane.shape), pltpu.roll(plane, NY_L - 1, 0))

    def z_minus(plane):
        return jnp.where(first_z, 0.0, pltpu.roll(plane, 1, 1))

    def z_plus(plane):
        return jnp.where(last_z, 0.0, pltpu.roll(plane, NZ - 1, 1))

    for c in visc_halo:
        c.wait()
    visc_s[0] = vx_lo[...] * x_lo_on
    visc_s[NX_L + 1] = vx_hi[...] * x_hi_on

    def couplings(x, _):
        here, below, above = visc_s[x + 1], visc_s[x], visc_s[x + 2]
        k_xm, k_xp = 0.5 * (here + below), 0.5 * (here + above)
        k_ym = 0.5 * (here + y_minus(here, vy_lo[pl.ds(x, 1), :] * y_lo_on))
        k_yp = 0.5 * (here + y_plus(here, vy_hi[pl.ds(x, 1), :] * y_hi_on))
        k_zm, k_zp = 0.5 * (here + z_minus(here)), 0.5 * (here + z_plus(here))
        kx[x] = k_xm
        kx[x + 1] = k_xp
        kym[x] = k_ym
        kyp[x] = k_yp
        kzm[x] = k_zm
        kzp[x] = k_zp
        damp[x] = relax_weight / (k_xm + k_xp + k_ym + k_yp + k_zm + k_zp)
        return 0

    lax.fori_loop(0, NX_L, couplings, 0, unroll=2)

    for n in range(SWEEPS):
        old, new = (state_a, state_b) if n % 2 == 0 else (state_b, state_a)
        for c in halo(n, old):
            c.wait()
        old[:, 0] = x_lo[n] * x_lo_on
        old[:, NX_L + 1] = x_hi[n] * x_hi_on

        def sweep(x, _, n=n, old=old, new=new):
            low = y_lo[n, x] * y_lo_on
            high = y_hi[n, x] * y_hi_on
            press = old[3, x + 1]
            press_near = [
                old[3, x],
                y_minus(press, low[3:4]),
                z_minus(press),
            ]
            weights = [kx[x + 1], kx[x], kyp[x], kym[x], kzp[x], kzm[x]]
            scale = damp[x]
            divergence = jnp.zeros_like(press)
            fresh = []
            for c in range(3):
                v = old[c, x + 1]
                near = [
                    old[c, x + 2],
                    old[c, x],
                    y_plus(v, high[c : c + 1]),
                    y_minus(v, low[c : c + 1]),
                    z_plus(v),
                    z_minus(v),
                ]
                forcing = press_near[c] - press
                for w, s in zip(weights, near):
                    forcing = forcing + w * (s - v)
                if c == 2:
                    forcing = forcing - gravity * dens_s[x]
                fresh.append(v + scale * forcing)
                divergence = divergence + (near[2 * c] - v)
            fresh.append(press - pressure_rate * visc_s[x + 1] * divergence)
            for c in range(4):
                new[c, x + 1] = fresh[c]
            if n + 1 < SWEEPS:
                face_lo[n + 1, x] = jnp.concatenate([f[0:1] for f in fresh], axis=0)
                face_hi[n + 1, x] = jnp.concatenate([f[15:16] for f in fresh], axis=0)
            return 0

        lax.fori_loop(0, NX_L, sweep, 0, unroll=2)
        if n + 1 < SWEEPS:
            for c in halo(n + 1, new):
                c.start()
        if n + 1 < SWEEPS:
            lax.fori_loop(1 + 5 * n, 6 + 5 * n, owner_markers, 0)
    last = state_a if SWEEPS % 2 == 0 else state_b
    stores = [
        pltpu.make_async_copy(last.at[pl.ds(0, 3), pl.ds(1, NX_L)], velocity_out, load_sem.at[5]),
        pltpu.make_async_copy(last.at[3, pl.ds(1, NX_L)], pressure_out, load_sem.at[6]),
    ]
    for c in stores:
        c.start()
    own = pltpu.make_async_copy(moments.at[0], arrived.at[0], load_sem.at[9])
    own.start()
    ids_out[...] = ids_recv[...]

    def arrive(k, _):
        moment_copy(k).wait()
        return 0

    lax.fori_loop(1, OWNERS, arrive, 0)

    def wait_markers(k, _):
        marker_store(k).wait()
        return 0

    lax.fori_loop(0, OWNERS, wait_markers, 0)
    own.wait()
    for c in stores:
        c.wait()


def home_kernel(
    moments, ids, visc, dens, velocity, pressure, markers,
    visc_out, dens_out, velocity_out, pressure_out, markers_out,
    arrived, visc_s, dens_s, velocity_s, pressure_s, markers_s, hits, hi_s, lo_s, sums, cells, sem,
):
    loads = [
        pltpu.make_async_copy(moments, arrived, sem.at[0]),
        pltpu.make_async_copy(visc, visc_s, sem.at[1]),
        pltpu.make_async_copy(dens, dens_s, sem.at[2]),
    ]
    stages = ((velocity, velocity_s, velocity_out), (pressure, pressure_s, pressure_out), (markers, markers_s, markers_out))
    fetches = [pltpu.make_async_copy(a, b, sem.at[3 + n]) for n, (a, b, c) in enumerate(stages)]
    copies = [pltpu.make_async_copy(b, c, sem.at[6 + n]) for n, (a, b, c) in enumerate(stages)]
    for c in loads + fetches:
        c.start()
    lane = lax.broadcasted_iota(jnp.int32, (8, 128), 1)
    rows = [jnp.full((8, 128), -1.0, F32) for _ in range(6)]
    for k in range(OWNERS):
        at = CAP * k
        t, off = at // 128, at % 128
        tile = ids[k]
        turned = pltpu.roll(tile, off, 1) if off else tile
        rows[t] = jnp.where((lane >= off) & (lane < off + CAP), turned, rows[t])
        over = off + CAP - 128
        if over > 0:
            rows[t + 1] = jnp.where(lane < over, turned, rows[t + 1])

    wide = [jnp.concatenate([r, r], axis=0) for r in rows]
    sub = lax.broadcasted_iota(jnp.int32, (16, 128), 0).astype(F32)

    def mark_hits(r, _):
        at = pl.multiple_of(r * 16, 16)
        here = sub + (r * 16).astype(F32)
        for t in range(6):
            hits[pl.ds(at, 16), pl.ds(128 * t, 128)] = jnp.where(wide[t] == here, 1.0, 0.0).astype(BF16)
        return 0

    lax.fori_loop(0, BRICKS // 16, mark_hits, 0, unroll=4)

    for c in loads:
        c.wait()

    def moment_pieces(k, _):
        hi, lo = split(arrived[k])
        at = pl.multiple_of(k * CAP, 16)
        hi_s[pl.ds(at, CAP), :] = hi
        lo_s[pl.ds(at, CAP), :] = lo
        return 0

    lax.fori_loop(0, OWNERS, moment_pieces, 0)

    def scatter(n, _):
        at = pl.ds(pl.multiple_of(n * 256, 256), 256)
        block = hits[at, :]
        total = jnp.dot(block, hi_s[...], preferred_element_type=F32)
        total = total + jnp.dot(block, lo_s[...], preferred_element_type=F32)
        for m in range(3):
            sums[m, at, :] = total[:, 128 * m : 128 * m + 128]
        return 0

    for fetch, c in zip(fetches, copies):
        fetch.wait()
        c.start()
    lax.fori_loop(0, 4, scatter, 0)
    group = lane // 8

    def to_cells(n, _):
        bj, h = n // 2, lax.rem(n, 2)
        for m in range(3):
            tiles = [
                sums[m, pl.ds(pl.multiple_of((bj * 32 + h * 16 + t) * 8, 8), 8), :] for t in range(16)
            ]
            tiles = group_transpose(tiles, group)
            for i in range(4):
                for j in range(4):
                    cells[m, h, pl.ds(16 * i + 4 * bj + j, 8, stride=64), :] = tiles[4 * i + j]
        return 0

    lax.fori_loop(0, 8, to_cells, 0)

    def finish(x, _):
        at = pl.ds(pl.multiple_of(x * 16, 16), 16)
        for h in range(2):
            part = pl.ds(128 * h, 128)
            below = 1.0 / (cells[0, h, at, :] + 1.0)
            visc_out[x, :, part] = jnp.exp((cells[1, h, at, :] + jnp.log(visc_s[x, :, part])) * below)
            dens_out[x, :, part] = (cells[2, h, at, :] + dens_s[x, :, part]) * below
        return 0

    lax.fori_loop(0, NX_L, finish, 0, unroll=2)
    for c in copies:
        c.wait()


def per_device(
    velocity, pressure, cell_visc, cell_dens, block_brick, block_counts, positions, start_visc, marker_dens
):
    vm = pl.BlockSpec(memory_space=pltpu.VMEM)
    hbm = pl.BlockSpec(memory_space=pl.ANY)
    dma = pltpu.SemaphoreType.DMA
    field = (NX_L, NY_L, NZ)
    padded = (NX_L + 2, NY_L, NZ)
    shape = jax.ShapeDtypeStruct
    velocity_next, pressure_next, markers, moments, ids = pl.pallas_call(
        step_kernel,
        out_shape=(
            shape((3,) + field, F32),
            shape(field, F32),
            shape((OWNERS, CAP, BLOCK), F32),
            shape((OWNERS, CAP, 384), F32),
            shape((OWNERS, 8, 128), F32),
        ),
        in_specs=[pl.BlockSpec(memory_space=pltpu.SMEM), vm] + [hbm] * 7,
        out_specs=(hbm, hbm, hbm, hbm, vm),
        scratch_shapes=[
            VMEM((4,) + padded, F32),
            VMEM((4,) + padded, F32),
            VMEM(padded, F32),
            VMEM(field, F32),
            VMEM((2, 1536, 128), F32),
            VMEM((BRICKS, 384), BF16),
            VMEM((BRICKS, 384), BF16),
            VMEM((4 * CAP, BRICKS), BF16),
            VMEM((OWNERS, 8, 128), F32),
            VMEM((OWNERS, 8, 128), F32),
            VMEM((OWNERS, CAP, 384), F32),
            VMEM((OWNERS, CAP, 384), F32),
            VMEM((NX_L + 1, NY_L, NZ), F32),
            VMEM(field, F32),
            VMEM(field, F32),
            VMEM(field, F32),
            VMEM(field, F32),
            VMEM(field, F32),
            VMEM((SWEEPS, 4, NY_L, NZ), F32),
            VMEM((SWEEPS, 4, NY_L, NZ), F32),
            VMEM((SWEEPS, NX_L, 4, NZ), F32),
            VMEM((SWEEPS, NX_L, 4, NZ), F32),
            VMEM((SWEEPS, NX_L, 4, NZ), F32),
            VMEM((SWEEPS, NX_L, 4, NZ), F32),
            VMEM((NY_L, NZ), F32),
            VMEM((NY_L, NZ), F32),
            VMEM((NX_L, NZ), F32),
            VMEM((NX_L, NZ), F32),
            VMEM((NX_L, NZ), F32),
            VMEM((NX_L, NZ), F32),
            VMEM((OWNERS, 3, CAP, BLOCK), F32),
            VMEM((OWNERS, CAP, BLOCK), F32),
            VMEM((OWNERS, CAP, BLOCK), F32),
            VMEM((OWNERS, CAP, BLOCK), F32),
            VMEM((OWNERS, CAP, 384), F32),
            VMEM((GROUPS, 2, 64, 128), F32),
            VMEM((GROUPS, 2, 32, 128), F32),
            VMEM((GROUPS, 2, 256, 256), BF16),
            dma((10,)),
            dma((OWNERS,)),
            dma((OWNERS,)),
            dma((OWNERS,)),
            dma((OWNERS,)),
            dma((SWEEPS, 4)),
            dma((SWEEPS, 4)),
            dma((4,)),
            dma((4,)),
            dma((OWNERS,)),
            dma((OWNERS,)),
            dma((OWNERS,)),
        ],
        compiler_params=pltpu.CompilerParams(
            collective_id=0, has_side_effects=True, vmem_limit_bytes=56 << 20
        ),
        name="step",
    )(
        block_counts, block_brick, velocity, pressure, cell_visc, cell_dens,
        positions, start_visc, marker_dens,
    )
    visc_next, dens_next, velocity_next, pressure_next, markers = pl.pallas_call(
        home_kernel,
        out_shape=(
            shape(field, F32),
            shape(field, F32),
            shape((3,) + field, F32),
            shape(field, F32),
            shape((OWNERS, CAP, BLOCK), F32),
        ),
        in_specs=[hbm, vm] + [hbm] * 5,
        out_specs=(vm, vm, hbm, hbm, hbm),
        scratch_shapes=[
            VMEM((OWNERS, CAP, 384), F32),
            VMEM(field, F32),
            VMEM(field, F32),
            VMEM((3,) + field, F32),
            VMEM(field, F32),
            VMEM((OWNERS, CAP, BLOCK), F32),
            VMEM((BRICKS, OWNERS * CAP), BF16),
            VMEM((OWNERS * CAP, 384), BF16),
            VMEM((OWNERS * CAP, 384), BF16),
            VMEM((3, BRICKS, 128), F32),
            VMEM((3, 2, 512, 128), F32),
            dma((9,)),
        ],
        compiler_params=pltpu.CompilerParams(vmem_limit_bytes=56 << 20),
        name="home",
    )(moments, ids, cell_visc, cell_dens, velocity_next, pressure_next, markers)
    return velocity_next, pressure_next, visc_next, dens_next, markers


def solution(mesh):
    in_specs = (
        P(None, "grid", "mark", None),
        P("grid", "mark", None),
        P("grid", "mark", None),
        P("grid", "mark", None),
        P(("grid", "mark"), None),
        P(("grid", "mark"), None),
        P(("grid", "mark"), None, None, None),
        P(("grid", "mark"), None, None),
        P(("grid", "mark"), None, None),
    )
    out_specs = (
        P(None, "grid", "mark", None),
        P("grid", "mark", None),
        P("grid", "mark", None),
        P("grid", "mark", None),
        P(("grid", "mark"), None, None),
    )
    return jax.shard_map(
        per_device, mesh=mesh, in_specs=in_specs, out_specs=out_specs, check_vma=False
    )
```

```python
import functools
import math
import jax
import jax.numpy as jnp
from jax import lax
from jax.sharding import PartitionSpec as P
from jax.experimental import pallas as pl
from jax.experimental.pallas import tpu as pltpu

F32, BF16 = jnp.float32, jnp.bfloat16
VMEM = pltpu.VMEM
CAP, BLOCK, OWNERS = 48, 256, 16
NT = (((1,), (1,)), ((), ()))
GROUPS = 6


def split(x):
    hi = x.astype(BF16)
    return hi, (x - hi.astype(F32)).astype(BF16)


def axis_weights(fraction, cells):
    half = 0.5 * cells
    factor = jnp.exp(2.0 * cells * fraction - 2.0 * half)
    centres = [i + 0.5 - half for i in range(cells)]
    powers = [None, factor]
    for i in range(2, cells):
        powers.append(powers[i // 2] * powers[i - i // 2])
    raw = [jnp.full_like(factor, math.exp(-centres[0] ** 2))]
    raw += [math.exp(-(centres[i] ** 2)) * powers[i] for i in range(1, cells)]
    total = functools.reduce(jnp.add, raw)
    scale = 1.0 / total
    weights = [r * scale for r in raw]
    mean = functools.reduce(jnp.add, [c * w for c, w in zip(centres, weights)])
    return weights, mean


def masks():
    sub = lax.broadcasted_iota(jnp.int32, (8, 128), 0)
    lane = lax.broadcasted_iota(jnp.int32, (8, 128), 1)
    sub2 = lax.broadcasted_iota(jnp.int32, (8, 256), 0)
    return sub, lane, sub2, sub < 4, sub2 < 4


def both(x, low):
    turned = pltpu.roll(x, 4, 0)
    return jnp.where(low, x, turned), jnp.where(low, turned, x)


def fold(a, b, low):
    return jnp.where(low, a, b) + pltpu.roll(jnp.where(low, b, a), 4, 0)


def skew(x, sub, sign):
    out = x
    for s in range(1, 4):
        out = jnp.where(sub % 4 == s, pltpu.roll(x, (sign * 32 * s) % 128, 1), out)
    return out


def pieces(tiles):
    his, los = [], []
    for n in range(0, len(tiles), 2):
        hi, lo = split(jnp.concatenate(tiles[n : n + 2], axis=0))
        his.append(hi)
        los.append(lo)
    return jnp.concatenate(his + los, axis=0)


def prepare(q, k, row, u, pos, bricks, wz_s, wy_s, planes):
    rows = pl.ds(row, 8)
    sub, lane, sub2, low, low2 = masks()
    wx, mean_x = axis_weights(pos[q, 0, rows, :], 4)
    wy, mean_y = axis_weights(pos[q, 1, rows, :], 4)
    wz, mean_z = axis_weights(pos[q, 2, rows, :], 8)
    for h in range(2):
        part = slice(128 * h, 128 * h + 128)
        for n in range(8):
            wz_s[u, h, pl.ds(8 * n, 8), :] = wz[n][:, part]
        for j in range(4):
            wy_s[u, h, pl.ds(8 * j, 8), :] = wy[j][:, part]
    for b in range(8):
        for h in range(2):
            col = wz_s[u, h, pl.ds(b, 8, stride=8), :]
            for jp in range(2):
                pair = [
                    col * jnp.broadcast_to(wy_s[u, h, pl.ds(8 * j + b, 1), :], (8, 128))
                    for j in (2 * jp, 2 * jp + 1)
                ]
                hi, lo = split(jnp.concatenate(pair, axis=0))
                at = 32 * (b % 4) + 16 * jp
                planes[u, b // 4, pl.ds(at, 16), pl.ds(128 * h, 128)] = hi
                planes[u, b // 4, pl.ds(128 + at, 16), pl.ds(128 * h, 128)] = lo

    diag = (lane // 32) == (sub % 4)
    turned_i = (lane // 32 + 4 - sub % 4) % 4
    c_i = turned_i.astype(F32) - 1.5
    c_j = ((lane // 8) % 4).astype(F32) - 1.5
    c_k = (lane % 8).astype(F32) - 3.5
    v = [both(skew(bricks[k, rows, pl.ds(128 * c, 128)], sub, 1), low) for c in range(3)]
    lefts = []
    for side in range(2):
        vx, vy, vz = [x[side] for x in v]
        kinds = [
            vx, vy, vz, c_j * vy, c_k * vz,
            c_j * vx + c_i * vy, c_k * vx + c_i * vz, c_k * vy + c_j * vz,
        ]
        tiles = []
        for kind in kinds:
            turned = [kind] + [pltpu.roll(kind, 128 - 32 * i, 1) for i in range(1, 4)]
            for ip in range(2):
                tile = jnp.where(low, turned[2 * ip], turned[2 * ip + 1])
                tiles.append(jnp.where(diag, tile, 0.0))
        lefts.append(pieces(tiles))
    pairs = ([], [])
    for ip in range(2):
        first, second = both(wx[2 * ip], low2), both(wx[2 * ip + 1], low2)
        for side in range(2):
            pairs[side].append(jnp.where(low2, first[side], second[side]))
    return lefts, pairs, (mean_x, mean_y, mean_z)


def strain(q, k, row, u, prepared, visc, dens, marker_out, count, planes):
    rows = pl.ds(row, 8)
    sub, lane, sub2, low, low2 = masks()
    lefts, pairs, (mean_x, mean_y, mean_z) = prepared
    results = []
    for side in range(2):
        left = jnp.concatenate([lefts[side], lefts[side]], axis=1)
        out = jnp.dot(left, planes[u, side], preferred_element_type=F32)
        results.append(out[:128] + out[128:])
    centred = [
        [pairs[side][ip] * jnp.where(low2, 2 * ip - 1.5, 2 * ip - 0.5) for ip in range(2)]
        for side in range(2)
    ]

    def along_x(kind, weights):
        at = 16 * kind
        sums = [
            results[side][at : at + 8] * weights[side][0]
            + results[side][at + 8 : at + 16] * weights[side][1]
            for side in range(2)
        ]
        return fold(*sums, low2)

    vx, vy, vz, yy, zz, xy, xz, yz = [along_x(n, pairs) for n in range(8)]
    xx = along_x(0, centred) - mean_x * vx
    yy = yy - mean_y * vy
    zz = zz - mean_z * vz
    xy = xy - mean_y * vx - mean_x * vy
    xz = xz - mean_z * vx - mean_x * vz
    yz = yz - mean_z * vy - mean_y * vz
    invariant = 2.0 * (xx * xx + yy * yy + zz * zz) + xy * xy + xz * xz + yz * yz
    shift = jnp.log(1.0 + invariant * 4.0) * (1.0 / 3.0)
    start = visc[q, rows, :]
    live = (sub2 + row) < count
    weakened = start * jnp.exp(-shift)
    marker_out[k, rows, :] = jnp.where(live, weakened, 0.0)
    carried = [
        jnp.where(live, 1.0, 0.0),
        jnp.where(live, jnp.log(weakened), 0.0),
        jnp.where(live, dens[q, rows, :], 0.0),
    ]
    carried = [both(c, low2) for c in carried]
    return [
        pieces([carried[m][side] * pairs[side][ip] for m in range(3) for ip in range(2)])
        for side in range(2)
    ]


def deposit(k, row, u, lefts, moments, planes):
    rows = pl.ds(row, 8)
    sub, lane, sub2, low, low2 = masks()
    diag = (lane // 32) == (sub % 4)
    sums = []
    for side in range(2):
        out = lax.dot_general(lefts[side], planes[u, side], NT, preferred_element_type=F32)
        sums.append(out[:48, :128] + out[:48, 128:] + out[48:, :128])
    for m in range(3):
        halves = []
        for side in range(2):
            p = [jnp.where(diag, sums[side][16 * m + 8 * ip : 16 * m + 8 * ip + 8], 0.0) for ip in range(2)]
            halves.append(
                jnp.where(low, p[0], pltpu.roll(p[0], 32, 1))
                + jnp.where(low, pltpu.roll(p[1], 64, 1), pltpu.roll(p[1], 96, 1))
            )
        moments[k, rows, pl.ds(128 * m, 128)] = skew(fold(*halves, low), sub, -1)


NX_L, NY_L, NZ = 32, 16, 256
BRICKS = 1024
MESH = pl.DeviceIdType.MESH
SWEEPS = 4
relax_weight = 0.6
pressure_rate = 0.25
gravity = 1.0


def group_transpose(tiles, group):
    tiles = list(tiles)
    for d in (8, 4, 2, 1):
        upper = (group & d) != 0
        for t in range(16):
            if t & d == 0:
                a, b = tiles[t], tiles[t + d]
                tiles[t] = jnp.where(upper, pltpu.roll(b, 8 * d, 1), a)
                tiles[t + d] = jnp.where(upper, b, pltpu.roll(a, 128 - 8 * d, 1))
    return tiles


PAIRS = (
    (0, 0), (0, 1), (1, 0), (0, 3), (3, 0), (1, 1), (3, 3), (1, 3),
    (3, 1), (0, 2), (2, 0), (2, 1), (1, 2), (2, 3), (3, 2), (2, 2),
)
LEAD = 7


def peers():
    g, me = lax.axis_index("grid"), lax.axis_index("mark")
    z, y = me // 4, lax.rem(me, 4)

    def chosen(k, values):
        if isinstance(k, int):
            return values[k]
        out = values[0]
        for n in range(1, OWNERS):
            out = jnp.where(k == n, values[n], out)
        return out

    def after(k):
        dz = chosen(k, [p[0] for p in PAIRS])
        dy = chosen(k, [p[1] for p in PAIRS])
        return lax.rem(z + dz, 4) * 4 + lax.rem(y + dy, 4)

    def before(k):
        dz = chosen(k, [4 - p[0] for p in PAIRS])
        dy = chosen(k, [4 - p[1] for p in PAIRS])
        return lax.rem(z + dz, 4) * 4 + lax.rem(y + dy, 4)

    return g, me, after, before


def remote(src, dst, send, recv, device):
    return pltpu.make_async_remote_copy(
        src_ref=src, dst_ref=dst, send_sem=send, recv_sem=recv, device_id=device, device_id_type=MESH
    )


def step_kernel(
    counts, brick_ids, velocity, pressure, visc, dens, positions, start_visc, marker_dens,
    velocity_out, pressure_out, marker_out, arrived, ids_out,
    state_a, state_b, visc_s, dens_s, halves, planes_hi, planes_lo, one_hot, ids_send, ids_recv,
    brick_send, bricks, kx, kym, kyp, kzm, kzp, damp, x_lo, x_hi, face_lo, face_hi, y_lo, y_hi,
    vx_lo, vx_hi, vface_lo, vface_hi, vy_lo, vy_hi, pos, mvisc, mdens, marker_s, moments, wz_s, wy_s, planes,
    load_sem, id_send, id_recv, b_send, b_recv, h_send, h_recv, v_send, v_recv, m_send, m_recv, out_sem,
):
    g, me, after, before = peers()
    ahead, behind = lax.rem(g + 1, 8), lax.rem(g + 7, 8)
    north, south = lax.rem(me + 1, OWNERS), lax.rem(me + OWNERS - 1, OWNERS)
    loads = [
        pltpu.make_async_copy(velocity, state_a.at[pl.ds(0, 3), pl.ds(1, NX_L)], load_sem.at[0]),
        pltpu.make_async_copy(pressure, state_a.at[3, pl.ds(1, NX_L)], load_sem.at[1]),
        pltpu.make_async_copy(visc, visc_s.at[pl.ds(1, NX_L)], load_sem.at[2]),
        pltpu.make_async_copy(dens, dens_s, load_sem.at[3]),
    ]
    marker_loads = [
        pltpu.make_async_copy(positions, pos, load_sem.at[4]),
        pltpu.make_async_copy(start_visc, mvisc, load_sem.at[7]),
        pltpu.make_async_copy(marker_dens, mdens, load_sem.at[8]),
    ]
    for c in loads + marker_loads:
        c.start()
    barrier = pltpu.get_barrier_semaphore()
    for k in range(1, OWNERS):
        pl.semaphore_signal(barrier, inc=1, device_id=(g, after(k)), device_id_type=MESH)
    pl.semaphore_signal(barrier, inc=1, device_id=(ahead, me), device_id_type=MESH)
    pl.semaphore_signal(barrier, inc=1, device_id=(behind, me), device_id_type=MESH)

    number = brick_ids[...]
    number = (((number >> 5) & 3) * 32 + (number & 31)) * 8 + (number >> 7)
    number = number.astype(F32)
    ids_send[...] = jnp.full((OWNERS, 8, 128), -1.0, F32)
    for q in range(OWNERS):
        ids_send[q, :, pl.ds(0, CAP)] = jnp.broadcast_to(number[q : q + 1], (8, CAP))

    ids_recv[0] = ids_send[me]
    for c in loads:
        c.wait()

    def first_faces(x, _):
        face_lo[0, x] = jnp.concatenate([state_a[c, x + 1, 0:1, :] for c in range(4)], axis=0)
        face_hi[0, x] = jnp.concatenate([state_a[c, x + 1, 15:16, :] for c in range(4)], axis=0)
        return 0

    lax.fori_loop(0, NX_L, first_faces, 0, unroll=4)
    for x in range(NX_L):
        vface_lo[x : x + 1, :] = visc_s[x + 1, 0:1, :]
        vface_hi[x : x + 1, :] = visc_s[x + 1, 15:16, :]
    pl.semaphore_wait(barrier, OWNERS + 1)

    def send_ids(k, _):
        remote(ids_send.at[after(k)], ids_recv.at[k], id_send.at[k], id_recv.at[k], (g, after(k))).start()
        return 0

    lax.fori_loop(1, OWNERS, send_ids, 0)
    def halo(n, state):
        return [
            remote(state.at[:, 1], x_hi.at[n], h_send.at[n, 0], h_recv.at[n, 0], (behind, me)),
            remote(state.at[:, NX_L], x_lo.at[n], h_send.at[n, 1], h_recv.at[n, 1], (ahead, me)),
            remote(face_lo.at[n], y_hi.at[n], h_send.at[n, 2], h_recv.at[n, 2], (g, south)),
            remote(face_hi.at[n], y_lo.at[n], h_send.at[n, 3], h_recv.at[n, 3], (g, north)),
        ]

    visc_halo = [
        remote(visc_s.at[1], vx_hi, v_send.at[0], v_recv.at[0], (behind, me)),
        remote(visc_s.at[NX_L], vx_lo, v_send.at[1], v_recv.at[1], (ahead, me)),
        remote(vface_lo, vy_hi, v_send.at[2], v_recv.at[2], (g, south)),
        remote(vface_hi, vy_lo, v_send.at[3], v_recv.at[3], (g, north)),
    ]
    for c in halo(0, state_a) + visc_halo:
        c.start()

    def to_halves(x, _):
        for c in range(3):
            plane = state_a[c, x + 1]
            at = pl.multiple_of(c * 512 + x * 16, 16)
            for h in range(2):
                halves[h, pl.ds(at, 16), :] = plane[:, 128 * h : 128 * h + 128]
        return 0

    lax.fori_loop(0, NX_L, to_halves, 0, unroll=2)
    group = lax.broadcasted_iota(jnp.int32, (8, 128), 1) // 8

    def to_bricks(n, _):
        bj, h = n // 2, lax.rem(n, 2)
        for c in range(3):
            tiles = [
                halves[h, pl.ds(c * 512 + 16 * i + 4 * bj + j, 8, stride=64), :]
                for i in range(4)
                for j in range(4)
            ]
            tiles = group_transpose(tiles, group)
            for t in range(0, 16, 2):
                hi, lo = split(jnp.concatenate(tiles[t : t + 2], axis=0))
                at = pl.multiple_of((bj * 32 + h * 16 + t) * 8, 16)
                planes_hi[pl.ds(at, 16), pl.ds(128 * c, 128)] = hi
                planes_lo[pl.ds(at, 16), pl.ds(128 * c, 128)] = lo
        return 0

    lax.fori_loop(0, 8, to_bricks, 0)

    def brick_copy(k):
        return remote(
            brick_send.at[k], bricks.at[k], b_send.at[k], b_recv.at[k], (g, before(k))
        )

    lanes = lax.broadcasted_iota(jnp.int32, (CAP, 128), 1).astype(F32)

    def hits_of(k, m):
        column = jnp.transpose(jnp.broadcast_to(ids_recv[k][0:1, :], (128, 128)))[:CAP]
        for t in range(8):
            hit = jnp.where(column == lanes + 128.0 * t, 1.0, 0.0).astype(BF16)
            one_hot[pl.ds(CAP * m, CAP), pl.ds(128 * t, 128)] = hit

    def gather(n, _):
        for m in range(4):
            hits_of(4 * n + m, m)
        found = jnp.dot(one_hot[...], planes_hi[...], preferred_element_type=F32)
        found = found + jnp.dot(one_hot[...], planes_lo[...], preferred_element_type=F32)
        for m in range(4):
            brick_send[4 * n + m] = found[CAP * m : CAP * m + CAP]
        for m in range(4):
            k = 4 * n + m

            @pl.when((k > 0) & (k <= LEAD))
            def _():
                brick_copy(k).start()

        return 0

    hits_of(0, 0)
    own = one_hot[pl.ds(0, CAP), :]
    bricks[0] = jnp.dot(own, planes_hi[...], preferred_element_type=F32) + jnp.dot(
        own, planes_lo[...], preferred_element_type=F32
    )
    for c in marker_loads:
        c.wait()

    def moment_copy(k):
        return remote(moments.at[k], arrived.at[k], m_send.at[k], m_recv.at[k], (g, after(k)))

    def marker_store(k):
        return pltpu.make_async_copy(marker_s.at[k], marker_out.at[after(k)], out_sem.at[k])

    def owner_markers(k, _):
        q = after(k)
        count = counts[0, q]

        @pl.when((k > 0) & (k + LEAD < OWNERS))
        def _():
            brick_copy(k + LEAD).start()

        @pl.when(k > 0)
        def _():
            brick_copy(k).wait()

        ready, spread = {}, {}
        for t in range(GROUPS + 4):
            if t < GROUPS:
                ready[t] = prepare(q, k, 8 * t, t, pos, bricks, wz_s, wy_s, planes)
            u = t - 2
            if 0 <= u < GROUPS:
                spread[u] = strain(q, k, 8 * u, u, ready.pop(u), mvisc, mdens, marker_s, count, planes)
            u = t - 4
            if 0 <= u < GROUPS:
                deposit(k, 8 * u, u, spread.pop(u), moments, planes)
        marker_store(k).start()

        @pl.when(k > 0)
        def _():
            moment_copy(k).start()

        return 0

    lax.fori_loop(0, 1, owner_markers, 0)
    def wait_ids(k, _):
        remote(ids_send.at[after(k)], ids_recv.at[k], id_send.at[k], id_recv.at[k], (g, after(k))).wait()
        return 0

    lax.fori_loop(1, OWNERS, wait_ids, 0)

    lax.fori_loop(0, 4, gather, 0)

    x_lo_on = (g > 0).astype(F32)
    x_hi_on = (g < 7).astype(F32)
    y_lo_on = (me > 0).astype(F32)
    y_hi_on = (me < OWNERS - 1).astype(F32)
    row = lax.broadcasted_iota(jnp.int32, (NY_L, NZ), 0)
    col = lax.broadcasted_iota(jnp.int32, (NY_L, NZ), 1)
    first_y, last_y = row == 0, row == NY_L - 1
    first_z, last_z = col == 0, col == NZ - 1

    def y_minus(plane, edge):
        return jnp.where(first_y, jnp.broadcast_to(edge, plane.shape), pltpu.roll(plane, 1, 0))

    def y_plus(plane, edge):
        return jnp.where(last_y, jnp.broadcast_to(edge, plane.shape), pltpu.roll(plane, NY_L - 1, 0))

    def z_minus(plane):
        return jnp.where(first_z, 0.0, pltpu.roll(plane, 1, 1))

    def z_plus(plane):
        return jnp.where(last_z, 0.0, pltpu.roll(plane, NZ - 1, 1))

    for c in visc_halo:
        c.wait()
    visc_s[0] = vx_lo[...] * x_lo_on
    visc_s[NX_L + 1] = vx_hi[...] * x_hi_on

    def couplings(x, _):
        here, below, above = visc_s[x + 1], visc_s[x], visc_s[x + 2]
        k_xm, k_xp = 0.5 * (here + below), 0.5 * (here + above)
        k_ym = 0.5 * (here + y_minus(here, vy_lo[pl.ds(x, 1), :] * y_lo_on))
        k_yp = 0.5 * (here + y_plus(here, vy_hi[pl.ds(x, 1), :] * y_hi_on))
        k_zm, k_zp = 0.5 * (here + z_minus(here)), 0.5 * (here + z_plus(here))
        kx[x] = k_xm
        kx[x + 1] = k_xp
        kym[x] = k_ym
        kyp[x] = k_yp
        kzm[x] = k_zm
        kzp[x] = k_zp
        damp[x] = relax_weight / (k_xm + k_xp + k_ym + k_yp + k_zm + k_zp)
        return 0

    lax.fori_loop(0, NX_L, couplings, 0, unroll=2)

    for n in range(SWEEPS):
        old, new = (state_a, state_b) if n % 2 == 0 else (state_b, state_a)
        for c in halo(n, old):
            c.wait()
        old[:, 0] = x_lo[n] * x_lo_on
        old[:, NX_L + 1] = x_hi[n] * x_hi_on

        def sweep(x, _, n=n, old=old, new=new):
            low = y_lo[n, x] * y_lo_on
            high = y_hi[n, x] * y_hi_on
            press = old[3, x + 1]
            press_near = [
                old[3, x],
                y_minus(press, low[3:4]),
                z_minus(press),
            ]
            weights = [kx[x + 1], kx[x], kyp[x], kym[x], kzp[x], kzm[x]]
            scale = damp[x]
            divergence = jnp.zeros_like(press)
            fresh = []
            for c in range(3):
                v = old[c, x + 1]
                near = [
                    old[c, x + 2],
                    old[c, x],
                    y_plus(v, high[c : c + 1]),
                    y_minus(v, low[c : c + 1]),
                    z_plus(v),
                    z_minus(v),
                ]
                forcing = press_near[c] - press
                for w, s in zip(weights, near):
                    forcing = forcing + w * (s - v)
                if c == 2:
                    forcing = forcing - gravity * dens_s[x]
                fresh.append(v + scale * forcing)
                divergence = divergence + (near[2 * c] - v)
            fresh.append(press - pressure_rate * visc_s[x + 1] * divergence)
            for c in range(4):
                new[c, x + 1] = fresh[c]
            if n + 1 < SWEEPS:
                face_lo[n + 1, x] = jnp.concatenate([f[0:1] for f in fresh], axis=0)
                face_hi[n + 1, x] = jnp.concatenate([f[15:16] for f in fresh], axis=0)
            return 0

        lax.fori_loop(0, NX_L, sweep, 0, unroll=2)
        if n + 1 < SWEEPS:
            for c in halo(n + 1, new):
                c.start()
        if n + 1 < SWEEPS:
            lax.fori_loop(1 + 5 * n, 6 + 5 * n, owner_markers, 0)
    last = state_a if SWEEPS % 2 == 0 else state_b
    stores = [
        pltpu.make_async_copy(last.at[pl.ds(0, 3), pl.ds(1, NX_L)], velocity_out, load_sem.at[5]),
        pltpu.make_async_copy(last.at[3, pl.ds(1, NX_L)], pressure_out, load_sem.at[6]),
    ]
    for c in stores:
        c.start()
    own = pltpu.make_async_copy(moments.at[0], arrived.at[0], load_sem.at[9])
    own.start()
    ids_out[...] = ids_recv[...]

    def arrive(k, _):
        moment_copy(k).wait()
        return 0

    lax.fori_loop(1, OWNERS, arrive, 0)

    def wait_markers(k, _):
        marker_store(k).wait()
        return 0

    lax.fori_loop(0, OWNERS, wait_markers, 0)
    own.wait()
    for c in stores:
        c.wait()


def home_kernel(
    moments, ids, visc, dens, velocity, pressure, markers,
    visc_out, dens_out, velocity_out, pressure_out, markers_out,
    arrived, visc_s, dens_s, velocity_s, pressure_s, markers_s, hits, hi_s, lo_s, sums, cells, sem,
):
    loads = [
        pltpu.make_async_copy(moments, arrived, sem.at[0]),
        pltpu.make_async_copy(visc, visc_s, sem.at[1]),
        pltpu.make_async_copy(dens, dens_s, sem.at[2]),
    ]
    stages = ((velocity, velocity_s, velocity_out), (pressure, pressure_s, pressure_out), (markers, markers_s, markers_out))
    fetches = [pltpu.make_async_copy(a, b, sem.at[3 + n]) for n, (a, b, c) in enumerate(stages)]
    copies = [pltpu.make_async_copy(b, c, sem.at[6 + n]) for n, (a, b, c) in enumerate(stages)]
    for c in loads + fetches:
        c.start()
    lane = lax.broadcasted_iota(jnp.int32, (8, 128), 1)
    rows = [jnp.full((8, 128), -1.0, F32) for _ in range(6)]
    for k in range(OWNERS):
        at = CAP * k
        t, off = at // 128, at % 128
        tile = ids[k]
        turned = pltpu.roll(tile, off, 1) if off else tile
        rows[t] = jnp.where((lane >= off) & (lane < off + CAP), turned, rows[t])
        over = off + CAP - 128
        if over > 0:
            rows[t + 1] = jnp.where(lane < over, turned, rows[t + 1])

    wide = [jnp.concatenate([r, r], axis=0) for r in rows]
    sub = lax.broadcasted_iota(jnp.int32, (16, 128), 0).astype(F32)

    def mark_hits(r, _):
        at = pl.multiple_of(r * 16, 16)
        here = sub + (r * 16).astype(F32)
        for t in range(6):
            hits[pl.ds(at, 16), pl.ds(128 * t, 128)] = jnp.where(wide[t] == here, 1.0, 0.0).astype(BF16)
        return 0

    lax.fori_loop(0, BRICKS // 16, mark_hits, 0, unroll=4)

    for c in loads:
        c.wait()

    def moment_pieces(k, _):
        hi, lo = split(arrived[k])
        at = pl.multiple_of(k * CAP, 16)
        hi_s[pl.ds(at, CAP), :] = hi
        lo_s[pl.ds(at, CAP), :] = lo
        return 0

    lax.fori_loop(0, OWNERS, moment_pieces, 0)

    group = lane // 8

    def scatter(n):
        at = pl.ds(256 * n, 256)
        block = hits[at, :]
        total = jnp.dot(block, hi_s[...], preferred_element_type=F32)
        total = total + jnp.dot(block, lo_s[...], preferred_element_type=F32)
        for m in range(3):
            sums[m, at, :] = total[:, 128 * m : 128 * m + 128]

    def to_cells(bj):
        for h in range(2):
            for m in range(3):
                tiles = [sums[m, pl.ds((bj * 32 + h * 16 + t) * 8, 8), :] for t in range(16)]
                tiles = group_transpose(tiles, group)
                for i in range(4):
                    for j in range(4):
                        cells[m, h, pl.ds(16 * i + 4 * bj + j, 8, stride=64), :] = tiles[4 * i + j]

    for fetch, c in zip(fetches, copies):
        fetch.wait()
        c.start()
    scatter(0)
    for n in range(4):
        if n < 3:
            scatter(n + 1)
        to_cells(n)

    def finish(x, _):
        at = pl.ds(pl.multiple_of(x * 16, 16), 16)
        for h in range(2):
            part = pl.ds(128 * h, 128)
            below = 1.0 / (cells[0, h, at, :] + 1.0)
            visc_out[x, :, part] = jnp.exp((cells[1, h, at, :] + jnp.log(visc_s[x, :, part])) * below)
            dens_out[x, :, part] = (cells[2, h, at, :] + dens_s[x, :, part]) * below
        return 0

    lax.fori_loop(0, NX_L, finish, 0, unroll=2)
    for c in copies:
        c.wait()


def per_device(
    velocity, pressure, cell_visc, cell_dens, block_brick, block_counts, positions, start_visc, marker_dens
):
    vm = pl.BlockSpec(memory_space=pltpu.VMEM)
    hbm = pl.BlockSpec(memory_space=pl.ANY)
    dma = pltpu.SemaphoreType.DMA
    field = (NX_L, NY_L, NZ)
    padded = (NX_L + 2, NY_L, NZ)
    shape = jax.ShapeDtypeStruct
    velocity_next, pressure_next, markers, moments, ids = pl.pallas_call(
        step_kernel,
        out_shape=(
            shape((3,) + field, F32),
            shape(field, F32),
            shape((OWNERS, CAP, BLOCK), F32),
            shape((OWNERS, CAP, 384), F32),
            shape((OWNERS, 8, 128), F32),
        ),
        in_specs=[pl.BlockSpec(memory_space=pltpu.SMEM), vm] + [hbm] * 7,
        out_specs=(hbm, hbm, hbm, hbm, vm),
        scratch_shapes=[
            VMEM((4,) + padded, F32),
            VMEM((4,) + padded, F32),
            VMEM(padded, F32),
            VMEM(field, F32),
            VMEM((2, 1536, 128), F32),
            VMEM((BRICKS, 384), BF16),
            VMEM((BRICKS, 384), BF16),
            VMEM((4 * CAP, BRICKS), BF16),
            VMEM((OWNERS, 8, 128), F32),
            VMEM((OWNERS, 8, 128), F32),
            VMEM((OWNERS, CAP, 384), F32),
            VMEM((OWNERS, CAP, 384), F32),
            VMEM((NX_L + 1, NY_L, NZ), F32),
            VMEM(field, F32),
            VMEM(field, F32),
            VMEM(field, F32),
            VMEM(field, F32),
            VMEM(field, F32),
            VMEM((SWEEPS, 4, NY_L, NZ), F32),
            VMEM((SWEEPS, 4, NY_L, NZ), F32),
            VMEM((SWEEPS, NX_L, 4, NZ), F32),
            VMEM((SWEEPS, NX_L, 4, NZ), F32),
            VMEM((SWEEPS, NX_L, 4, NZ), F32),
            VMEM((SWEEPS, NX_L, 4, NZ), F32),
            VMEM((NY_L, NZ), F32),
            VMEM((NY_L, NZ), F32),
            VMEM((NX_L, NZ), F32),
            VMEM((NX_L, NZ), F32),
            VMEM((NX_L, NZ), F32),
            VMEM((NX_L, NZ), F32),
            VMEM((OWNERS, 3, CAP, BLOCK), F32),
            VMEM((OWNERS, CAP, BLOCK), F32),
            VMEM((OWNERS, CAP, BLOCK), F32),
            VMEM((OWNERS, CAP, BLOCK), F32),
            VMEM((OWNERS, CAP, 384), F32),
            VMEM((GROUPS, 2, 64, 128), F32),
            VMEM((GROUPS, 2, 32, 128), F32),
            VMEM((GROUPS, 2, 256, 256), BF16),
            dma((10,)),
            dma((OWNERS,)),
            dma((OWNERS,)),
            dma((OWNERS,)),
            dma((OWNERS,)),
            dma((SWEEPS, 4)),
            dma((SWEEPS, 4)),
            dma((4,)),
            dma((4,)),
            dma((OWNERS,)),
            dma((OWNERS,)),
            dma((OWNERS,)),
        ],
        compiler_params=pltpu.CompilerParams(
            collective_id=0, has_side_effects=True, vmem_limit_bytes=56 << 20
        ),
        name="step",
    )(
        block_counts, block_brick, velocity, pressure, cell_visc, cell_dens,
        positions, start_visc, marker_dens,
    )
    visc_next, dens_next, velocity_next, pressure_next, markers = pl.pallas_call(
        home_kernel,
        out_shape=(
            shape(field, F32),
            shape(field, F32),
            shape((3,) + field, F32),
            shape(field, F32),
            shape((OWNERS, CAP, BLOCK), F32),
        ),
        in_specs=[hbm, vm] + [hbm] * 5,
        out_specs=(vm, vm, hbm, hbm, hbm),
        scratch_shapes=[
            VMEM((OWNERS, CAP, 384), F32),
            VMEM(field, F32),
            VMEM(field, F32),
            VMEM((3,) + field, F32),
            VMEM(field, F32),
            VMEM((OWNERS, CAP, BLOCK), F32),
            VMEM((BRICKS, OWNERS * CAP), BF16),
            VMEM((OWNERS * CAP, 384), BF16),
            VMEM((OWNERS * CAP, 384), BF16),
            VMEM((3, BRICKS, 128), F32),
            VMEM((3, 2, 512, 128), F32),
            dma((9,)),
        ],
        compiler_params=pltpu.CompilerParams(vmem_limit_bytes=56 << 20),
        name="home",
    )(moments, ids, cell_visc, cell_dens, velocity_next, pressure_next, markers)
    return velocity_next, pressure_next, visc_next, dens_next, markers


def solution(mesh):
    in_specs = (
        P(None, "grid", "mark", None),
        P("grid", "mark", None),
        P("grid", "mark", None),
        P("grid", "mark", None),
        P(("grid", "mark"), None),
        P(("grid", "mark"), None),
        P(("grid", "mark"), None, None, None),
        P(("grid", "mark"), None, None),
        P(("grid", "mark"), None, None),
    )
    out_specs = (
        P(None, "grid", "mark", None),
        P("grid", "mark", None),
        P("grid", "mark", None),
        P("grid", "mark", None),
        P(("grid", "mark"), None, None),
    )
    return jax.shard_map(
        per_device, mesh=mesh, in_specs=in_specs, out_specs=out_specs, check_vma=False
    )
```

```python
import functools
import math
import jax
import jax.numpy as jnp
from jax import lax
from jax.sharding import PartitionSpec as P
from jax.experimental import pallas as pl
from jax.experimental.pallas import tpu as pltpu

F32, BF16 = jnp.float32, jnp.bfloat16
VMEM = pltpu.VMEM
CAP, BLOCK, OWNERS = 48, 256, 16
NT = (((1,), (1,)), ((), ()))
GROUPS = 6


def split(x):
    hi = x.astype(BF16)
    return hi, (x - hi.astype(F32)).astype(BF16)


def axis_weights(fraction, cells):
    half = 0.5 * cells
    turn = 2.0 / math.log(2.0)
    factor = jnp.exp2((turn * cells) * fraction - turn * half)
    centres = [i + 0.5 - half for i in range(cells)]
    powers = [None, factor]
    for i in range(2, cells):
        powers.append(powers[i // 2] * powers[i - i // 2])
    raw = [jnp.full_like(factor, math.exp(-centres[0] ** 2))]
    raw += [math.exp(-(centres[i] ** 2)) * powers[i] for i in range(1, cells)]
    total = functools.reduce(jnp.add, raw)
    scale = 1.0 / total
    weights = [r * scale for r in raw]
    mean = functools.reduce(
        jnp.add, [centres[-1 - n] * (weights[-1 - n] - weights[n]) for n in range(cells // 2)]
    )
    return weights, mean


def masks():
    sub = lax.broadcasted_iota(jnp.int32, (8, 128), 0)
    lane = lax.broadcasted_iota(jnp.int32, (8, 128), 1)
    sub2 = lax.broadcasted_iota(jnp.int32, (8, 256), 0)
    return sub, lane, sub2, sub < 4, sub2 < 4


def both(x, low):
    turned = pltpu.roll(x, 4, 0)
    return jnp.where(low, x, turned), jnp.where(low, turned, x)


def fold(a, b, low):
    return jnp.where(low, a, b) + pltpu.roll(jnp.where(low, b, a), 4, 0)


def skew(x, sub, sign):
    out = x
    for s in range(1, 4):
        out = jnp.where(sub % 4 == s, pltpu.roll(x, (sign * 32 * s) % 128, 1), out)
    return out


def pieces(tiles):
    his, los = [], []
    for n in range(0, len(tiles), 2):
        hi, lo = split(jnp.concatenate(tiles[n : n + 2], axis=0))
        his.append(hi)
        los.append(lo)
    return jnp.concatenate(his + los, axis=0)


def prepare(q, k, row, u, pos, bricks, wz_s, wy_s, planes):
    rows = pl.ds(row, 8)
    sub, lane, sub2, low, low2 = masks()
    wx, mean_x = axis_weights(pos[q, 0, rows, :], 4)
    wy, mean_y = axis_weights(pos[q, 1, rows, :], 4)
    wz, mean_z = axis_weights(pos[q, 2, rows, :], 8)
    for h in range(2):
        part = slice(128 * h, 128 * h + 128)
        for n in range(8):
            wz_s[u, h, pl.ds(8 * n, 8), :] = wz[n][:, part]
        for j in range(4):
            wy_s[u, h, pl.ds(8 * j, 8), :] = wy[j][:, part]
    for b in range(8):
        for h in range(2):
            col = wz_s[u, h, pl.ds(b, 8, stride=8), :]
            for jp in range(2):
                pair = [
                    col * jnp.broadcast_to(wy_s[u, h, pl.ds(8 * j + b, 1), :], (8, 128))
                    for j in (2 * jp, 2 * jp + 1)
                ]
                hi, lo = split(jnp.concatenate(pair, axis=0))
                at = 32 * (b % 4) + 16 * jp
                planes[u, b // 4, pl.ds(at, 16), pl.ds(128 * h, 128)] = hi
                planes[u, b // 4, pl.ds(128 + at, 16), pl.ds(128 * h, 128)] = lo

    diag = (lane // 32) == (sub % 4)
    turned_i = (lane // 32 + 4 - sub % 4) % 4
    c_i = turned_i.astype(F32) - 1.5
    c_j = ((lane // 8) % 4).astype(F32) - 1.5
    c_k = (lane % 8).astype(F32) - 3.5
    v = [both(skew(bricks[k, rows, pl.ds(128 * c, 128)], sub, 1), low) for c in range(3)]
    sub16 = lax.broadcasted_iota(jnp.int32, (16, 128), 0)
    lane16 = lax.broadcasted_iota(jnp.int32, (16, 128), 1)
    low16 = sub16 % 8 < 4
    diag16 = (lane16 // 32) == (sub16 % 4)
    lefts = []
    for side in range(2):
        vx, vy, vz = [x[side] for x in v]
        kinds = [
            vx, vy, vz, c_j * vy, c_k * vz,
            c_j * vx + c_i * vy, c_k * vx + c_i * vz, c_k * vy + c_j * vz,
        ]
        parts = []
        for n in range(0, 8, 2):
            parts.append(split(jnp.concatenate(kinds[n : n + 2], axis=0)))
        left = []
        for piece in range(2):
            for part in parts:
                src = part[piece]
                turned = [src] + [pltpu.roll(src, 128 - 32 * i, 1) for i in range(1, 4)]
                for ip in range(2):
                    tile = jnp.where(low16, turned[2 * ip], turned[2 * ip + 1])
                    left.append(jnp.where(diag16, tile, jnp.zeros_like(tile)))
        lefts.append(jnp.concatenate(left, axis=0))
    pairs = ([], [])
    for ip in range(2):
        first, second = both(wx[2 * ip], low2), both(wx[2 * ip + 1], low2)
        for side in range(2):
            pairs[side].append(jnp.where(low2, first[side], second[side]))
    return lefts, pairs, (mean_x, mean_y, mean_z)


def strain(q, k, row, u, prepared, visc, dens, marker_out, count, planes):
    rows = pl.ds(row, 8)
    sub, lane, sub2, low, low2 = masks()
    lefts, pairs, (mean_x, mean_y, mean_z) = prepared
    results = []
    for side in range(2):
        left = jnp.concatenate([lefts[side], lefts[side]], axis=1)
        out = jnp.dot(left, planes[u, side], preferred_element_type=F32)
        results.append(out[:128] + out[128:])
    centred = [
        [pairs[side][ip] * jnp.where(low2, 2 * ip - 1.5, 2 * ip - 0.5) for ip in range(2)]
        for side in range(2)
    ]

    def along_x(kind, weights):
        at = 32 * (kind // 2) + 8 * (kind % 2)
        sums = [
            results[side][at : at + 8] * weights[side][0]
            + results[side][at + 16 : at + 24] * weights[side][1]
            for side in range(2)
        ]
        return fold(*sums, low2)

    vx, vy, vz, yy, zz, xy, xz, yz = [along_x(n, pairs) for n in range(8)]
    xx = along_x(0, centred) - mean_x * vx
    yy = yy - mean_y * vy
    zz = zz - mean_z * vz
    xy = xy - mean_y * vx - mean_x * vy
    xz = xz - mean_z * vx - mean_x * vz
    yz = yz - mean_z * vy - mean_y * vz
    invariant = 2.0 * (xx * xx + yy * yy + zz * zz) + xy * xy + xz * xz + yz * yz
    shift = jnp.log2(1.0 + invariant * 4.0) * (-1.0 / 3.0)
    start = visc[q, rows, :]
    live = (sub2 + row) < count
    weakened = start * jnp.exp2(shift)
    marker_out[k, rows, :] = jnp.where(live, weakened, 0.0)
    carried = [
        jnp.where(live, 1.0, 0.0),
        jnp.where(live, math.log(2.0) * (jnp.log2(start) + shift), 0.0),
        jnp.where(live, dens[q, rows, :], 0.0),
    ]
    carried = [both(c, low2) for c in carried]
    return [
        pieces([carried[m][side] * pairs[side][ip] for m in range(3) for ip in range(2)])
        for side in range(2)
    ]


def deposit(k, row, u, lefts, moments, planes):
    rows = pl.ds(row, 8)
    sub, lane, sub2, low, low2 = masks()
    diag = (lane // 32) == (sub % 4)
    sums = []
    for side in range(2):
        out = lax.dot_general(lefts[side], planes[u, side], NT, preferred_element_type=F32)
        sums.append(out[:48, :128] + out[:48, 128:] + out[48:, :128])
    for m in range(3):
        halves = []
        for side in range(2):
            p = [jnp.where(diag, sums[side][16 * m + 8 * ip : 16 * m + 8 * ip + 8], 0.0) for ip in range(2)]
            halves.append(
                jnp.where(low, p[0], pltpu.roll(p[0], 32, 1))
                + jnp.where(low, pltpu.roll(p[1], 64, 1), pltpu.roll(p[1], 96, 1))
            )
        moments[k, rows, pl.ds(128 * m, 128)] = skew(fold(*halves, low), sub, -1)


NX_L, NY_L, NZ = 32, 16, 256
BRICKS = 1024
MESH = pl.DeviceIdType.MESH
SWEEPS = 4
relax_weight = 0.6
pressure_rate = 0.25
gravity = 1.0


def group_transpose(tiles, group):
    tiles = list(tiles)
    for d in (8, 4, 2, 1):
        upper = (group & d) != 0
        for t in range(16):
            if t & d == 0:
                a, b = tiles[t], tiles[t + d]
                tiles[t] = jnp.where(upper, pltpu.roll(b, 8 * d, 1), a)
                tiles[t + d] = jnp.where(upper, b, pltpu.roll(a, 128 - 8 * d, 1))
    return tiles


PAIRS = (
    (0, 0), (0, 1), (1, 0), (0, 3), (3, 0), (1, 1), (3, 3), (1, 3),
    (3, 1), (0, 2), (2, 0), (2, 1), (1, 2), (2, 3), (3, 2), (2, 2),
)
LEAD = 7


def peers():
    g, me = lax.axis_index("grid"), lax.axis_index("mark")
    z, y = me // 4, lax.rem(me, 4)

    def chosen(k, values):
        if isinstance(k, int):
            return values[k]
        out = values[0]
        for n in range(1, OWNERS):
            out = jnp.where(k == n, values[n], out)
        return out

    def after(k):
        dz = chosen(k, [p[0] for p in PAIRS])
        dy = chosen(k, [p[1] for p in PAIRS])
        return lax.rem(z + dz, 4) * 4 + lax.rem(y + dy, 4)

    def before(k):
        dz = chosen(k, [4 - p[0] for p in PAIRS])
        dy = chosen(k, [4 - p[1] for p in PAIRS])
        return lax.rem(z + dz, 4) * 4 + lax.rem(y + dy, 4)

    return g, me, after, before


def remote(src, dst, send, recv, device):
    return pltpu.make_async_remote_copy(
        src_ref=src, dst_ref=dst, send_sem=send, recv_sem=recv, device_id=device, device_id_type=MESH
    )


def step_kernel(
    counts, ids_in, velocity, pressure, visc, dens, positions, start_visc, marker_dens,
    velocity_out, pressure_out, marker_out, arrived, ids_out,
    brick_ids, state_a, state_b, visc_s, dens_s, halves, planes_hi, planes_lo, one_hot, ids_send, ids_recv,
    brick_send, bricks, kx, kym, kyp, kzm, kzp, damp, x_lo, x_hi, face_lo, face_hi, y_lo, y_hi,
    vx_lo, vx_hi, vface_lo, vface_hi, vy_lo, vy_hi, pos, mvisc, mdens, marker_s, moments, wz_s, wy_s, planes,
    load_sem, id_send, id_recv, b_send, b_recv, h_send, h_recv, v_send, v_recv, m_send, m_recv, out_sem,
):
    g, me, after, before = peers()
    ahead, behind = lax.rem(g + 1, 8), lax.rem(g + 7, 8)
    north, south = lax.rem(me + 1, OWNERS), lax.rem(me + OWNERS - 1, OWNERS)
    loads = [
        pltpu.make_async_copy(velocity, state_a.at[pl.ds(0, 3), pl.ds(1, NX_L)], load_sem.at[0]),
        pltpu.make_async_copy(pressure, state_a.at[3, pl.ds(1, NX_L)], load_sem.at[1]),
        pltpu.make_async_copy(visc, visc_s.at[pl.ds(1, NX_L)], load_sem.at[2]),
        pltpu.make_async_copy(dens, dens_s, load_sem.at[3]),
    ]
    ids_load = pltpu.make_async_copy(ids_in, brick_ids, load_sem.at[10])
    ids_load.start()
    marker_loads = [
        pltpu.make_async_copy(positions, pos, load_sem.at[4]),
        pltpu.make_async_copy(start_visc, mvisc, load_sem.at[7]),
        pltpu.make_async_copy(marker_dens, mdens, load_sem.at[8]),
    ]
    for c in loads + marker_loads:
        c.start()
    barrier = pltpu.get_barrier_semaphore()
    for k in range(1, OWNERS):
        pl.semaphore_signal(barrier, inc=1, device_id=(g, after(k)), device_id_type=MESH)
    pl.semaphore_signal(barrier, inc=1, device_id=(ahead, me), device_id_type=MESH)
    pl.semaphore_signal(barrier, inc=1, device_id=(behind, me), device_id_type=MESH)

    ids_load.wait()
    number = brick_ids[...]
    number = (((number >> 5) & 3) * 32 + (number & 31)) * 8 + (number >> 7)
    number = number.astype(F32)
    ids_send[...] = jnp.full((OWNERS, 8, 128), -1.0, F32)
    for q in range(OWNERS):
        ids_send[q, :, pl.ds(0, CAP)] = jnp.broadcast_to(number[q : q + 1], (8, CAP))

    ids_recv[0] = ids_send[me]
    for c in loads:
        c.wait()

    def first_faces(x, _):
        face_lo[0, x] = jnp.concatenate([state_a[c, x + 1, 0:1, :] for c in range(4)], axis=0)
        face_hi[0, x] = jnp.concatenate([state_a[c, x + 1, 15:16, :] for c in range(4)], axis=0)
        return 0

    lax.fori_loop(0, NX_L, first_faces, 0, unroll=4)
    for x in range(NX_L):
        vface_lo[x : x + 1, :] = visc_s[x + 1, 0:1, :]
        vface_hi[x : x + 1, :] = visc_s[x + 1, 15:16, :]
    pl.semaphore_wait(barrier, OWNERS + 1)

    def send_ids(k, _):
        remote(ids_send.at[after(k)], ids_recv.at[k], id_send.at[k], id_recv.at[k], (g, after(k))).start()
        return 0

    lax.fori_loop(1, OWNERS, send_ids, 0)
    def halo(n, state):
        return [
            remote(state.at[:, 1], x_hi.at[n], h_send.at[n, 0], h_recv.at[n, 0], (behind, me)),
            remote(state.at[:, NX_L], x_lo.at[n], h_send.at[n, 1], h_recv.at[n, 1], (ahead, me)),
            remote(face_lo.at[n], y_hi.at[n], h_send.at[n, 2], h_recv.at[n, 2], (g, south)),
            remote(face_hi.at[n], y_lo.at[n], h_send.at[n, 3], h_recv.at[n, 3], (g, north)),
        ]

    visc_halo = [
        remote(visc_s.at[1], vx_hi, v_send.at[0], v_recv.at[0], (behind, me)),
        remote(visc_s.at[NX_L], vx_lo, v_send.at[1], v_recv.at[1], (ahead, me)),
        remote(vface_lo, vy_hi, v_send.at[2], v_recv.at[2], (g, south)),
        remote(vface_hi, vy_lo, v_send.at[3], v_recv.at[3], (g, north)),
    ]
    for c in halo(0, state_a) + visc_halo:
        c.start()

    def to_halves(x, _):
        for c in range(3):
            plane = state_a[c, x + 1]
            at = pl.multiple_of(c * 512 + x * 16, 16)
            for h in range(2):
                halves[h, pl.ds(at, 16), :] = plane[:, 128 * h : 128 * h + 128]
        return 0

    lax.fori_loop(0, NX_L, to_halves, 0, unroll=2)
    group = lax.broadcasted_iota(jnp.int32, (8, 128), 1) // 8

    def to_bricks(n, _):
        bj, h = n // 2, lax.rem(n, 2)
        for c in range(3):
            tiles = [
                halves[h, pl.ds(c * 512 + 16 * i + 4 * bj + j, 8, stride=64), :]
                for i in range(4)
                for j in range(4)
            ]
            tiles = group_transpose(tiles, group)
            for t in range(0, 16, 2):
                hi, lo = split(jnp.concatenate(tiles[t : t + 2], axis=0))
                at = pl.multiple_of((bj * 32 + h * 16 + t) * 8, 16)
                planes_hi[pl.ds(at, 16), pl.ds(128 * c, 128)] = hi
                planes_lo[pl.ds(at, 16), pl.ds(128 * c, 128)] = lo
        return 0

    lax.fori_loop(0, 8, to_bricks, 0)

    def brick_copy(k):
        return remote(
            brick_send.at[k], bricks.at[k], b_send.at[k], b_recv.at[k], (g, before(k))
        )

    lanes = lax.broadcasted_iota(jnp.int32, (CAP, 128), 1).astype(F32)

    def hits_of(k, m):
        column = jnp.transpose(jnp.broadcast_to(ids_recv[k][0:1, :], (128, 128)))[:CAP]
        for t in range(8):
            hit = jnp.where(column == lanes + 128.0 * t, 1.0, 0.0).astype(BF16)
            one_hot[pl.ds(CAP * m, CAP), pl.ds(128 * t, 128)] = hit

    def gather(n, _):
        for m in range(4):
            hits_of(4 * n + m, m)
        found = jnp.dot(one_hot[...], planes_hi[...], preferred_element_type=F32)
        found = found + jnp.dot(one_hot[...], planes_lo[...], preferred_element_type=F32)
        for m in range(4):
            brick_send[4 * n + m] = found[CAP * m : CAP * m + CAP]
        for m in range(4):
            k = 4 * n + m

            @pl.when((k > 0) & (k <= LEAD))
            def _():
                brick_copy(k).start()

        return 0

    hits_of(0, 0)
    own = one_hot[pl.ds(0, CAP), :]
    bricks[0] = jnp.dot(own, planes_hi[...], preferred_element_type=F32) + jnp.dot(
        own, planes_lo[...], preferred_element_type=F32
    )
    for c in marker_loads:
        c.wait()

    def moment_copy(k):
        return remote(moments.at[k], arrived.at[k], m_send.at[k], m_recv.at[k], (g, after(k)))

    def marker_store(k):
        return pltpu.make_async_copy(marker_s.at[k], marker_out.at[after(k)], out_sem.at[k])

    def owner_markers(k, _):
        q = after(k)
        count = counts[0, q]

        @pl.when((k > 0) & (k + LEAD < OWNERS))
        def _():
            brick_copy(k + LEAD).start()

        @pl.when(k > 0)
        def _():
            brick_copy(k).wait()

        ready, spread = {}, {}
        for t in range(GROUPS + 4):
            if t < GROUPS:
                ready[t] = prepare(q, k, 8 * t, t, pos, bricks, wz_s, wy_s, planes)
            u = t - 2
            if 0 <= u < GROUPS:
                spread[u] = strain(q, k, 8 * u, u, ready.pop(u), mvisc, mdens, marker_s, count, planes)
            u = t - 4
            if 0 <= u < GROUPS:
                deposit(k, 8 * u, u, spread.pop(u), moments, planes)
        marker_store(k).start()

        @pl.when(k > 0)
        def _():
            moment_copy(k).start()

        return 0

    lax.fori_loop(0, 1, owner_markers, 0)
    def wait_ids(k, _):
        remote(ids_send.at[after(k)], ids_recv.at[k], id_send.at[k], id_recv.at[k], (g, after(k))).wait()
        return 0

    lax.fori_loop(1, OWNERS, wait_ids, 0)

    ids_store = pltpu.make_async_copy(ids_recv, ids_out, load_sem.at[11])
    ids_store.start()
    lax.fori_loop(0, 4, gather, 0)

    x_lo_on = (g > 0).astype(F32)
    x_hi_on = (g < 7).astype(F32)
    y_lo_on = (me > 0).astype(F32)
    y_hi_on = (me < OWNERS - 1).astype(F32)
    row = lax.broadcasted_iota(jnp.int32, (NY_L, NZ), 0)
    col = lax.broadcasted_iota(jnp.int32, (NY_L, NZ), 1)
    first_y, last_y = row == 0, row == NY_L - 1
    first_z, last_z = col == 0, col == NZ - 1

    def y_minus(plane, edge):
        return jnp.where(first_y, jnp.broadcast_to(edge, plane.shape), pltpu.roll(plane, 1, 0))

    def y_plus(plane, edge):
        return jnp.where(last_y, jnp.broadcast_to(edge, plane.shape), pltpu.roll(plane, NY_L - 1, 0))

    def z_minus(plane):
        return jnp.where(first_z, 0.0, pltpu.roll(plane, 1, 1))

    def z_plus(plane):
        return jnp.where(last_z, 0.0, pltpu.roll(plane, NZ - 1, 1))

    for c in visc_halo:
        c.wait()
    visc_s[0] = vx_lo[...] * x_lo_on
    visc_s[NX_L + 1] = vx_hi[...] * x_hi_on

    def couplings(x, _):
        here, below, above = visc_s[x + 1], visc_s[x], visc_s[x + 2]
        k_xm, k_xp = 0.5 * (here + below), 0.5 * (here + above)
        k_ym = 0.5 * (here + y_minus(here, vy_lo[pl.ds(x, 1), :] * y_lo_on))
        k_yp = 0.5 * (here + y_plus(here, vy_hi[pl.ds(x, 1), :] * y_hi_on))
        k_zm, k_zp = 0.5 * (here + z_minus(here)), 0.5 * (here + z_plus(here))
        kx[x] = k_xm
        kx[x + 1] = k_xp
        kym[x] = k_ym
        kyp[x] = k_yp
        kzm[x] = k_zm
        kzp[x] = k_zp
        damp[x] = relax_weight / (k_xm + k_xp + k_ym + k_yp + k_zm + k_zp)
        return 0

    lax.fori_loop(0, NX_L, couplings, 0, unroll=2)

    for n in range(SWEEPS):
        old, new = (state_a, state_b) if n % 2 == 0 else (state_b, state_a)
        for c in halo(n, old):
            c.wait()
        old[:, 0] = x_lo[n] * x_lo_on
        old[:, NX_L + 1] = x_hi[n] * x_hi_on

        def sweep(x, _, n=n, old=old, new=new):
            low = y_lo[n, x] * y_lo_on
            high = y_hi[n, x] * y_hi_on
            press = old[3, x + 1]
            press_near = [
                old[3, x],
                y_minus(press, low[3:4]),
                z_minus(press),
            ]
            weights = [kx[x + 1], kx[x], kyp[x], kym[x], kzp[x], kzm[x]]
            scale = damp[x]
            divergence = jnp.zeros_like(press)
            fresh = []
            for c in range(3):
                v = old[c, x + 1]
                near = [
                    old[c, x + 2],
                    old[c, x],
                    y_plus(v, high[c : c + 1]),
                    y_minus(v, low[c : c + 1]),
                    z_plus(v),
                    z_minus(v),
                ]
                forcing = press_near[c] - press
                for w, s in zip(weights, near):
                    forcing = forcing + w * (s - v)
                if c == 2:
                    forcing = forcing - gravity * dens_s[x]
                fresh.append(v + scale * forcing)
                divergence = divergence + (near[2 * c] - v)
            fresh.append(press - pressure_rate * visc_s[x + 1] * divergence)
            for c in range(4):
                new[c, x + 1] = fresh[c]
            if n + 1 < SWEEPS:
                face_lo[n + 1, x] = jnp.concatenate([f[0:1] for f in fresh], axis=0)
                face_hi[n + 1, x] = jnp.concatenate([f[15:16] for f in fresh], axis=0)
            return 0

        lax.fori_loop(0, NX_L, sweep, 0, unroll=4)
        if n + 1 < SWEEPS:
            for c in halo(n + 1, new):
                c.start()
        if n + 1 < SWEEPS:
            lax.fori_loop(1 + 5 * n, 6 + 5 * n, owner_markers, 0)
    last = state_a if SWEEPS % 2 == 0 else state_b
    stores = [
        pltpu.make_async_copy(last.at[pl.ds(0, 3), pl.ds(1, NX_L)], velocity_out, load_sem.at[5]),
        pltpu.make_async_copy(last.at[3, pl.ds(1, NX_L)], pressure_out, load_sem.at[6]),
    ]
    for c in stores:
        c.start()
    own = pltpu.make_async_copy(moments.at[0], arrived.at[0], load_sem.at[9])
    own.start()

    def arrive(k, _):
        moment_copy(k).wait()
        return 0

    lax.fori_loop(1, OWNERS, arrive, 0)

    def wait_markers(k, _):
        marker_store(k).wait()
        return 0

    lax.fori_loop(0, OWNERS, wait_markers, 0)
    own.wait()
    ids_store.wait()
    for c in stores:
        c.wait()


def home_kernel(
    moments, ids_in, visc, dens, velocity, pressure, markers,
    visc_out, dens_out, velocity_out, pressure_out, markers_out,
    ids, visc_new, dens_new, arrived, visc_s, dens_s, velocity_s, pressure_s, markers_s, hits, hi_s, lo_s, sums, cells, sem,
):
    loads = [
        pltpu.make_async_copy(moments, arrived, sem.at[0]),
        pltpu.make_async_copy(visc, visc_s, sem.at[1]),
        pltpu.make_async_copy(dens, dens_s, sem.at[2]),
    ]
    stages = ((velocity, velocity_s, velocity_out), (pressure, pressure_s, pressure_out), (markers, markers_s, markers_out))
    fetches = [pltpu.make_async_copy(a, b, sem.at[3 + n]) for n, (a, b, c) in enumerate(stages)]
    copies = [pltpu.make_async_copy(b, c, sem.at[6 + n]) for n, (a, b, c) in enumerate(stages)]
    ids_load = pltpu.make_async_copy(ids_in, ids, sem.at[9])
    for c in [ids_load] + loads + fetches:
        c.start()
    ids_load.wait()
    lane = lax.broadcasted_iota(jnp.int32, (8, 128), 1)
    rows = [jnp.full((8, 128), -1.0, F32) for _ in range(6)]
    for k in range(OWNERS):
        at = CAP * k
        t, off = at // 128, at % 128
        tile = ids[k]
        turned = pltpu.roll(tile, off, 1) if off else tile
        rows[t] = jnp.where((lane >= off) & (lane < off + CAP), turned, rows[t])
        over = off + CAP - 128
        if over > 0:
            rows[t + 1] = jnp.where(lane < over, turned, rows[t + 1])

    wide = [jnp.concatenate([r, r], axis=0) for r in rows]
    sub = lax.broadcasted_iota(jnp.int32, (16, 128), 0).astype(F32)

    def mark_hits(r, _):
        at = pl.multiple_of(r * 16, 16)
        here = sub + (r * 16).astype(F32)
        for t in range(6):
            hits[pl.ds(at, 16), pl.ds(128 * t, 128)] = jnp.where(wide[t] == here, 1.0, 0.0).astype(BF16)
        return 0

    lax.fori_loop(0, BRICKS // 16, mark_hits, 0, unroll=4)

    for c in loads:
        c.wait()

    def moment_pieces(k, _):
        hi, lo = split(arrived[k])
        at = pl.multiple_of(k * CAP, 16)
        hi_s[pl.ds(at, CAP), :] = hi
        lo_s[pl.ds(at, CAP), :] = lo
        return 0

    lax.fori_loop(0, OWNERS, moment_pieces, 0, unroll=4)

    group = lane // 8

    def scatter(n):
        at = pl.ds(256 * n, 256)
        block = hits[at, :]
        total = jnp.dot(block, hi_s[...], preferred_element_type=F32)
        total = total + jnp.dot(block, lo_s[...], preferred_element_type=F32)
        for m in range(3):
            sums[m, at, :] = total[:, 128 * m : 128 * m + 128]

    def to_cells(bj):
        for h in range(2):
            for m in range(3):
                tiles = [sums[m, pl.ds((bj * 32 + h * 16 + t) * 8, 8), :] for t in range(16)]
                tiles = group_transpose(tiles, group)
                for i in range(4):
                    for j in range(4):
                        cells[m, h, pl.ds(16 * i + 4 * bj + j, 8, stride=64), :] = tiles[4 * i + j]

    for fetch, c in zip(fetches, copies):
        fetch.wait()
        c.start()
    scatter(0)
    for n in range(4):
        if n < 3:
            scatter(n + 1)
        to_cells(n)

    def finish(x, _):
        at = pl.ds(pl.multiple_of(x * 16, 16), 16)
        for h in range(2):
            part = pl.ds(128 * h, 128)
            below = 1.0 / (cells[0, h, at, :] + 1.0)
            visc_new[x, :, part] = jnp.exp((cells[1, h, at, :] + jnp.log(visc_s[x, :, part])) * below)
            dens_new[x, :, part] = (cells[2, h, at, :] + dens_s[x, :, part]) * below
        return 0

    for n in range(4):
        lax.fori_loop(8 * n, 8 * n + 8, finish, 0, unroll=2)
        part = pl.ds(8 * n, 8)
        for m, (new, out) in enumerate(((visc_new, visc_out), (dens_new, dens_out))):
            c = pltpu.make_async_copy(new.at[part], out.at[part], sem.at[10 + 2 * n + m])
            c.start()
            copies.append(c)
    for c in copies:
        c.wait()


def per_device(
    velocity, pressure, cell_visc, cell_dens, block_brick, block_counts, positions, start_visc, marker_dens
):
    hbm = pl.BlockSpec(memory_space=pl.ANY)
    dma = pltpu.SemaphoreType.DMA
    field = (NX_L, NY_L, NZ)
    padded = (NX_L + 2, NY_L, NZ)
    shape = jax.ShapeDtypeStruct
    velocity_next, pressure_next, markers, moments, ids = pl.pallas_call(
        step_kernel,
        out_shape=(
            shape((3,) + field, F32),
            shape(field, F32),
            shape((OWNERS, CAP, BLOCK), F32),
            shape((OWNERS, CAP, 384), F32),
            shape((OWNERS, 8, 128), F32),
        ),
        in_specs=[pl.BlockSpec(memory_space=pltpu.SMEM)] + [hbm] * 8,
        out_specs=(hbm,) * 5,
        scratch_shapes=[
            VMEM((OWNERS, CAP), jnp.int32),
            VMEM((4,) + padded, F32),
            VMEM((4,) + padded, F32),
            VMEM(padded, F32),
            VMEM(field, F32),
            VMEM((2, 1536, 128), F32),
            VMEM((BRICKS, 384), BF16),
            VMEM((BRICKS, 384), BF16),
            VMEM((4 * CAP, BRICKS), BF16),
            VMEM((OWNERS, 8, 128), F32),
            VMEM((OWNERS, 8, 128), F32),
            VMEM((OWNERS, CAP, 384), F32),
            VMEM((OWNERS, CAP, 384), F32),
            VMEM((NX_L + 1, NY_L, NZ), F32),
            VMEM(field, F32),
            VMEM(field, F32),
            VMEM(field, F32),
            VMEM(field, F32),
            VMEM(field, F32),
            VMEM((SWEEPS, 4, NY_L, NZ), F32),
            VMEM((SWEEPS, 4, NY_L, NZ), F32),
            VMEM((SWEEPS, NX_L, 4, NZ), F32),
            VMEM((SWEEPS, NX_L, 4, NZ), F32),
            VMEM((SWEEPS, NX_L, 4, NZ), F32),
            VMEM((SWEEPS, NX_L, 4, NZ), F32),
            VMEM((NY_L, NZ), F32),
            VMEM((NY_L, NZ), F32),
            VMEM((NX_L, NZ), F32),
            VMEM((NX_L, NZ), F32),
            VMEM((NX_L, NZ), F32),
            VMEM((NX_L, NZ), F32),
            VMEM((OWNERS, 3, CAP, BLOCK), F32),
            VMEM((OWNERS, CAP, BLOCK), F32),
            VMEM((OWNERS, CAP, BLOCK), F32),
            VMEM((OWNERS, CAP, BLOCK), F32),
            VMEM((OWNERS, CAP, 384), F32),
            VMEM((GROUPS, 2, 64, 128), F32),
            VMEM((GROUPS, 2, 32, 128), F32),
            VMEM((GROUPS, 2, 256, 256), BF16),
            dma((12,)),
            dma((OWNERS,)),
            dma((OWNERS,)),
            dma((OWNERS,)),
            dma((OWNERS,)),
            dma((SWEEPS, 4)),
            dma((SWEEPS, 4)),
            dma((4,)),
            dma((4,)),
            dma((OWNERS,)),
            dma((OWNERS,)),
            dma((OWNERS,)),
        ],
        compiler_params=pltpu.CompilerParams(
            collective_id=0, has_side_effects=True, vmem_limit_bytes=56 << 20
        ),
        name="step",
    )(
        block_counts, block_brick, velocity, pressure, cell_visc, cell_dens,
        positions, start_visc, marker_dens,
    )
    visc_next, dens_next, velocity_next, pressure_next, markers = pl.pallas_call(
        home_kernel,
        out_shape=(
            shape(field, F32),
            shape(field, F32),
            shape((3,) + field, F32),
            shape(field, F32),
            shape((OWNERS, CAP, BLOCK), F32),
        ),
        in_specs=[hbm] * 7,
        out_specs=(hbm,) * 5,
        scratch_shapes=[
            VMEM((OWNERS, 8, 128), F32),
            VMEM(field, F32),
            VMEM(field, F32),
            VMEM((OWNERS, CAP, 384), F32),
            VMEM(field, F32),
            VMEM(field, F32),
            VMEM((3,) + field, F32),
            VMEM(field, F32),
            VMEM((OWNERS, CAP, BLOCK), F32),
            VMEM((BRICKS, OWNERS * CAP), BF16),
            VMEM((OWNERS * CAP, 384), BF16),
            VMEM((OWNERS * CAP, 384), BF16),
            VMEM((3, BRICKS, 128), F32),
            VMEM((3, 2, 512, 128), F32),
            dma((18,)),
        ],
        compiler_params=pltpu.CompilerParams(vmem_limit_bytes=56 << 20),
        name="home",
    )(moments, ids, cell_visc, cell_dens, velocity_next, pressure_next, markers)
    return velocity_next, pressure_next, visc_next, dens_next, markers


def solution(mesh):
    in_specs = (
        P(None, "grid", "mark", None),
        P("grid", "mark", None),
        P("grid", "mark", None),
        P("grid", "mark", None),
        P(("grid", "mark"), None),
        P(("grid", "mark"), None),
        P(("grid", "mark"), None, None, None),
        P(("grid", "mark"), None, None),
        P(("grid", "mark"), None, None),
    )
    out_specs = (
        P(None, "grid", "mark", None),
        P("grid", "mark", None),
        P("grid", "mark", None),
        P("grid", "mark", None),
        P(("grid", "mark"), None, None),
    )
    return jax.shard_map(
        per_device, mesh=mesh, in_specs=in_specs, out_specs=out_specs, check_vma=False
    )
```

```python
import functools
import math
import jax
import jax.numpy as jnp
from jax import lax
from jax.sharding import PartitionSpec as P
from jax.experimental import pallas as pl
from jax.experimental.pallas import tpu as pltpu

F32, BF16 = jnp.float32, jnp.bfloat16
VMEM = pltpu.VMEM
CAP, BLOCK, OWNERS = 48, 256, 16
NT = (((1,), (1,)), ((), ()))
GROUPS = 6


def split(x):
    hi = x.astype(BF16)
    return hi, (x - hi.astype(F32)).astype(BF16)


def axis_weights(fraction, cells):
    half = 0.5 * cells
    turn = 2.0 / math.log(2.0)
    factor = jnp.exp2((turn * cells) * fraction - turn * half)
    centres = [i + 0.5 - half for i in range(cells)]
    powers = [None, factor]
    for i in range(2, cells):
        powers.append(powers[i // 2] * powers[i - i // 2])
    raw = [jnp.full_like(factor, math.exp(-centres[0] ** 2))]
    raw += [math.exp(-(centres[i] ** 2)) * powers[i] for i in range(1, cells)]
    total = functools.reduce(jnp.add, raw)
    scale = 1.0 / total
    weights = [r * scale for r in raw]
    mean = functools.reduce(
        jnp.add, [centres[-1 - n] * (weights[-1 - n] - weights[n]) for n in range(cells // 2)]
    )
    return weights, mean


def masks():
    sub = lax.broadcasted_iota(jnp.int32, (8, 128), 0)
    lane = lax.broadcasted_iota(jnp.int32, (8, 128), 1)
    sub2 = lax.broadcasted_iota(jnp.int32, (8, 256), 0)
    return sub, lane, sub2, sub < 4, sub2 < 4


def both(x, low):
    turned = pltpu.roll(x, 4, 0)
    return jnp.where(low, x, turned), jnp.where(low, turned, x)


def fold(a, b, low):
    return jnp.where(low, a, b) + pltpu.roll(jnp.where(low, b, a), 4, 0)


def skew(x, sub, sign):
    out = x
    for s in range(1, 4):
        out = jnp.where(sub % 4 == s, pltpu.roll(x, (sign * 32 * s) % 128, 1), out)
    return out


def pieces(tiles):
    his, los = [], []
    for n in range(0, len(tiles), 2):
        hi, lo = split(jnp.concatenate(tiles[n : n + 2], axis=0))
        his.append(hi)
        los.append(lo)
    return jnp.concatenate(his + los, axis=0)


def prepare(q, k, row, u, pos, bricks, wz_s, wy_s, planes):
    rows = pl.ds(row, 8)
    sub, lane, sub2, low, low2 = masks()
    wx, mean_x = axis_weights(pos[q, 0, rows, :], 4)
    wy, mean_y = axis_weights(pos[q, 1, rows, :], 4)
    wz, mean_z = axis_weights(pos[q, 2, rows, :], 8)
    for h in range(2):
        part = slice(128 * h, 128 * h + 128)
        for n in range(8):
            wz_s[u, h, pl.ds(8 * n, 8), :] = wz[n][:, part]
        for j in range(4):
            wy_s[u, h, pl.ds(8 * j, 8), :] = wy[j][:, part]
    for b in range(8):
        for h in range(2):
            col = wz_s[u, h, pl.ds(b, 8, stride=8), :]
            for jp in range(2):
                pair = [
                    col * jnp.broadcast_to(wy_s[u, h, pl.ds(8 * j + b, 1), :], (8, 128))
                    for j in (2 * jp, 2 * jp + 1)
                ]
                hi, lo = split(jnp.concatenate(pair, axis=0))
                at = 32 * (b % 4) + 16 * jp
                planes[u, b // 4, pl.ds(at, 16), pl.ds(128 * h, 128)] = hi
                planes[u, b // 4, pl.ds(128 + at, 16), pl.ds(128 * h, 128)] = lo

    diag = (lane // 32) == (sub % 4)
    turned_i = (lane // 32 + 4 - sub % 4) % 4
    c_i = turned_i.astype(F32) - 1.5
    c_j = ((lane // 8) % 4).astype(F32) - 1.5
    c_k = (lane % 8).astype(F32) - 3.5
    v = [both(skew(bricks[k, rows, pl.ds(128 * c, 128)], sub, 1), low) for c in range(3)]
    sub16 = lax.broadcasted_iota(jnp.int32, (16, 128), 0)
    lane16 = lax.broadcasted_iota(jnp.int32, (16, 128), 1)
    low16 = sub16 % 8 < 4
    diag16 = (lane16 // 32) == (sub16 % 4)
    lefts = []
    for side in range(2):
        vx, vy, vz = [x[side] for x in v]
        kinds = [
            vx, vy, vz, c_j * vy, c_k * vz,
            c_j * vx + c_i * vy, c_k * vx + c_i * vz, c_k * vy + c_j * vz,
        ]
        parts = []
        for n in range(0, 8, 2):
            parts.append(split(jnp.concatenate(kinds[n : n + 2], axis=0)))
        left = []
        for piece in range(2):
            for part in parts:
                src = part[piece]
                turned = [src] + [pltpu.roll(src, 128 - 32 * i, 1) for i in range(1, 4)]
                for ip in range(2):
                    tile = jnp.where(low16, turned[2 * ip], turned[2 * ip + 1])
                    left.append(jnp.where(diag16, tile, jnp.zeros_like(tile)))
        lefts.append(jnp.concatenate(left, axis=0))
    pairs = ([], [])
    for ip in range(2):
        first, second = both(wx[2 * ip], low2), both(wx[2 * ip + 1], low2)
        for side in range(2):
            pairs[side].append(jnp.where(low2, first[side], second[side]))
    return lefts, pairs, (mean_x, mean_y, mean_z)


def strain(q, k, row, u, prepared, visc, dens, marker_out, count, planes):
    rows = pl.ds(row, 8)
    sub, lane, sub2, low, low2 = masks()
    lefts, pairs, (mean_x, mean_y, mean_z) = prepared
    results = []
    for side in range(2):
        left = jnp.concatenate([lefts[side], lefts[side]], axis=1)
        out = jnp.dot(left, planes[u, side], preferred_element_type=F32)
        results.append(out[:128] + out[128:])
    centred = [
        [pairs[side][ip] * jnp.where(low2, 2 * ip - 1.5, 2 * ip - 0.5) for ip in range(2)]
        for side in range(2)
    ]

    def along_x(kind, weights):
        at = 32 * (kind // 2) + 8 * (kind % 2)
        sums = [
            results[side][at : at + 8] * weights[side][0]
            + results[side][at + 16 : at + 24] * weights[side][1]
            for side in range(2)
        ]
        return fold(*sums, low2)

    vx, vy, vz, yy, zz, xy, xz, yz = [along_x(n, pairs) for n in range(8)]
    xx = along_x(0, centred) - mean_x * vx
    yy = yy - mean_y * vy
    zz = zz - mean_z * vz
    xy = xy - mean_y * vx - mean_x * vy
    xz = xz - mean_z * vx - mean_x * vz
    yz = yz - mean_z * vy - mean_y * vz
    invariant = 2.0 * (xx * xx + yy * yy + zz * zz) + xy * xy + xz * xz + yz * yz
    shift = jnp.log2(1.0 + invariant * 4.0) * (-1.0 / 3.0)
    start = visc[q, rows, :]
    live = (sub2 + row) < count
    weakened = start * jnp.exp2(shift)
    marker_out[k, rows, :] = jnp.where(live, weakened, 0.0)
    carried = [
        jnp.where(live, 1.0, 0.0),
        jnp.where(live, math.log(2.0) * (jnp.log2(start) + shift), 0.0),
        jnp.where(live, dens[q, rows, :], 0.0),
    ]
    carried = [both(c, low2) for c in carried]
    return [
        pieces([carried[m][side] * pairs[side][ip] for m in range(3) for ip in range(2)])
        for side in range(2)
    ]


def deposit(k, row, u, lefts, moments, planes):
    rows = pl.ds(row, 8)
    sub, lane, sub2, low, low2 = masks()
    diag = (lane // 32) == (sub % 4)
    sums = []
    for side in range(2):
        out = lax.dot_general(lefts[side], planes[u, side], NT, preferred_element_type=F32)
        sums.append(out[:48, :128] + out[:48, 128:] + out[48:, :128])
    for m in range(3):
        halves = []
        for side in range(2):
            p = [jnp.where(diag, sums[side][16 * m + 8 * ip : 16 * m + 8 * ip + 8], 0.0) for ip in range(2)]
            halves.append(
                jnp.where(low, p[0], pltpu.roll(p[0], 32, 1))
                + jnp.where(low, pltpu.roll(p[1], 64, 1), pltpu.roll(p[1], 96, 1))
            )
        moments[k, rows, pl.ds(128 * m, 128)] = skew(fold(*halves, low), sub, -1)


NX_L, NY_L, NZ = 32, 16, 256
BRICKS = 1024
MESH = pl.DeviceIdType.MESH
SWEEPS = 4
relax_weight = 0.6
pressure_rate = 0.25
gravity = 1.0


def group_transpose(tiles, group):
    tiles = list(tiles)
    for d in (8, 4, 2, 1):
        upper = (group & d) != 0
        for t in range(16):
            if t & d == 0:
                a, b = tiles[t], tiles[t + d]
                tiles[t] = jnp.where(upper, pltpu.roll(b, 8 * d, 1), a)
                tiles[t + d] = jnp.where(upper, b, pltpu.roll(a, 128 - 8 * d, 1))
    return tiles


PAIRS = (
    (0, 0), (0, 1), (1, 0), (0, 3), (3, 0), (1, 1), (3, 3), (1, 3),
    (3, 1), (0, 2), (2, 0), (2, 1), (1, 2), (2, 3), (3, 2), (2, 2),
)
LEAD = 7


def peers():
    g, me = lax.axis_index("grid"), lax.axis_index("mark")
    z, y = me // 4, lax.rem(me, 4)

    def chosen(k, values):
        if isinstance(k, int):
            return values[k]
        out = values[0]
        for n in range(1, OWNERS):
            out = jnp.where(k == n, values[n], out)
        return out

    def after(k):
        dz = chosen(k, [p[0] for p in PAIRS])
        dy = chosen(k, [p[1] for p in PAIRS])
        return lax.rem(z + dz, 4) * 4 + lax.rem(y + dy, 4)

    def before(k):
        dz = chosen(k, [4 - p[0] for p in PAIRS])
        dy = chosen(k, [4 - p[1] for p in PAIRS])
        return lax.rem(z + dz, 4) * 4 + lax.rem(y + dy, 4)

    return g, me, after, before


def remote(src, dst, send, recv, device):
    return pltpu.make_async_remote_copy(
        src_ref=src, dst_ref=dst, send_sem=send, recv_sem=recv, device_id=device, device_id_type=MESH
    )


def step_kernel(
    counts, ids_in, velocity, pressure, visc, dens, positions, start_visc, marker_dens,
    velocity_out, pressure_out, marker_out, arrived, ids_out,
    brick_ids, state_a, state_b, visc_s, dens_s, halves, planes_hi, planes_lo, one_hot, ids_send, ids_recv,
    brick_send, bricks, kx, kym, kyp, kzm, kzp, damp, x_lo, x_hi, face_lo, face_hi, y_lo, y_hi,
    vx_lo, vx_hi, vface_lo, vface_hi, vy_lo, vy_hi, pos, mvisc, mdens, marker_s, moments, wz_s, wy_s, planes,
    load_sem, id_send, id_recv, b_send, b_recv, h_send, h_recv, v_send, v_recv, m_send, m_recv, out_sem,
):
    g, me, after, before = peers()
    ahead, behind = lax.rem(g + 1, 8), lax.rem(g + 7, 8)
    north, south = lax.rem(me + 1, OWNERS), lax.rem(me + OWNERS - 1, OWNERS)
    loads = [
        pltpu.make_async_copy(velocity, state_a.at[pl.ds(0, 3), pl.ds(1, NX_L)], load_sem.at[0]),
        pltpu.make_async_copy(pressure, state_a.at[3, pl.ds(1, NX_L)], load_sem.at[1]),
        pltpu.make_async_copy(visc, visc_s.at[pl.ds(1, NX_L)], load_sem.at[2]),
        pltpu.make_async_copy(dens, dens_s, load_sem.at[3]),
    ]
    ids_load = pltpu.make_async_copy(ids_in, brick_ids, load_sem.at[10])
    ids_load.start()
    marker_loads = [
        pltpu.make_async_copy(positions, pos, load_sem.at[4]),
        pltpu.make_async_copy(start_visc, mvisc, load_sem.at[7]),
        pltpu.make_async_copy(marker_dens, mdens, load_sem.at[8]),
    ]
    for c in loads + marker_loads:
        c.start()
    barrier = pltpu.get_barrier_semaphore()
    for k in range(1, OWNERS):
        pl.semaphore_signal(barrier, inc=1, device_id=(g, after(k)), device_id_type=MESH)
    pl.semaphore_signal(barrier, inc=1, device_id=(ahead, me), device_id_type=MESH)
    pl.semaphore_signal(barrier, inc=1, device_id=(behind, me), device_id_type=MESH)

    ids_load.wait()
    number = brick_ids[...]
    number = (((number >> 5) & 3) * 32 + (number & 31)) * 8 + (number >> 7)
    number = number.astype(F32)
    ids_send[...] = jnp.full((OWNERS, 8, 128), -1.0, F32)
    for q in range(OWNERS):
        ids_send[q, :, pl.ds(0, CAP)] = jnp.broadcast_to(number[q : q + 1], (8, CAP))

    ids_recv[0] = ids_send[me]
    for c in loads:
        c.wait()

    def first_faces(x, _):
        face_lo[0, x] = jnp.concatenate([state_a[c, x + 1, 0:1, :] for c in range(4)], axis=0)
        face_hi[0, x] = jnp.concatenate([state_a[c, x + 1, 15:16, :] for c in range(4)], axis=0)
        return 0

    lax.fori_loop(0, NX_L, first_faces, 0, unroll=4)
    for x in range(NX_L):
        vface_lo[x : x + 1, :] = visc_s[x + 1, 0:1, :]
        vface_hi[x : x + 1, :] = visc_s[x + 1, 15:16, :]
    pl.semaphore_wait(barrier, OWNERS + 1)

    def send_ids(k, _):
        remote(ids_send.at[after(k)], ids_recv.at[k], id_send.at[k], id_recv.at[k], (g, after(k))).start()
        return 0

    lax.fori_loop(1, OWNERS, send_ids, 0)
    def halo(n, state):
        return [
            remote(state.at[:, 1], x_hi.at[n], h_send.at[n, 0], h_recv.at[n, 0], (behind, me)),
            remote(state.at[:, NX_L], x_lo.at[n], h_send.at[n, 1], h_recv.at[n, 1], (ahead, me)),
            remote(face_lo.at[n], y_hi.at[n], h_send.at[n, 2], h_recv.at[n, 2], (g, south)),
            remote(face_hi.at[n], y_lo.at[n], h_send.at[n, 3], h_recv.at[n, 3], (g, north)),
        ]

    visc_halo = [
        remote(visc_s.at[1], vx_hi, v_send.at[0], v_recv.at[0], (behind, me)),
        remote(visc_s.at[NX_L], vx_lo, v_send.at[1], v_recv.at[1], (ahead, me)),
        remote(vface_lo, vy_hi, v_send.at[2], v_recv.at[2], (g, south)),
        remote(vface_hi, vy_lo, v_send.at[3], v_recv.at[3], (g, north)),
    ]
    for c in halo(0, state_a) + visc_halo:
        c.start()

    def to_halves(x, _):
        for c in range(3):
            plane = state_a[c, x + 1]
            at = pl.multiple_of(c * 512 + x * 16, 16)
            for h in range(2):
                halves[h, pl.ds(at, 16), :] = plane[:, 128 * h : 128 * h + 128]
        return 0

    lax.fori_loop(0, NX_L, to_halves, 0, unroll=4)
    group = lax.broadcasted_iota(jnp.int32, (8, 128), 1) // 8

    def to_bricks(n, _):
        bj, h = n // 2, lax.rem(n, 2)
        for c in range(3):
            tiles = [
                halves[h, pl.ds(c * 512 + 16 * i + 4 * bj + j, 8, stride=64), :]
                for i in range(4)
                for j in range(4)
            ]
            tiles = group_transpose(tiles, group)
            for t in range(0, 16, 2):
                hi, lo = split(jnp.concatenate(tiles[t : t + 2], axis=0))
                at = pl.multiple_of((bj * 32 + h * 16 + t) * 8, 16)
                planes_hi[pl.ds(at, 16), pl.ds(128 * c, 128)] = hi
                planes_lo[pl.ds(at, 16), pl.ds(128 * c, 128)] = lo
        return 0

    lax.fori_loop(0, 8, to_bricks, 0, unroll=2)

    def brick_copy(k):
        return remote(
            brick_send.at[k], bricks.at[k], b_send.at[k], b_recv.at[k], (g, before(k))
        )

    lanes = lax.broadcasted_iota(jnp.int32, (CAP, 128), 1).astype(F32)

    def hits_of(k, m):
        column = jnp.transpose(jnp.broadcast_to(ids_recv[k][0:1, :], (128, 128)))[:CAP]
        for t in range(8):
            hit = jnp.where(column == lanes + 128.0 * t, 1.0, 0.0).astype(BF16)
            one_hot[pl.ds(CAP * m, CAP), pl.ds(128 * t, 128)] = hit

    def gather(n, _):
        for m in range(8):
            hits_of(8 * n + m, m)
        found = jnp.dot(one_hot[...], planes_hi[...], preferred_element_type=F32)
        found = found + jnp.dot(one_hot[...], planes_lo[...], preferred_element_type=F32)
        for m in range(8):
            brick_send[8 * n + m] = found[CAP * m : CAP * m + CAP]
        for m in range(8):
            k = 8 * n + m

            @pl.when((k > 0) & (k <= LEAD))
            def _():
                brick_copy(k).start()

        return 0

    hits_of(0, 0)
    own = one_hot[pl.ds(0, CAP), :]
    bricks[0] = jnp.dot(own, planes_hi[...], preferred_element_type=F32) + jnp.dot(
        own, planes_lo[...], preferred_element_type=F32
    )
    for c in marker_loads:
        c.wait()

    def moment_copy(k):
        return remote(moments.at[k], arrived.at[k], m_send.at[k], m_recv.at[k], (g, after(k)))

    def marker_store(k):
        return pltpu.make_async_copy(marker_s.at[k], marker_out.at[after(k)], out_sem.at[k])

    def owner_markers(k, _):
        q = after(k)
        count = counts[0, q]

        @pl.when((k > 0) & (k + LEAD < OWNERS))
        def _():
            brick_copy(k + LEAD).start()

        @pl.when(k > 0)
        def _():
            brick_copy(k).wait()

        ready, spread = {}, {}
        for t in range(GROUPS + 4):
            if t < GROUPS:
                ready[t] = prepare(q, k, 8 * t, t, pos, bricks, wz_s, wy_s, planes)
            u = t - 2
            if 0 <= u < GROUPS:
                spread[u] = strain(q, k, 8 * u, u, ready.pop(u), mvisc, mdens, marker_s, count, planes)
            u = t - 4
            if 0 <= u < GROUPS:
                deposit(k, 8 * u, u, spread.pop(u), moments, planes)
        marker_store(k).start()

        @pl.when(k > 0)
        def _():
            moment_copy(k).start()

        return 0

    lax.fori_loop(0, 1, owner_markers, 0)
    def wait_ids(k, _):
        remote(ids_send.at[after(k)], ids_recv.at[k], id_send.at[k], id_recv.at[k], (g, after(k))).wait()
        return 0

    lax.fori_loop(1, OWNERS, wait_ids, 0)

    ids_store = pltpu.make_async_copy(ids_recv, ids_out, load_sem.at[11])
    ids_store.start()
    lax.fori_loop(0, 2, gather, 0)

    x_lo_on = (g > 0).astype(F32)
    x_hi_on = (g < 7).astype(F32)
    y_lo_on = (me > 0).astype(F32)
    y_hi_on = (me < OWNERS - 1).astype(F32)
    row = lax.broadcasted_iota(jnp.int32, (NY_L, NZ), 0)
    col = lax.broadcasted_iota(jnp.int32, (NY_L, NZ), 1)
    first_y, last_y = row == 0, row == NY_L - 1
    first_z, last_z = col == 0, col == NZ - 1

    def y_minus(plane, edge):
        return jnp.where(first_y, jnp.broadcast_to(edge, plane.shape), pltpu.roll(plane, 1, 0))

    def y_plus(plane, edge):
        return jnp.where(last_y, jnp.broadcast_to(edge, plane.shape), pltpu.roll(plane, NY_L - 1, 0))

    def z_minus(plane):
        return jnp.where(first_z, 0.0, pltpu.roll(plane, 1, 1))

    def z_plus(plane):
        return jnp.where(last_z, 0.0, pltpu.roll(plane, NZ - 1, 1))

    for c in visc_halo:
        c.wait()
    visc_s[0] = vx_lo[...] * x_lo_on
    visc_s[NX_L + 1] = vx_hi[...] * x_hi_on

    def couplings(x, _):
        here, below, above = visc_s[x + 1], visc_s[x], visc_s[x + 2]
        k_xm, k_xp = 0.5 * (here + below), 0.5 * (here + above)
        k_ym = 0.5 * (here + y_minus(here, vy_lo[pl.ds(x, 1), :] * y_lo_on))
        k_yp = 0.5 * (here + y_plus(here, vy_hi[pl.ds(x, 1), :] * y_hi_on))
        k_zm, k_zp = 0.5 * (here + z_minus(here)), 0.5 * (here + z_plus(here))
        kx[x] = k_xm
        kx[x + 1] = k_xp
        kym[x] = k_ym
        kyp[x] = k_yp
        kzm[x] = k_zm
        kzp[x] = k_zp
        damp[x] = relax_weight / (k_xm + k_xp + k_ym + k_yp + k_zm + k_zp)
        return 0

    lax.fori_loop(0, NX_L, couplings, 0, unroll=4)

    for n in range(SWEEPS):
        old, new = (state_a, state_b) if n % 2 == 0 else (state_b, state_a)
        for c in halo(n, old):
            c.wait()
        old[:, 0] = x_lo[n] * x_lo_on
        old[:, NX_L + 1] = x_hi[n] * x_hi_on

        def sweep(x, _, n=n, old=old, new=new):
            low = y_lo[n, x] * y_lo_on
            high = y_hi[n, x] * y_hi_on
            press = old[3, x + 1]
            press_near = [
                old[3, x],
                y_minus(press, low[3:4]),
                z_minus(press),
            ]
            weights = [kx[x + 1], kx[x], kyp[x], kym[x], kzp[x], kzm[x]]
            scale = damp[x]
            divergence = jnp.zeros_like(press)
            fresh = []
            for c in range(3):
                v = old[c, x + 1]
                near = [
                    old[c, x + 2],
                    old[c, x],
                    y_plus(v, high[c : c + 1]),
                    y_minus(v, low[c : c + 1]),
                    z_plus(v),
                    z_minus(v),
                ]
                forcing = press_near[c] - press
                for w, s in zip(weights, near):
                    forcing = forcing + w * (s - v)
                if c == 2:
                    forcing = forcing - gravity * dens_s[x]
                fresh.append(v + scale * forcing)
                divergence = divergence + (near[2 * c] - v)
            fresh.append(press - pressure_rate * visc_s[x + 1] * divergence)
            for c in range(4):
                new[c, x + 1] = fresh[c]
            if n + 1 < SWEEPS:
                face_lo[n + 1, x] = jnp.concatenate([f[0:1] for f in fresh], axis=0)
                face_hi[n + 1, x] = jnp.concatenate([f[15:16] for f in fresh], axis=0)
            return 0

        lax.fori_loop(0, NX_L, sweep, 0, unroll=4)
        if n + 1 < SWEEPS:
            for c in halo(n + 1, new):
                c.start()
        if n + 1 < SWEEPS:
            lax.fori_loop(1 + 5 * n, 6 + 5 * n, owner_markers, 0)
    last = state_a if SWEEPS % 2 == 0 else state_b
    stores = [
        pltpu.make_async_copy(last.at[pl.ds(0, 3), pl.ds(1, NX_L)], velocity_out, load_sem.at[5]),
        pltpu.make_async_copy(last.at[3, pl.ds(1, NX_L)], pressure_out, load_sem.at[6]),
    ]
    for c in stores:
        c.start()
    own = pltpu.make_async_copy(moments.at[0], arrived.at[0], load_sem.at[9])
    own.start()

    def arrive(k, _):
        moment_copy(k).wait()
        return 0

    lax.fori_loop(1, OWNERS, arrive, 0)

    def wait_markers(k, _):
        marker_store(k).wait()
        return 0

    lax.fori_loop(0, OWNERS, wait_markers, 0)
    own.wait()
    ids_store.wait()
    for c in stores:
        c.wait()


def home_kernel(
    moments, ids_in, visc, dens, velocity, pressure, markers,
    visc_out, dens_out, velocity_out, pressure_out, markers_out,
    ids, visc_new, dens_new, arrived, visc_s, dens_s, velocity_s, pressure_s, markers_s, hits, hi_s, lo_s, sums, cells, sem,
):
    loads = [
        pltpu.make_async_copy(moments, arrived, sem.at[0]),
        pltpu.make_async_copy(visc, visc_s, sem.at[1]),
        pltpu.make_async_copy(dens, dens_s, sem.at[2]),
    ]
    stages = ((velocity, velocity_s, velocity_out), (pressure, pressure_s, pressure_out), (markers, markers_s, markers_out))
    fetches = [pltpu.make_async_copy(a, b, sem.at[3 + n]) for n, (a, b, c) in enumerate(stages)]
    copies = [pltpu.make_async_copy(b, c, sem.at[6 + n]) for n, (a, b, c) in enumerate(stages)]
    ids_load = pltpu.make_async_copy(ids_in, ids, sem.at[9])
    for c in [ids_load] + loads + fetches:
        c.start()
    ids_load.wait()
    lane = lax.broadcasted_iota(jnp.int32, (8, 128), 1)
    rows = [jnp.full((8, 128), -1.0, F32) for _ in range(6)]
    for k in range(OWNERS):
        at = CAP * k
        t, off = at // 128, at % 128
        tile = ids[k]
        turned = pltpu.roll(tile, off, 1) if off else tile
        rows[t] = jnp.where((lane >= off) & (lane < off + CAP), turned, rows[t])
        over = off + CAP - 128
        if over > 0:
            rows[t + 1] = jnp.where(lane < over, turned, rows[t + 1])

    wide = [jnp.concatenate([r, r], axis=0) for r in rows]
    sub = lax.broadcasted_iota(jnp.int32, (16, 128), 0).astype(F32)

    def mark_hits(r, _):
        at = pl.multiple_of(r * 16, 16)
        here = sub + (r * 16).astype(F32)
        for t in range(6):
            hits[pl.ds(at, 16), pl.ds(128 * t, 128)] = jnp.where(wide[t] == here, 1.0, 0.0).astype(BF16)
        return 0

    lax.fori_loop(0, BRICKS // 16, mark_hits, 0, unroll=4)

    for c in loads:
        c.wait()

    def moment_pieces(k, _):
        hi, lo = split(arrived[k])
        at = pl.multiple_of(k * CAP, 16)
        hi_s[pl.ds(at, CAP), :] = hi
        lo_s[pl.ds(at, CAP), :] = lo
        return 0

    lax.fori_loop(0, OWNERS, moment_pieces, 0, unroll=4)

    group = lane // 8

    def scatter(n):
        at = pl.ds(256 * n, 256)
        block = hits[at, :]
        total = jnp.dot(block, hi_s[...], preferred_element_type=F32)
        total = total + jnp.dot(block, lo_s[...], preferred_element_type=F32)
        for m in range(3):
            sums[m, at, :] = total[:, 128 * m : 128 * m + 128]

    def to_cells(bj):
        for h in range(2):
            for m in range(3):
                tiles = [sums[m, pl.ds((bj * 32 + h * 16 + t) * 8, 8), :] for t in range(16)]
                tiles = group_transpose(tiles, group)
                for i in range(4):
                    for j in range(4):
                        cells[m, h, pl.ds(16 * i + 4 * bj + j, 8, stride=64), :] = tiles[4 * i + j]

    for fetch, c in zip(fetches, copies):
        fetch.wait()
        c.start()
    scatter(0)
    for n in range(4):
        if n < 3:
            scatter(n + 1)
        to_cells(n)

    def finish(x, _):
        at = pl.ds(pl.multiple_of(x * 16, 16), 16)
        for h in range(2):
            part = pl.ds(128 * h, 128)
            below = 1.0 / (cells[0, h, at, :] + 1.0)
            visc_new[x, :, part] = jnp.exp((cells[1, h, at, :] + jnp.log(visc_s[x, :, part])) * below)
            dens_new[x, :, part] = (cells[2, h, at, :] + dens_s[x, :, part]) * below
        return 0

    for n in range(4):
        lax.fori_loop(8 * n, 8 * n + 8, finish, 0, unroll=2)
        part = pl.ds(8 * n, 8)
        for m, (new, out) in enumerate(((visc_new, visc_out), (dens_new, dens_out))):
            c = pltpu.make_async_copy(new.at[part], out.at[part], sem.at[10 + 2 * n + m])
            c.start()
            copies.append(c)
    for c in copies:
        c.wait()


def per_device(
    velocity, pressure, cell_visc, cell_dens, block_brick, block_counts, positions, start_visc, marker_dens
):
    hbm = pl.BlockSpec(memory_space=pl.ANY)
    dma = pltpu.SemaphoreType.DMA
    field = (NX_L, NY_L, NZ)
    padded = (NX_L + 2, NY_L, NZ)
    shape = jax.ShapeDtypeStruct
    velocity_next, pressure_next, markers, moments, ids = pl.pallas_call(
        step_kernel,
        out_shape=(
            shape((3,) + field, F32),
            shape(field, F32),
            shape((OWNERS, CAP, BLOCK), F32),
            shape((OWNERS, CAP, 384), F32),
            shape((OWNERS, 8, 128), F32),
        ),
        in_specs=[pl.BlockSpec(memory_space=pltpu.SMEM)] + [hbm] * 8,
        out_specs=(hbm,) * 5,
        scratch_shapes=[
            VMEM((OWNERS, CAP), jnp.int32),
            VMEM((4,) + padded, F32),
            VMEM((4,) + padded, F32),
            VMEM(padded, F32),
            VMEM(field, F32),
            VMEM((2, 1536, 128), F32),
            VMEM((BRICKS, 384), BF16),
            VMEM((BRICKS, 384), BF16),
            VMEM((8 * CAP, BRICKS), BF16),
            VMEM((OWNERS, 8, 128), F32),
            VMEM((OWNERS, 8, 128), F32),
            VMEM((OWNERS, CAP, 384), F32),
            VMEM((OWNERS, CAP, 384), F32),
            VMEM((NX_L + 1, NY_L, NZ), F32),
            VMEM(field, F32),
            VMEM(field, F32),
            VMEM(field, F32),
            VMEM(field, F32),
            VMEM(field, F32),
            VMEM((SWEEPS, 4, NY_L, NZ), F32),
            VMEM((SWEEPS, 4, NY_L, NZ), F32),
            VMEM((SWEEPS, NX_L, 4, NZ), F32),
            VMEM((SWEEPS, NX_L, 4, NZ), F32),
            VMEM((SWEEPS, NX_L, 4, NZ), F32),
            VMEM((SWEEPS, NX_L, 4, NZ), F32),
            VMEM((NY_L, NZ), F32),
            VMEM((NY_L, NZ), F32),
            VMEM((NX_L, NZ), F32),
            VMEM((NX_L, NZ), F32),
            VMEM((NX_L, NZ), F32),
            VMEM((NX_L, NZ), F32),
            VMEM((OWNERS, 3, CAP, BLOCK), F32),
            VMEM((OWNERS, CAP, BLOCK), F32),
            VMEM((OWNERS, CAP, BLOCK), F32),
            VMEM((OWNERS, CAP, BLOCK), F32),
            VMEM((OWNERS, CAP, 384), F32),
            VMEM((GROUPS, 2, 64, 128), F32),
            VMEM((GROUPS, 2, 32, 128), F32),
            VMEM((GROUPS, 2, 256, 256), BF16),
            dma((12,)),
            dma((OWNERS,)),
            dma((OWNERS,)),
            dma((OWNERS,)),
            dma((OWNERS,)),
            dma((SWEEPS, 4)),
            dma((SWEEPS, 4)),
            dma((4,)),
            dma((4,)),
            dma((OWNERS,)),
            dma((OWNERS,)),
            dma((OWNERS,)),
        ],
        compiler_params=pltpu.CompilerParams(
            collective_id=0, has_side_effects=True, vmem_limit_bytes=56 << 20
        ),
        name="step",
    )(
        block_counts, block_brick, velocity, pressure, cell_visc, cell_dens,
        positions, start_visc, marker_dens,
    )
    visc_next, dens_next, velocity_next, pressure_next, markers = pl.pallas_call(
        home_kernel,
        out_shape=(
            shape(field, F32),
            shape(field, F32),
            shape((3,) + field, F32),
            shape(field, F32),
            shape((OWNERS, CAP, BLOCK), F32),
        ),
        in_specs=[hbm] * 7,
        out_specs=(hbm,) * 5,
        scratch_shapes=[
            VMEM((OWNERS, 8, 128), F32),
            VMEM(field, F32),
            VMEM(field, F32),
            VMEM((OWNERS, CAP, 384), F32),
            VMEM(field, F32),
            VMEM(field, F32),
            VMEM((3,) + field, F32),
            VMEM(field, F32),
            VMEM((OWNERS, CAP, BLOCK), F32),
            VMEM((BRICKS, OWNERS * CAP), BF16),
            VMEM((OWNERS * CAP, 384), BF16),
            VMEM((OWNERS * CAP, 384), BF16),
            VMEM((3, BRICKS, 128), F32),
            VMEM((3, 2, 512, 128), F32),
            dma((18,)),
        ],
        compiler_params=pltpu.CompilerParams(vmem_limit_bytes=56 << 20),
        name="home",
    )(moments, ids, cell_visc, cell_dens, velocity_next, pressure_next, markers)
    return velocity_next, pressure_next, visc_next, dens_next, markers


def solution(mesh):
    in_specs = (
        P(None, "grid", "mark", None),
        P("grid", "mark", None),
        P("grid", "mark", None),
        P("grid", "mark", None),
        P(("grid", "mark"), None),
        P(("grid", "mark"), None),
        P(("grid", "mark"), None, None, None),
        P(("grid", "mark"), None, None),
        P(("grid", "mark"), None, None),
    )
    out_specs = (
        P(None, "grid", "mark", None),
        P("grid", "mark", None),
        P("grid", "mark", None),
        P("grid", "mark", None),
        P(("grid", "mark"), None, None),
    )
    return jax.shard_map(
        per_device, mesh=mesh, in_specs=in_specs, out_specs=out_specs, check_vma=False
    )
```
